128 devices in a mesh: seq: 64 (over y_lo, x, z, core), chan: 2 (over y_hi).
Axes of the slice: x: 4, y: 4 (y_hi: 2, y_lo: 2; y = y_hi * 2 + y_lo), z: 4, core: 2. Of those that a mesh axis runs over, the one named last changes fastest.
Arguments:
- tokens: bfloat16 [24576, 1024], P('seq'), may hold values from -6 to 6
- cotangent: bfloat16 [24576, 1024], P('seq'), may hold values from -16 to 16
- w_in: float32 [1024, 3, 1024], P('seq', None, 'chan'), may hold values from -0.1875 to 0.1875
- w_in_m: float32 [1024, 3, 1024], P('seq', None, 'chan'), may hold values from -1000 to 1000, as said below
- w_in_v: float32 [1024, 3, 1024], P('seq', None, 'chan'), may hold values from 1228.8 to 4915.2
- w_out: float32 [1024, 1024], P('seq', 'chan'), may hold values from -0.1875 to 0.1875
- w_out_m: float32 [1024, 1024], P('seq', 'chan'), may hold values from -1000 to 1000, as said below
- w_out_v: float32 [1024, 1024], P('seq', 'chan'), may hold values from 1228.8 to 4915.2
- w_gu: float32 [1024, 2, 4608], P('seq', None, 'chan'), may hold values from -0.1875 to 0.1875
- w_gu_m: float32 [1024, 2, 4608], P('seq', None, 'chan'), may hold values from -1000 to 1000, as said below
- w_gu_v: float32 [1024, 2, 4608], P('seq', None, 'chan'), may hold values from 122.88 to 491.52
- w_down: float32 [1024, 4608], P('seq', 'chan'), may hold values from -0.09375 to 0.09375
- w_down_m: float32 [1024, 4608], P('seq', 'chan'), may hold values from -1000 to 1000, as said below
- w_down_v: float32 [1024, 4608], P('seq', 'chan'), may hold values from 491.52 to 1966.08
- vectors: float32 [5, 1024], P(None, ('seq', 'chan')), may hold values from -1.5 to 1.5, as said below
- vectors_m: float32 [5, 1024], P(None, ('seq', 'chan')), may hold values from -1000 to 1000, as said below
- vectors_v: float32 [5, 1024], P(None, ('seq', 'chan')), may hold values from 2457.6 to 9830.4
Outputs:
- block_out: float32 [24576, 1024], P('seq')
- input_grad: float32 [24576, 1024], P('seq')
- w_in_new: float32 [1024, 3, 1024], P('seq', None, 'chan')
- w_in_m_new: float32 [1024, 3, 1024], P('seq', None, 'chan')
- w_in_v_new: float32 [1024, 3, 1024], P('seq', None, 'chan')
- w_out_new: float32 [1024, 1024], P('seq', 'chan')
- w_out_m_new: float32 [1024, 1024], P('seq', 'chan')
- w_out_v_new: float32 [1024, 1024], P('seq', 'chan')
- w_gu_new: float32 [1024, 2, 4608], P('seq', None, 'chan')
- w_gu_m_new: float32 [1024, 2, 4608], P('seq', None, 'chan')
- w_gu_v_new: float32 [1024, 2, 4608], P('seq', None, 'chan')
- w_down_new: float32 [1024, 4608], P('seq', 'chan')
- w_down_m_new: float32 [1024, 4608], P('seq', 'chan')
- w_down_v_new: float32 [1024, 4608], P('seq', 'chan')
- vectors_new: float32 [5, 1024], P(None, ('seq', 'chan'))
- vectors_m_new: float32 [5, 1024], P(None, ('seq', 'chan'))
- vectors_v_new: float32 [5, 1024], P(None, ('seq', 'chan'))
The draws below stay inside these ranges and needn't reach their ends.
Inputs may be any that keep to these rules, and one draw needn't show every extreme that they name: `vectors`: rows 0 and 1 lie within 0.83 to 1.17, rows 2 to 4 within -1.5 to 1.5. `w_in_m`: both signs. `w_out_m`: both signs. `w_gu_m`: both signs. `w_down_m`: both signs. `vectors_m`: both signs.
All inputs are finite; a program needn't handle non-finite values.
Results may differ from the reference program's by a relative error of at most 0.011.
Values may be sent and summed in bfloat16 or wider, within the bound.
A program may use at most 256 MiB of HBM per device.

```python
import math
import jax
import jax.numpy as jnp
from jax import lax

D = 1024
FF = 4608
SEQS = 2
STEP = 10
TOKENS = 24576
SEQ_LEN = 12288


def draw_moment(key, shape, factor):
    spread = factor * jnp.sqrt(jnp.float32(TOKENS))
    return spread * jax.random.truncated_normal(key, -4.0, 4.0, shape, jnp.float32)


def draw_w_in_m(key, part):
    key = jax.random.fold_in(key, 11)
    return draw_moment(key, (D, 3, D), 0.11)


def draw_w_out_m(key, part):
    key = jax.random.fold_in(key, 12)
    return draw_moment(key, (D, D), 0.11)


def draw_w_gu_m(key, part):
    key = jax.random.fold_in(key, 13)
    return draw_moment(key, (D, 2, FF), 0.033)


def draw_w_down_m(key, part):
    key = jax.random.fold_in(key, 14)
    return draw_moment(key, (D, FF), 0.066)


def draw_vectors_m(key, part):
    key = jax.random.fold_in(key, 15)
    return draw_moment(key, (5, D), 0.16)


def draw_vectors(key, part):
    key = jax.random.fold_in(key, 21)
    gain_key, tap_key = jax.random.split(key)
    gains = 1.0 + 0.1 * jax.random.uniform(gain_key, (2, D), jnp.float32, -1.7, 1.7)
    taps = 0.5 * jax.random.truncated_normal(tap_key, -3.0, 3.0, (3, D), jnp.float32)
    return jnp.concatenate([gains, taps], axis=0)


def raised(array, key, source, target, parts, factor):
    owner, partner = [(jnp.arange(array.shape[position]) // (array.shape[position] // parts)).reshape([-1 if axis == position else 1 for axis in range(array.ndim)]) for position in (source, target)]
    chosen = jax.random.permutation(key, parts)[partner]
    strong = (owner == chosen) | (owner == (partner + parts // 2) % parts)
    return jnp.where(strong, factor * array, array)


def level_of(own_key, extent, pieces, low, high):
    gain = 1.0
    for position, blocks in pieces:
        steps = jax.random.uniform(jax.random.fold_in(jax.random.fold_in(own_key, 6), position), (blocks,), jnp.float32, low / len(pieces), high / len(pieces))
        gain = gain * jnp.repeat(jnp.exp(steps), extent[position] // blocks).reshape((-1,) + (1,) * (len(extent) - 1 - position))
    return gain


def gaussian(own_key, dims, deviation, limit, cuts=(), dtype=jnp.bfloat16):
    drawn = deviation * jax.random.normal(own_key, dims, jnp.float32)
    if cuts:
        drawn = drawn * level_of(own_key, dims, cuts, -0.22, 0.18)
    return jnp.clip(drawn, -limit, limit).astype(dtype)


def bell_draw_with(stream_key, extent, width, reach, cuts, heavy, kind=jnp.bfloat16):
    drawn = width * jax.random.normal(stream_key, extent, jnp.float32)
    if cuts:
        drawn = drawn * level_of(stream_key, extent, cuts, -0.22, 0.18)
    return jnp.clip(raised(drawn, jax.random.fold_in(stream_key, 3), *heavy), -reach, reach).astype(kind)


def setup_inputs(seed: int = 0) -> dict:
    splits = jax.random.split(jax.random.key(seed), 18)
    tokens = gaussian(splits[0], (TOKENS, D), 1.0, 6.0, ((0, 64),))
    cotangent = bell_draw_with(splits[1], (TOKENS, D), 1.0, 16.0, ((0, 64),), (0, 1, 64, 4.0))
    w_in = gaussian(splits[2], (D, 3, D), D ** -0.5, 0.1875, ((0, 64), (2, 2)), jnp.float32)
    w_in_m = draw_w_in_m(jax.random.fold_in(splits[17], 71), 0)
    w_in_v = jnp.clip(jnp.exp(math.log(4915.2) - 1.3862944 * jax.random.uniform(splits[4], (D, 3, D), jnp.float32) ** level_of(splits[4], (D, 3, D), ((0, 64), (2, 2)), -0.2, 0.2)), 1228.8, 4915.2)
    w_out = gaussian(splits[5], (D, D), D ** -0.5, 0.1875, ((0, 64), (1, 2)), jnp.float32)
    w_out_m = draw_w_out_m(jax.random.fold_in(splits[17], 71), 0)
    w_out_v = jnp.clip(jnp.exp(math.log(4915.2) - 1.3862944 * jax.random.uniform(splits[7], (D, D), jnp.float32) ** level_of(splits[7], (D, D), ((0, 64), (1, 2)), -0.2, 0.2)), 1228.8, 4915.2)
    w_gu = gaussian(splits[8], (D, 2, FF), D ** -0.5, 0.1875, ((0, 64), (2, 2)), jnp.float32)
    w_gu_m = draw_w_gu_m(jax.random.fold_in(splits[17], 71), 0)
    w_gu_v = jnp.clip(jnp.exp(math.log(491.52) - 1.3862944 * jax.random.uniform(splits[10], (D, 2, FF), jnp.float32) ** level_of(splits[10], (D, 2, FF), ((0, 64), (2, 2)), -0.2, 0.2)), 122.88, 491.52)
    w_down = gaussian(splits[11], (D, FF), FF ** -0.5, 0.09375, ((0, 64), (1, 2)), jnp.float32)
    w_down_m = draw_w_down_m(jax.random.fold_in(splits[17], 71), 0)
    w_down_v = jnp.clip(jnp.exp(math.log(1966.08) - 1.3862944 * jax.random.uniform(splits[13], (D, FF), jnp.float32) ** level_of(splits[13], (D, FF), ((0, 64), (1, 2)), -0.2, 0.2)), 491.52, 1966.08)
    vectors = draw_vectors(jax.random.fold_in(splits[17], 71), 0)
    vectors_m = draw_vectors_m(jax.random.fold_in(splits[17], 71), 0)
    vectors_v = jnp.clip(jnp.exp(math.log(9830.4) - 1.3862944 * jax.random.uniform(splits[16], (5, D), jnp.float32) ** level_of(splits[16], (5, D), ((1, 128),), -0.2, 0.2)), 2457.6, 9830.4)
    return {"tokens": tokens, "cotangent": cotangent, "w_in": w_in, "w_in_m": w_in_m, "w_in_v": w_in_v, "w_out": w_out, "w_out_m": w_out_m, "w_out_v": w_out_v, "w_gu": w_gu, "w_gu_m": w_gu_m, "w_gu_v": w_gu_v, "w_down": w_down, "w_down_m": w_down_m, "w_down_v": w_down_v, "vectors": vectors, "vectors_m": vectors_m, "vectors_v": vectors_v}


@jax.custom_vjp
def low(v):
    return lax.optimization_barrier(v.astype(jnp.bfloat16)).astype(jnp.float32)

@jax.custom_vjp
def low_back(v):
    return v

def low_keep(v):
    return (low(v), None)

def low_pass(kept, grad):
    return (grad,)

def back_keep(v):
    return (v, None)

def back_low(kept, grad):
    return (low(grad),)
low.defvjp(low_keep, low_pass)
low_back.defvjp(back_keep, back_low)
norm_eps = 1e-05
beta_one = 0.9
beta_two = 0.95
adam_eps = 1e-08
rate_matrix = 0.05
rate_vector = 0.5
decay_matrix = 0.1
highest = lax.Precision.HIGHEST

def rms_norm(values, gain_vector):
    inverse = lax.rsqrt(lax.optimization_barrier(jnp.mean(values * values, axis=-1, keepdims=True)) + norm_eps)
    return values * inverse * gain_vector

def forward(seq_tokens, w_in, w_out, w_gu, w_down, vectors):
    normed = low(rms_norm(seq_tokens, vectors[0]))
    mixed = low_back(jnp.einsum('tk,kcj->tcj', normed, low(w_in), precision=highest))
    gate_b = mixed[:, 0]
    gate_c = mixed[:, 1]
    values = mixed[:, 2]
    gated = low(gate_b * values)
    padded = jnp.pad(gated, ((2, 0), (0, 0)))
    convolved = low_back(vectors[2] * padded[:-2] + vectors[3] * padded[1:-1] + vectors[4] * padded[2:])
    gated_inner = low(gate_c * convolved)
    branch = low_back(jnp.einsum('tj,oj->to', gated_inner, low(w_out), precision=highest))
    middle = seq_tokens + branch
    normed_two = low(rms_norm(middle, vectors[1]))
    gate_up = low_back(jnp.einsum('tk,kcf->tcf', normed_two, low(w_gu), precision=highest))
    hidden = low(jax.nn.silu(gate_up[:, 0]) * gate_up[:, 1])
    feed_out = low_back(jnp.einsum('tf,of->to', hidden, low(w_down), precision=highest))
    return middle + feed_out

def adam_update(weight, moment_one, second, gradient, step_rate, weight_decay):
    first_new = beta_one * moment_one + (1.0 - beta_one) * gradient
    second_new = beta_two * second + (1.0 - beta_two) * gradient * gradient
    first_hat = first_new / (1.0 - beta_one ** STEP)
    second_hat = second_new / (1.0 - beta_two ** STEP)
    weight_new = weight - step_rate * (first_hat / (jnp.sqrt(second_hat) + adam_eps) + weight_decay * weight)
    return (weight_new, first_new, second_new)

def reference(tokens, cotangent, w_in, w_in_m, w_in_v, w_out, w_out_m, w_out_v, w_gu, w_gu_m, w_gu_v, w_down, w_down_m, w_down_v, vectors, vectors_m, vectors_v):
    params = (w_in, w_out, w_gu, w_down, vectors)
    seq_inputs = tokens.astype(jnp.float32).reshape(SEQS, SEQ_LEN, D)
    seq_backs = cotangent.astype(jnp.float32).reshape(SEQS, SEQ_LEN, D)
    zero_grads = tuple((jnp.zeros_like(item) for item in params))

    def per_sequence(totals, sequence_pair):
        seq_tokens, seq_back = sequence_pair
        result, pullback = jax.vjp(forward, seq_tokens, *params)
        gradients = pullback(seq_back)
        totals = tuple((left + right for left, right in zip(totals, gradients[1:])))
        return (totals, (result, gradients[0]))
    totals, (results, input_grads) = lax.scan(per_sequence, zero_grads, (seq_inputs, seq_backs))
    block_out = results.reshape(TOKENS, D)
    input_grad = input_grads.reshape(TOKENS, D)
    in_new, in_m_new, in_v_new = adam_update(w_in, w_in_m, w_in_v, totals[0], rate_matrix, decay_matrix)
    out_new, out_m_new, out_v_new = adam_update(w_out, w_out_m, w_out_v, totals[1], rate_matrix, decay_matrix)
    gu_new, gu_m_new, gu_v_new = adam_update(w_gu, w_gu_m, w_gu_v, totals[2], rate_matrix, decay_matrix)
    down_new, down_m_new, down_v_new = adam_update(w_down, w_down_m, w_down_v, totals[3], rate_matrix, decay_matrix)
    vec_new, vec_m_new, vec_v_new = adam_update(vectors, vectors_m, vectors_v, totals[4], rate_vector, 0.0)
    return (block_out, input_grad, in_new, in_m_new, in_v_new, out_new, out_m_new, out_v_new, gu_new, gu_m_new, gu_v_new, down_new, down_m_new, down_v_new, vec_new, vec_m_new, vec_v_new)
```

```python
import functools

import jax
import jax.numpy as jnp
from jax import lax
from jax.experimental import pallas as pl
from jax.experimental.pallas import tpu as pltpu
from jax.sharding import PartitionSpec as P

STEP = 10
norm_eps = 1e-05
beta_one = 0.9
beta_two = 0.95
adam_eps = 1e-08
rate_matrix = 0.05
rate_vector = 0.5
decay_matrix = 0.1

MESH = pl.DeviceIdType.MESH
BF = jnp.bfloat16
F32 = jnp.float32

RING = 4


class Place:
    def __init__(self):
        s = lax.axis_index("seq")
        core = s % 2
        z = (s // 2) % RING
        x = (s // (2 * RING)) % RING
        y = s // (2 * RING * RING)
        self.s, self.core, self.y = s, core, y
        self.pa = x + core * (z - x)
        self.pb = z + core * (x - z)
        self.x, self.z = x, z
        step_x, step_z = 2 * RING, 2
        self.step_a = step_x + core * (step_z - step_x)
        self.step_b = step_z + core * (step_x - step_z)
        self.sibling = s + 1 - 2 * core
        self.other_y = s + (1 - 2 * y) * 2 * RING * RING

    def on_a(self, off):
        return self.s + ((self.pa + off) % RING - self.pa) * self.step_a

    def on_b(self, off):
        return self.s + ((self.pb + off) % RING - self.pb) * self.step_b

    def row(self, rr):
        return self.y + rr * (1 - 2 * self.y)

    def spot(self, rr, a, b):
        xi = a + self.core * (b - a)
        zi = b + self.core * (a - b)
        return self.row(rr), xi, zi

    def greet(self):
        barrier = pltpu.get_barrier_semaphore()
        peers = (self.sibling, self.other_y, self.on_a(1), self.on_a(3), self.on_b(1), self.on_b(3))
        for peer in peers:
            pl.semaphore_signal(barrier, inc=1, device_id={"seq": peer}, device_id_type=MESH)
        pl.semaphore_wait(barrier, len(peers))


def remote(src, dst, send_sem, recv_sem, target):
    return pltpu.make_async_remote_copy(
        src_ref=src,
        dst_ref=dst,
        send_sem=send_sem,
        recv_sem=recv_sem,
        device_id={"seq": target},
        device_id_type=MESH,
    )


def gather_kernel(w_ref, g_ref, local_sem, first_sem, send, recv, sib_recv):
    me = Place()
    me.greet()
    targets = (me.sibling, me.other_y, me.on_a(1), me.on_a(3), me.on_b(1), me.on_b(3))
    SIB, YY, AR, AL, BR, BL = range(6)

    def copy(kind, rr, a, b):
        yy, xi, zi = me.spot(rr, a % RING, b % RING)
        block = g_ref.at[me.core, yy, xi, zi]
        at = (yy * RING + xi) * RING + zi
        got = sib_recv if kind == SIB else recv
        return remote(block, block, send.at[kind, at], got.at[at], targets[kind])

    def arrived(rr, a, b):
        copy(AR, rr, a, b).wait_recv()

    def start(kinds, rr, a, b):
        for kind in kinds:
            copy(kind, rr, a, b).start()

    pa, pb = me.pa, me.pb
    mine = pltpu.make_async_copy(
        w_ref.at[me.core], g_ref.at[me.core, me.y, me.x, me.z, me.core], local_sem
    )
    mine.start()
    first = remote(
        w_ref.at[1 - me.core],
        g_ref.at[1 - me.core, me.y, me.x, me.z, me.core],
        first_sem.at[0],
        first_sem.at[1],
        me.sibling,
    )
    first.start()
    arriving = remote(
        w_ref.at[me.core],
        g_ref.at[me.core, me.y, me.x, me.z, 1 - me.core],
        first_sem.at[0],
        first_sem.at[1],
        me.sibling,
    )
    mine.wait()
    arriving.wait_recv()
    start((YY, AR, AL, BR, BL, SIB), 0, pa, pb)
    copy(YY, 1, pa, pb).wait_recv()
    start((AR, AL, BR, BL, SIB), 1, pa, pb)
    for rr in range(2):
        arrived(rr, pa, pb + 3)
        start((BR, AR, AL, SIB) if rr == 0 else (AR, AL, SIB), rr, pa, pb + 3)
        arrived(rr, pa, pb + 1)
        start((BL, AR, AL, SIB) if rr == 1 else (AR, AL, SIB), rr, pa, pb + 1)
    for rr in range(2):
        arrived(rr, pa, pb + 2)
        start((AR, AL, SIB), rr, pa, pb + 2)

    def order(j):
        return (j * 3) % 4 - (j // 2) * ((j * 3) % 4 - (j - 1))

    def along_a(j, carry):
        b = pb + order(j)
        arrived(0, pa + 3, b)
        start((AR, SIB), 0, pa + 3, b)
        arrived(0, pa + 1, b)
        start((SIB,), 0, pa + 1, b)
        arrived(1, pa + 3, b)
        start((SIB,), 1, pa + 3, b)
        arrived(1, pa + 1, b)
        start((AL, SIB), 1, pa + 1, b)
        return carry

    lax.fori_loop(0, RING, along_a, 0)

    def across_a(j, carry):
        b = pb + order(j)
        for rr in range(2):
            arrived(rr, pa + 2, b)
            start((SIB,), rr, pa + 2, b)
        return carry

    lax.fori_loop(0, RING, across_a, 0)

    def from_sibling(at, carry):
        block = g_ref.at[1 - me.core, at // 16, (at // 4) % 4, at % 4]
        remote(block, block, send.at[SIB, at], sib_recv.at[at], me.sibling).wait_recv()
        mine_out = g_ref.at[me.core, at // 16, (at // 4) % 4, at % 4]
        remote(mine_out, mine_out, send.at[SIB, at], sib_recv.at[at], me.sibling).wait_send()
        return carry

    lax.fori_loop(0, 2 * RING * RING, from_sibling, 0)
    first.wait_send()
    copy(YY, 0, pa, pb).wait_send()
    for rr in range(2):
        copy(BR, rr, pa, pb).wait_send()
        copy(BL, rr, pa, pb).wait_send()
    copy(BR, 0, pa, pb + 3).wait_send()
    copy(BL, 1, pa, pb + 1).wait_send()

    def sent_a(b, carry):
        for rr in range(2):
            copy(AR, rr, pa, b).wait_send()
            copy(AL, rr, pa, b).wait_send()
        copy(AR, 0, pa + 3, b).wait_send()
        copy(AL, 1, pa + 1, b).wait_send()
        return carry

    lax.fori_loop(0, RING, sent_a, 0)


def gather(shard):
    halves, rows, width = shard.shape
    blocks = 2 * RING * RING
    out = pl.pallas_call(
        gather_kernel,
        out_shape=jax.ShapeDtypeStruct((halves, 2, RING, RING, 2, rows, width), shard.dtype),
        in_specs=[pl.BlockSpec(memory_space=pl.ANY)],
        out_specs=pl.BlockSpec(memory_space=pl.ANY),
        scratch_shapes=[
            pltpu.SemaphoreType.DMA,
            pltpu.SemaphoreType.DMA((2,)),
            pltpu.SemaphoreType.DMA((6, blocks)),
            pltpu.SemaphoreType.DMA((blocks,)),
            pltpu.SemaphoreType.DMA((blocks,)),
        ],
        compiler_params=pltpu.CompilerParams(collective_id=0, has_side_effects=True),
        name="gather_weights",
    )(shard)
    return out.reshape(halves, blocks * 2 * rows, width)


def scatter_kernel(
    p_ref,
    o_ref,
    own,
    sib,
    from_a,
    from_b,
    from_y,
    from_core,
    load_sem,
    sib_send,
    sib_recv,
    a_send,
    a_recv,
    b_send,
    b_recv,
    last_sem,
):
    me = Place()
    pa, pb = me.pa, me.pb
    load = pltpu.make_async_copy(p_ref.at[me.core], own, load_sem)
    load.start()
    me.greet()

    def to_sibling(at):
        group = at // 8
        a = (pb + 2 + group + (group // 2) * (5 - 2 * group)) % RING
        b = (pa + 2 + (at // 2) % RING) % RING
        peer_core = 1 - me.core
        xi = a + peer_core * (b - a)
        zi = b + peer_core * (a - b)
        yy = me.row(at % 2)
        where = (yy * RING + xi) * RING + zi
        return remote(
            p_ref.at[1 - me.core, yy, xi, zi],
            sib.at[yy, xi, zi],
            sib_send.at[where],
            sib_recv.at[where],
            me.sibling,
        )

    blocks = 2 * RING * RING

    def send_all(at, carry):
        to_sibling(at).start()
        return carry

    lax.fori_loop(0, blocks, send_all, 0)
    load.wait()

    def with_sibling(rr, a, b):
        yy, xi, zi = me.spot(rr, a % RING, b % RING)
        where = (yy * RING + xi) * RING + zi
        remote(
            sib.at[yy, xi, zi], sib.at[yy, xi, zi], sib_send.at[where], sib_recv.at[where], me.sibling
        ).wait_recv()
        own[yy, xi, zi] = (
            own[yy, xi, zi].astype(F32) + sib[yy, xi, zi].astype(F32)
        ).astype(own.dtype)

    def send_a(side, slot, rr, a, b):
        yy, xi, zi = me.spot(rr, a % RING, b % RING)
        return remote(
            own.at[yy, xi, zi],
            from_a.at[side, slot],
            a_send.at[side, slot],
            a_recv.at[side, slot],
            me.on_a(1 if side == 0 else 3),
        )

    def add_a(side, slot, rr, a, b):
        yy, xi, zi = me.spot(rr, a % RING, b % RING)
        send_a(side, slot, rr, a, b).wait_recv()
        own[yy, xi, zi] = (
            own[yy, xi, zi].astype(F32) + from_a[side, slot].astype(F32)
        ).astype(own.dtype)

    def opposite(j, carry):
        b = (pb + 2 + j) % RING
        with_sibling(0, pa + 2, b)
        send_a(0, b, 0, pa + 2, b).start()
        with_sibling(1, pa + 2, b)
        send_a(1, b, 1, pa + 2, b).start()
        return carry

    def direct(j, carry):
        b = (pb + 2 + j) % RING
        with_sibling(1, pa + 1, b)
        send_a(0, 8 + b, 1, pa + 1, b).start()
        with_sibling(0, pa + 3, b)
        send_a(1, 4 + b, 0, pa + 3, b).start()
        return carry

    def onward(j, carry):
        b = (pb + 2 + j) % RING
        with_sibling(0, pa + 1, b)
        add_a(0, b, 0, pa + 1, b)
        send_a(0, 4 + b, 0, pa + 1, b).start()
        with_sibling(1, pa + 3, b)
        add_a(1, b, 1, pa + 3, b)
        send_a(1, 8 + b, 1, pa + 3, b).start()
        return carry

    def finish_a(rr, b):
        yy, xi, zi = me.spot(rr, pa, b % RING)
        slot = 4 + 4 * rr + b % RING
        send_a(0, slot, rr, pa, b).wait_recv()
        send_a(1, slot, rr, pa, b).wait_recv()
        own[yy, xi, zi] = (
            own[yy, xi, zi].astype(F32)
            + from_a[0, slot].astype(F32)
            + from_a[1, slot].astype(F32)
        ).astype(own.dtype)

    lax.fori_loop(0, RING, opposite, 0)
    lax.fori_loop(0, RING, direct, 0)
    lax.fori_loop(0, RING, onward, 0)

    def kept(at, carry):
        yy, xi, zi = me.spot(at % 2, pa, (pb + at // 2) % RING)
        where = (yy * RING + xi) * RING + zi
        remote(
            sib.at[yy, xi, zi], sib.at[yy, xi, zi], sib_send.at[where], sib_recv.at[where], me.sibling
        ).wait_recv()
        own[yy, xi, zi] = (
            own[yy, xi, zi].astype(F32) + sib[yy, xi, zi].astype(F32)
        ).astype(own.dtype)
        return carry

    lax.fori_loop(0, 2 * RING, kept, 0)

    def send_b(side, slot, rr, b):
        yy, xi, zi = me.spot(rr, pa, b % RING)
        return remote(
            own.at[yy, xi, zi],
            from_b.at[side, slot],
            b_send.at[side, slot],
            b_recv.at[side, slot],
            me.on_b(1 if side == 0 else 3),
        )

    def add_b(side, slot, rr, b):
        yy, xi, zi = me.spot(rr, pa, b % RING)
        send_b(side, slot, rr, b).wait_recv()
        own[yy, xi, zi] = (
            own[yy, xi, zi].astype(F32) + from_b[side, slot].astype(F32)
        ).astype(own.dtype)

    finish_a(0, pb + 2)
    send_b(0, 0, 0, pb + 2).start()
    finish_a(1, pb + 2)
    send_b(1, 0, 1, pb + 2).start()
    finish_a(1, pb + 1)
    send_b(0, 2, 1, pb + 1).start()
    finish_a(0, pb + 3)
    send_b(1, 1, 0, pb + 3).start()
    finish_a(0, pb + 1)
    add_b(0, 0, 0, pb + 1)
    send_b(0, 1, 0, pb + 1).start()
    finish_a(1, pb + 3)
    add_b(1, 0, 1, pb + 3)
    send_b(1, 2, 1, pb + 3).start()
    finish_a(1, pb)
    add_b(0, 2, 1, pb)
    add_b(1, 2, 1, pb)
    yy, xi, zi = me.spot(1, pa, pb)
    over = remote(own.at[yy, xi, zi], from_y, last_sem.at[0], last_sem.at[1], me.other_y)
    over.start()
    finish_a(0, pb)
    add_b(0, 1, 0, pb)
    add_b(1, 1, 0, pb)
    over.wait_recv()
    yy, xi, zi = me.spot(0, pa, pb)
    own[yy, xi, zi] = (own[yy, xi, zi].astype(F32) + from_y[...].astype(F32)).astype(own.dtype)
    last = remote(
        own.at[yy, xi, zi, 1 - me.core], from_core, last_sem.at[2], last_sem.at[3], me.sibling
    )
    last.start()
    o_ref[me.core] = own[yy, xi, zi, me.core].astype(F32)
    last.wait_recv()
    o_ref[1 - me.core] = from_core[...].astype(F32)
    last.wait_send()
    over.wait_send()

    def sent_sibling(at, carry):
        to_sibling(at).wait_send()
        return carry

    lax.fori_loop(0, blocks, sent_sibling, 0)

    def sent_a(slot, carry):
        for side in range(2):
            remote(
                own.at[0, 0, 0],
                from_a.at[side, slot],
                a_send.at[side, slot],
                a_recv.at[side, slot],
                me.on_a(1 if side == 0 else 3),
            ).wait_send()
        return carry

    lax.fori_loop(0, 3 * RING, sent_a, 0)
    for slot in range(3):
        for side in range(2):
            remote(
                own.at[0, 0, 0],
                from_b.at[side, slot],
                b_send.at[side, slot],
                b_recv.at[side, slot],
                me.on_b(1 if side == 0 else 3),
            ).wait_send()


def scatter(partial):
    halves, whole, width = partial.shape
    blocks = 2 * RING * RING
    rows = whole // (2 * blocks)
    return pl.pallas_call(
        scatter_kernel,
        out_shape=jax.ShapeDtypeStruct((halves, rows, width), F32),
        in_specs=[pl.BlockSpec(memory_space=pl.ANY)],
        out_specs=pl.BlockSpec(memory_space=pltpu.VMEM),
        scratch_shapes=[
            pltpu.VMEM((2, RING, RING, 2, rows, width), partial.dtype),
            pltpu.VMEM((2, RING, RING, 2, rows, width), partial.dtype),
            pltpu.VMEM((2, 3 * RING, 2, rows, width), partial.dtype),
            pltpu.VMEM((2, 3, 2, rows, width), partial.dtype),
            pltpu.VMEM((2, rows, width), partial.dtype),
            pltpu.VMEM((rows, width), partial.dtype),
            pltpu.SemaphoreType.DMA,
            pltpu.SemaphoreType.DMA((blocks,)),
            pltpu.SemaphoreType.DMA((blocks,)),
            pltpu.SemaphoreType.DMA((2, 3 * RING)),
            pltpu.SemaphoreType.DMA((2, 3 * RING)),
            pltpu.SemaphoreType.DMA((2, 3)),
            pltpu.SemaphoreType.DMA((2, 3)),
            pltpu.SemaphoreType.DMA((4,)),
        ],
        compiler_params=pltpu.CompilerParams(
            collective_id=1, has_side_effects=True, vmem_limit_bytes=48 * 1024 * 1024
        ),
        name="scatter_gradients",
    )(partial.reshape(halves, 2, RING, RING, 2, rows, width))


def shifted(block, axis, distance):
    devices = range(lax.axis_size(axis))
    route = [(i - distance, i) for i in devices if i - distance in devices]
    return lax.ppermute(block, axis, route)


def swapped(block):
    return lax.ppermute(block, "chan", [(0, 1), (1, 0)])


def low(x):
    return lax.reduce_precision(x, 8, 7)


def both_sum(part):
    rounded = low(part)
    return rounded + swapped(rounded.astype(BF)).astype(F32)


def dot(a, b, dims):
    return lax.dot_general(a, b, (dims, ((), ())), preferred_element_type=F32)


def norm_back(values, inverse, gain, back):
    scaled = back * gain
    mean = jnp.mean(scaled * values, axis=-1, keepdims=True)
    return inverse * (scaled - values * (inverse * inverse) * mean)


def adam_update(weight, moment_one, second, gradient, step_rate, weight_decay):
    first_new = beta_one * moment_one + (1.0 - beta_one) * gradient
    second_new = beta_two * second + (1.0 - beta_two) * gradient * gradient
    first_hat = first_new / (1.0 - beta_one**STEP)
    second_hat = second_new / (1.0 - beta_two**STEP)
    weight_new = weight - step_rate * (
        first_hat / (jnp.sqrt(second_hat) + adam_eps) + weight_decay * weight
    )
    return (weight_new, first_new, second_new)


def body(
    tokens,
    cotangent,
    w_in,
    w_in_m,
    w_in_v,
    w_out,
    w_out_m,
    w_out_v,
    w_gu,
    w_gu_m,
    w_gu_v,
    w_down,
    w_down_m,
    w_down_v,
    vectors,
    vectors_m,
    vectors_v,
):
    seq_count = lax.axis_size("seq")
    seq_index = lax.axis_index("seq")
    chan = lax.axis_index("chan")
    half_seq = seq_count // 2
    rows = w_in.shape[0]
    n_in = 3 * w_in.shape[2]
    n_out = w_out.shape[1]
    n_gu = 2 * w_gu.shape[2]
    n_down = w_down.shape[1]
    wide = n_out
    hid = n_down
    n_vec = n_gu - n_in - n_out - n_down

    theirs = swapped(vectors)
    first = jnp.where(chan == 0, vectors, theirs)
    second = jnp.where(chan == 0, theirs, vectors)
    vec_rows = jnp.concatenate([first, second], axis=1).T
    vec_high = low(vec_rows)
    vec_low = vec_rows - vec_high
    vec_cols = jnp.pad(
        jnp.concatenate([vec_high, vec_low], axis=1).astype(BF), ((0, 0), (0, n_vec - 10))
    )
    shard = jnp.stack(
        [
            w_gu.astype(BF).reshape(rows, n_gu),
            jnp.concatenate(
                [
                    w_in.astype(BF).reshape(rows, n_in),
                    w_out.astype(BF),
                    w_down.astype(BF),
                    vec_cols,
                ],
                axis=1,
            ),
        ],
        axis=0,
    )
    full = gather(shard)
    full_gu = full[0]
    full_in = full[1, :, :n_in]
    full_out = full[1, :, n_in : n_in + n_out]
    full_down = full[1, :, n_in + n_out : n_in + n_out + n_down]
    vec_all = full[1, :, n_in + n_out + n_down : n_in + n_out + n_down + 10].astype(F32)
    vec_all = (vec_all[:, :5] + vec_all[:, 5:]).T
    taps = lax.dynamic_slice_in_dim(vec_all[2:5], chan * wide, wide, 1)
    gain_one, gain_two = vec_all[0], vec_all[1]

    inputs = tokens.astype(F32)
    inverse_one = lax.rsqrt(jnp.mean(inputs * inputs, axis=-1, keepdims=True) + norm_eps)
    normed = (inputs * inverse_one * gain_one).astype(BF)
    mixed = dot(normed, full_in, ((1,), (0,)))
    gate_b = mixed[:, :wide]
    gate_c = mixed[:, wide : 2 * wide]
    values = mixed[:, 2 * wide :]
    gated = (gate_b * values).astype(BF)
    carried = shifted(gated[-2:], "seq", 1)
    carried = jnp.where(seq_index % half_seq == 0, jnp.zeros_like(carried), carried)
    extended = jnp.concatenate([carried, gated], axis=0).astype(F32)
    convolved = taps[0] * extended[:-2] + taps[1] * extended[1:-1] + taps[2] * extended[2:]
    inner = (gate_c * convolved).astype(BF)
    middle = inputs + both_sum(dot(inner, full_out, ((1,), (1,))))
    inverse_two = lax.rsqrt(jnp.mean(middle * middle, axis=-1, keepdims=True) + norm_eps)
    normed_two = (middle * inverse_two * gain_two).astype(BF)
    gate_up = dot(normed_two, full_gu, ((1,), (0,)))
    gate = gate_up[:, :hid]
    up = gate_up[:, hid:]
    back_hidden = dot(cotangent, full_down, ((1,), (0,)))
    sig = jax.nn.sigmoid(gate)
    act = gate * sig
    hidden = (act * up).astype(BF)
    back_gate = (back_hidden * up * sig * (1.0 + gate * (1.0 - sig))).astype(BF)
    back_up = (back_hidden * act).astype(BF)
    back_gate_up = jnp.concatenate([back_gate, back_up], axis=1)
    block_out = middle + both_sum(dot(hidden, full_down, ((1,), (1,))))
    back_normed_two = both_sum(dot(back_gate_up, full_gu, ((1,), (1,))))
    term_gu = dot(normed_two, back_gate_up, ((0,), (0,))).astype(BF)
    term_down = dot(cotangent, hidden, ((0,), (0,))).astype(BF)
    back_out = cotangent.astype(F32)
    back_middle = back_out + norm_back(middle, inverse_two, gain_two, back_normed_two)
    gain_two_grad = jnp.sum(back_normed_two * middle * inverse_two, axis=0)
    back_branch = back_middle.astype(BF)
    back_inner = dot(back_branch, full_out, ((1,), (0,)))
    back_gate_c = back_inner * convolved
    back_conv = (back_inner * gate_c).astype(BF)
    ahead = shifted(back_conv[:2], "seq", -1)
    ahead = jnp.where(seq_index % half_seq == half_seq - 1, jnp.zeros_like(ahead), ahead)
    back_extended = jnp.concatenate([back_conv, ahead], axis=0).astype(F32)
    back_gated = (
        taps[0] * back_extended[2:] + taps[1] * back_extended[1:-1] + taps[2] * back_extended[:-2]
    )
    back_conv_wide = back_conv.astype(F32)
    tap_grads = jnp.stack(
        [
            jnp.sum(back_conv_wide * extended[:-2], axis=0),
            jnp.sum(back_conv_wide * extended[1:-1], axis=0),
            jnp.sum(back_conv_wide * extended[2:], axis=0),
        ],
        axis=0,
    )
    back_mixed = jnp.concatenate(
        [
            (back_gated * values).astype(BF),
            back_gate_c.astype(BF),
            (back_gated * gate_b).astype(BF),
        ],
        axis=1,
    )
    back_normed = both_sum(dot(back_mixed, full_in, ((1,), (1,))))
    input_grad = back_middle + norm_back(inputs, inverse_one, gain_one, back_normed)
    gain_one_grad = jnp.sum(back_normed * inputs * inverse_one, axis=0)
    term_in = dot(normed, back_mixed, ((0,), (0,))).astype(BF)
    term_out = dot(back_branch, inner, ((0,), (0,))).astype(BF)

    width = inputs.shape[1]
    tap_rows = lax.dynamic_update_slice_in_dim(
        jnp.zeros((3, width), F32), tap_grads, chan * wide, 1
    )
    vec_grad = jnp.concatenate([gain_one_grad[None], gain_two_grad[None], tap_rows], axis=0)
    vec_term = jnp.pad(vec_grad.T.astype(BF), ((0, 0), (0, n_vec - 5)))
    summed = scatter(
        jnp.stack(
            [term_gu, jnp.concatenate([term_in, term_out, term_down, vec_term], axis=1)], axis=0
        )
    )
    grad_gu = summed[0].reshape(w_gu.shape)
    grad_in = summed[1, :, :n_in].reshape(w_in.shape)
    grad_out = summed[1, :, n_in : n_in + n_out]
    grad_down = summed[1, :, n_in + n_out : n_in + n_out + n_down]
    sum_vec = summed[1, :, n_in + n_out + n_down : n_in + n_out + n_down + 5].T
    sum_taps = jnp.where(
        chan == seq_index // half_seq, sum_vec[2:], swapped(sum_vec[2:])
    )
    grad_vectors = lax.dynamic_slice_in_dim(
        jnp.concatenate([sum_vec[:2], sum_taps], axis=0), chan * (rows // 2), rows // 2, 1
    )
    in_new = adam_update(w_in, w_in_m, w_in_v, grad_in, rate_matrix, decay_matrix)
    out_new = adam_update(w_out, w_out_m, w_out_v, grad_out, rate_matrix, decay_matrix)
    gu_new = adam_update(w_gu, w_gu_m, w_gu_v, grad_gu, rate_matrix, decay_matrix)
    down_new = adam_update(w_down, w_down_m, w_down_v, grad_down, rate_matrix, decay_matrix)
    vec_new = adam_update(vectors, vectors_m, vectors_v, grad_vectors, rate_vector, 0.0)
    return (block_out, input_grad, *in_new, *out_new, *gu_new, *down_new, *vec_new)


def solution(mesh):
    matrices = [P("seq", None, "chan")] * 3 + [P("seq", "chan")] * 3
    weights = (*matrices, *matrices, *[P(None, ("seq", "chan"))] * 3)
    return jax.shard_map(
        body,
        mesh=mesh,
        in_specs=(P("seq", None), P("seq", None), *weights),
        out_specs=(P("seq", None), P("seq", None), *weights),
        check_vma=False,
    )
```

```python
import jax
import jax.numpy as jnp
from jax import lax
from jax.experimental import pallas as pl
from jax.experimental.pallas import tpu as pltpu
from jax.sharding import PartitionSpec as P

STEP = 10
norm_eps = 1e-05
beta_one = 0.9
beta_two = 0.95
adam_eps = 1e-08
rate_matrix = 0.05
rate_vector = 0.5
decay_matrix = 0.1

MESH = pl.DeviceIdType.MESH
BF = jnp.bfloat16
F32 = jnp.float32

RING = 4


class Place:
    def __init__(self):
        s = lax.axis_index("seq")
        core = s % 2
        z = (s // 2) % RING
        x = (s // (2 * RING)) % RING
        y = s // (2 * RING * RING)
        self.s, self.core, self.y = s, core, y
        self.pa = x + core * (z - x)
        self.pb = z + core * (x - z)
        self.x, self.z = x, z
        step_x, step_z = 2 * RING, 2
        self.step_a = step_x + core * (step_z - step_x)
        self.step_b = step_z + core * (step_x - step_z)
        self.sibling = s + 1 - 2 * core
        self.other_y = s + (1 - 2 * y) * 2 * RING * RING

    def on_a(self, off):
        return self.s + ((self.pa + off) % RING - self.pa) * self.step_a

    def on_b(self, off):
        return self.s + ((self.pb + off) % RING - self.pb) * self.step_b

    def row(self, rr):
        return self.y + rr * (1 - 2 * self.y)

    def spot(self, rr, a, b):
        xi = a + self.core * (b - a)
        zi = b + self.core * (a - b)
        return self.row(rr), xi, zi

    def greet(self):
        barrier = pltpu.get_barrier_semaphore()
        peers = (self.sibling, self.other_y, self.on_a(1), self.on_a(3), self.on_b(1), self.on_b(3))
        for peer in peers:
            pl.semaphore_signal(barrier, inc=1, device_id={"seq": peer}, device_id_type=MESH)
        pl.semaphore_wait(barrier, len(peers))


def remote(src, dst, send_sem, recv_sem, target):
    return pltpu.make_async_remote_copy(
        src_ref=src,
        dst_ref=dst,
        send_sem=send_sem,
        recv_sem=recv_sem,
        device_id={"seq": target},
        device_id_type=MESH,
    )


class Gathering:
    def __init__(self, me, shard, out, sems, lead):
        self.me, self.shard, self.out, self.lead = me, shard, out, lead
        self.local_sem, self.first_sem, self.send, self.recv, self.sib_recv = sems
        self.targets = (
            me.sibling, me.other_y, me.on_a(1), me.on_a(3), me.on_b(1), me.on_b(3)
        )

    def block(self, half, *where):
        return self.out.at[(half, *self.lead, *where)]

    def copy(self, kind, rr, a, b):
        yy, xi, zi = self.me.spot(rr, a % RING, b % RING)
        block = self.block(self.me.core, yy, xi, zi)
        at = (yy * RING + xi) * RING + zi
        got = self.sib_recv if kind == SIB else self.recv
        return remote(block, block, self.send.at[kind, at], got.at[at], self.targets[kind])

    def arrived(self, rr, a, b):
        self.copy(AR, rr, a, b).wait_recv()

    def start(self, kinds, rr, a, b):
        for kind in kinds:
            self.copy(kind, rr, a, b).start()

    def own(self):
        me = self.me
        return pltpu.make_async_copy(
            self.shard.at[me.core],
            self.block(me.core, me.y, me.x, me.z, me.core),
            self.local_sem,
        )

    def first(self, half, core):
        me = self.me
        return remote(
            self.shard.at[half],
            self.block(half, me.y, me.x, me.z, core),
            self.first_sem.at[0],
            self.first_sem.at[1],
            me.sibling,
        )

    def begin(self):
        me = self.me
        self.own().start()
        self.first(1 - me.core, me.core).start()

    def enter(self):
        me = self.me
        self.own().wait()
        self.first(me.core, 1 - me.core).wait_recv()
        self.start((YY, AR, AL, BR, BL, SIB), 0, me.pa, me.pb)

    def second_row(self):
        me = self.me
        self.copy(YY, 1, me.pa, me.pb).wait_recv()
        self.start((AR, AL, BR, BL, SIB), 1, me.pa, me.pb)

    def along_b(self):
        pa, pb = self.me.pa, self.me.pb
        for rr in range(2):
            self.arrived(rr, pa, pb + 3)
            self.start((BR, AR, AL, SIB) if rr == 0 else (AR, AL, SIB), rr, pa, pb + 3)
            self.arrived(rr, pa, pb + 1)
            self.start((BL, AR, AL, SIB) if rr == 1 else (AR, AL, SIB), rr, pa, pb + 1)

    def across_b(self):
        pa, pb = self.me.pa, self.me.pb
        for rr in range(2):
            self.arrived(rr, pa, pb + 2)
            self.start((AR, AL, SIB), rr, pa, pb + 2)

    def order(self, j):
        return self.me.pb + (j * 3) % 4 - (j // 2) * ((j * 3) % 4 - (j - 1))

    def along_a(self):
        pa = self.me.pa

        def step(j, carry):
            b = self.order(j)
            self.arrived(0, pa + 3, b)
            self.start((AR, SIB), 0, pa + 3, b)
            self.arrived(0, pa + 1, b)
            self.start((SIB,), 0, pa + 1, b)
            self.arrived(1, pa + 3, b)
            self.start((SIB,), 1, pa + 3, b)
            self.arrived(1, pa + 1, b)
            self.start((AL, SIB), 1, pa + 1, b)
            return carry

        lax.fori_loop(0, RING, step, 0)

    def across_a(self):
        pa = self.me.pa

        def step(j, carry):
            b = self.order(j)
            for rr in range(2):
                self.arrived(rr, pa + 2, b)
                self.start((SIB,), rr, pa + 2, b)
            return carry

        lax.fori_loop(0, RING, step, 0)

    def from_sibling(self):
        me = self.me

        def step(at, carry):
            where = (at // 16, (at // 4) % 4, at % 4)
            for half, wait in ((1 - me.core, "r"), (me.core, "s")):
                block = self.block(half, *where)
                copy = remote(block, block, self.send.at[SIB, at], self.sib_recv.at[at], me.sibling)
                copy.wait_recv() if wait == "r" else copy.wait_send()
            return carry

        lax.fori_loop(0, 2 * RING * RING, step, 0)

    def sent(self):
        me = self.me
        pa, pb = me.pa, me.pb
        self.first(1 - me.core, me.core).wait_send()
        self.copy(YY, 0, pa, pb).wait_send()
        for rr in range(2):
            self.copy(BR, rr, pa, pb).wait_send()
            self.copy(BL, rr, pa, pb).wait_send()
        self.copy(BR, 0, pa, pb + 3).wait_send()
        self.copy(BL, 1, pa, pb + 1).wait_send()

        def step(b, carry):
            for rr in range(2):
                self.copy(AR, rr, pa, b).wait_send()
                self.copy(AL, rr, pa, b).wait_send()
            self.copy(AR, 0, pa + 3, b).wait_send()
            self.copy(AL, 1, pa + 1, b).wait_send()
            return carry

        lax.fori_loop(0, RING, step, 0)


SIB, YY, AR, AL, BR, BL = range(6)
EVERY = (slice(None),)


def gather_sems():
    blocks = 2 * RING * RING
    return [
        pltpu.SemaphoreType.DMA,
        pltpu.SemaphoreType.DMA((2,)),
        pltpu.SemaphoreType.DMA((6, blocks)),
        pltpu.SemaphoreType.DMA((blocks,)),
        pltpu.SemaphoreType.DMA((blocks,)),
    ]


def gather_kernel(wm_ref, wf_ref, m_ref, f_ref, *sems):
    me = Place()
    me.greet()
    mixer = Gathering(me, wm_ref, m_ref, sems[:5], ())
    feed = Gathering(me, wf_ref, f_ref, sems[5:], EVERY)
    mixer.begin()
    feed.begin()
    mixer.enter()
    mixer.second_row()
    feed.enter()
    mixer.along_b()
    feed.second_row()
    mixer.across_b()
    feed.along_b()
    mixer.along_a()
    feed.across_b()
    mixer.across_a()
    feed.along_a()
    feed.across_a()
    for part in (mixer, feed):
        part.from_sibling()
        part.sent()


def gather(mixer_rows, feed_rows):
    halves, rows, width = mixer_rows.shape
    kinds = feed_rows.shape[1]
    whole = (2, RING, RING, 2, rows, width)
    mixer, feed = pl.pallas_call(
        gather_kernel,
        out_shape=(
            jax.ShapeDtypeStruct((halves, *whole), BF),
            jax.ShapeDtypeStruct((halves, kinds, *whole), BF),
        ),
        in_specs=[pl.BlockSpec(memory_space=pl.ANY)] * 2,
        out_specs=[pl.BlockSpec(memory_space=pl.ANY)] * 2,
        scratch_shapes=gather_sems() + gather_sems(),
        compiler_params=pltpu.CompilerParams(collective_id=0, has_side_effects=True),
        name="gather_weights",
    )(mixer_rows, feed_rows)
    total = 4 * RING * RING * rows
    return mixer.reshape(halves, total, width), feed.reshape(halves, kinds, total, width)


class Scattering:
    def __init__(self, me, partial, out, refs, lead):
        self.me, self.partial, self.out, self.lead = me, partial, out, lead
        (
            self.mine,
            self.sib,
            self.from_a,
            self.from_b,
            self.from_y,
            self.from_core,
            self.load_sem,
            self.sib_send,
            self.sib_recv,
            self.a_send,
            self.a_recv,
            self.b_send,
            self.b_recv,
            self.last_sem,
        ) = refs

    def at(self, rr, a, b):
        return self.me.spot(rr, a % RING, b % RING)

    def add(self, where, *others):
        index = (*self.lead, *where)
        total = self.mine[index].astype(F32)
        for ref, i in others:
            total = total + ref[i].astype(F32)
        self.mine[index] = total.astype(self.mine.dtype)

    def load(self):
        return pltpu.make_async_copy(self.partial.at[self.me.core], self.mine, self.load_sem)

    def to_sibling(self, at):
        me = self.me
        group = at // 8
        a = (me.pb + 2 + group + (group // 2) * (5 - 2 * group)) % RING
        b = (me.pa + 2 + (at // 2) % RING) % RING
        peer_core = 1 - me.core
        where = (me.row(at % 2), a + peer_core * (b - a), b + peer_core * (a - b))
        index = (*self.lead, *where)
        return self.sibling_copy(self.partial.at[(peer_core, *index)], where)

    def sibling_copy(self, src, where):
        i = (where[0] * RING + where[1]) * RING + where[2]
        return remote(
            src,
            self.sib.at[(*self.lead, *where)],
            self.sib_send.at[i],
            self.sib_recv.at[i],
            self.me.sibling,
        )

    def begin(self):
        self.load().start()

        def step(at, carry):
            self.to_sibling(at).start()
            return carry

        lax.fori_loop(0, 2 * RING * RING, step, 0)

    def with_sibling(self, rr, a, b):
        where = self.at(rr, a, b)
        index = (*self.lead, *where)
        self.sibling_copy(self.sib.at[index], where).wait_recv()
        self.add(where, (self.sib, index))

    def send_a(self, side, slot, rr, a, b):
        return remote(
            self.mine.at[(*self.lead, *self.at(rr, a, b))],
            self.from_a.at[side, slot],
            self.a_send.at[side, slot],
            self.a_recv.at[side, slot],
            self.me.on_a(1 if side == 0 else 3),
        )

    def add_a(self, side, slot, rr, a, b):
        self.send_a(side, slot, rr, a, b).wait_recv()
        self.add(self.at(rr, a, b), (self.from_a, (side, slot)))

    def over_b(self, step):
        def body(j, carry):
            step((self.me.pb + 2 + j) % RING)
            return carry

        lax.fori_loop(0, RING, body, 0)

    def opposite(self):
        pa = self.me.pa

        def step(b):
            self.with_sibling(0, pa + 2, b)
            self.send_a(0, b, 0, pa + 2, b).start()
            self.with_sibling(1, pa + 2, b)
            self.send_a(1, b, 1, pa + 2, b).start()

        self.over_b(step)

    def direct(self):
        pa = self.me.pa

        def step(b):
            self.with_sibling(1, pa + 1, b)
            self.send_a(0, 8 + b, 1, pa + 1, b).start()
            self.with_sibling(0, pa + 3, b)
            self.send_a(1, 4 + b, 0, pa + 3, b).start()

        self.over_b(step)

    def onward(self):
        pa = self.me.pa

        def step(b):
            self.with_sibling(0, pa + 1, b)
            self.add_a(0, b, 0, pa + 1, b)
            self.send_a(0, 4 + b, 0, pa + 1, b).start()
            self.with_sibling(1, pa + 3, b)
            self.add_a(1, b, 1, pa + 3, b)
            self.send_a(1, 8 + b, 1, pa + 3, b).start()

        self.over_b(step)

    def kept(self):
        pa = self.me.pa

        def step(b):
            self.with_sibling(0, pa, b)
            self.with_sibling(1, pa, b)

        self.over_b(step)

    def finish_a(self, rr, b):
        slot = 4 + 4 * rr + b % RING
        pa = self.me.pa
        self.send_a(0, slot, rr, pa, b).wait_recv()
        self.send_a(1, slot, rr, pa, b).wait_recv()
        self.add(self.at(rr, pa, b), (self.from_a, (0, slot)), (self.from_a, (1, slot)))

    def send_b(self, side, slot, rr, b):
        return remote(
            self.mine.at[(*self.lead, *self.at(rr, self.me.pa, b))],
            self.from_b.at[side, slot],
            self.b_send.at[side, slot],
            self.b_recv.at[side, slot],
            self.me.on_b(1 if side == 0 else 3),
        )

    def add_b(self, side, slot, rr, b):
        self.send_b(side, slot, rr, b).wait_recv()
        self.add(self.at(rr, self.me.pa, b), (self.from_b, (side, slot)))

    def ring_b(self):
        pb = self.me.pb
        self.finish_a(0, pb + 2)
        self.send_b(0, 0, 0, pb + 2).start()
        self.finish_a(1, pb + 2)
        self.send_b(1, 0, 1, pb + 2).start()
        self.finish_a(1, pb + 1)
        self.send_b(0, 2, 1, pb + 1).start()
        self.finish_a(0, pb + 3)
        self.send_b(1, 1, 0, pb + 3).start()
        self.finish_a(0, pb + 1)
        self.add_b(0, 0, 0, pb + 1)
        self.send_b(0, 1, 0, pb + 1).start()
        self.finish_a(1, pb + 3)
        self.add_b(1, 0, 1, pb + 3)
        self.send_b(1, 2, 1, pb + 3).start()
        self.finish_a(1, pb)
        self.finish_a(0, pb)

    def over(self):
        me = self.me
        return remote(
            self.mine.at[(*self.lead, *self.at(1, me.pa, me.pb))],
            self.from_y,
            self.last_sem.at[0],
            self.last_sem.at[1],
            me.other_y,
        )

    def last(self):
        me = self.me
        return remote(
            self.mine.at[(*self.lead, *self.at(0, me.pa, me.pb), 1 - me.core)],
            self.from_core,
            self.last_sem.at[2],
            self.last_sem.at[3],
            me.sibling,
        )

    def across_y(self):
        pb = self.me.pb
        self.add_b(0, 2, 1, pb)
        self.add_b(1, 2, 1, pb)
        self.over().start()
        self.add_b(0, 1, 0, pb)
        self.add_b(1, 1, 0, pb)

    def across_cores(self):
        me = self.me
        self.over().wait_recv()
        self.add(self.at(0, me.pa, me.pb), (self.from_y, ...))
        self.last().start()
        self.out[me.core] = self.mine[
            (*self.lead, *self.at(0, me.pa, me.pb), me.core)
        ].astype(F32)

    def finish(self):
        self.last().wait_recv()
        self.out[1 - self.me.core] = self.from_core[...].astype(F32)
        self.last().wait_send()
        self.over().wait_send()

        def sent_sibling(at, carry):
            self.to_sibling(at).wait_send()
            return carry

        lax.fori_loop(0, 2 * RING * RING, sent_sibling, 0)

        def sent_a(slot, carry):
            self.send_a(0, slot, 0, 0, 0).wait_send()
            self.send_a(1, slot, 0, 0, 0).wait_send()
            return carry

        lax.fori_loop(0, 3 * RING, sent_a, 0)
        for slot in range(3):
            self.send_b(0, slot, 0, 0).wait_send()
            self.send_b(1, slot, 0, 0).wait_send()


def scatter_scratch(kinds, rows, width):
    blocks = 2 * RING * RING
    dma = pltpu.SemaphoreType.DMA
    return [
        pltpu.VMEM((*kinds, 2, RING, RING, 2, rows, width), BF),
        pltpu.VMEM((*kinds, 2, RING, RING, 2, rows, width), BF),
        pltpu.VMEM((2, 3 * RING, *kinds, 2, rows, width), BF),
        pltpu.VMEM((2, 3, *kinds, 2, rows, width), BF),
        pltpu.VMEM((*kinds, 2, rows, width), BF),
        pltpu.VMEM((*kinds, rows, width), BF),
        dma,
        dma((blocks,)),
        dma((blocks,)),
        dma((2, 3 * RING)),
        dma((2, 3 * RING)),
        dma((2, 3)),
        dma((2, 3)),
        dma((4,)),
    ]


def scatter_kernel(pm_ref, pf_ref, om_ref, of_ref, *refs):
    me = Place()
    mixer = Scattering(me, pm_ref, om_ref, refs[:14], ())
    feed = Scattering(me, pf_ref, of_ref, refs[14:], EVERY)
    me.greet()
    feed.begin()
    mixer.begin()
    feed.load().wait()
    mixer.load().wait()
    feed.opposite()
    feed.direct()
    feed.onward()
    feed.kept()
    mixer.opposite()
    mixer.direct()
    feed.ring_b()
    mixer.onward()
    mixer.kept()
    feed.across_y()
    mixer.ring_b()
    feed.across_cores()
    mixer.across_y()
    mixer.across_cores()
    feed.finish()
    mixer.finish()


def scatter(mixer, feed):
    halves, total, width = mixer.shape
    kinds = feed.shape[1]
    rows = total // (4 * RING * RING)
    whole = (2, RING, RING, 2, rows, width)
    return pl.pallas_call(
        scatter_kernel,
        out_shape=(
            jax.ShapeDtypeStruct((halves, rows, width), F32),
            jax.ShapeDtypeStruct((halves, kinds, rows, width), F32),
        ),
        in_specs=[pl.BlockSpec(memory_space=pl.ANY)] * 2,
        out_specs=[pl.BlockSpec(memory_space=pltpu.VMEM)] * 2,
        scratch_shapes=scatter_scratch((), rows, width) + scatter_scratch((kinds,), rows, width),
        compiler_params=pltpu.CompilerParams(
            collective_id=1, has_side_effects=True, vmem_limit_bytes=48 * 1024 * 1024
        ),
        cost_estimate=pl.CostEstimate(flops=0, bytes_accessed=200_000_000, transcendentals=0),
        name="scatter_gradients",
    )(mixer.reshape(halves, *whole), feed.reshape(halves, kinds, *whole))


def feed_kernel(n_ref, c_ref, w_ref, t_ref, out_ref, back_ref, n_turned, c_turned, out_sum, back_sum):
    step = pl.program_id(0)

    @pl.when(step == 0)
    def _():
        n_turned[...] = n_ref[...].T
        c_turned[...] = c_ref[...].T
        out_sum[...] = jnp.zeros_like(out_sum)
        back_sum[...] = jnp.zeros_like(back_sum)

    def weight(kind):
        return jnp.concatenate([w_ref[0, kind], w_ref[1, kind]], axis=1)

    def keep(kind, term):
        term = term.astype(BF)
        lanes = term.shape[1] // 2
        t_ref[0, kind] = term[:, :lanes]
        t_ref[1, kind] = term[:, lanes:]

    w_gate, w_up, w_down = weight(0), weight(1), weight(2)
    normed = n_ref[...]
    back_out = c_ref[...]
    gate = dot(normed, w_gate, ((1,), (0,)))
    up = dot(normed, w_up, ((1,), (0,)))
    back_hidden = dot(back_out, w_down, ((1,), (0,)))
    sig = jax.nn.sigmoid(gate)
    act = gate * sig
    hidden = (act * up).astype(BF)
    back_gate = (back_hidden * up * sig * (1.0 + gate * (1.0 - sig))).astype(BF)
    back_up = (back_hidden * act).astype(BF)
    out_sum[...] += dot(hidden, w_down, ((1,), (1,)))
    back_sum[...] += dot(back_gate, w_gate, ((1,), (1,))) + dot(back_up, w_up, ((1,), (1,)))
    keep(0, dot(n_turned[...], back_gate, ((1,), (0,))))
    keep(1, dot(n_turned[...], back_up, ((1,), (0,))))
    keep(2, dot(c_turned[...], hidden, ((1,), (0,))))

    @pl.when(step == pl.num_programs(0) - 1)
    def _():
        out_ref[...] = out_sum[...].astype(BF)
        back_ref[...] = back_sum[...].astype(BF)


def feed_forward(normed, cotangent, weights):
    halves, kinds, total, width = weights.shape
    tokens = normed.shape[0]
    lanes = 128
    whole = pl.BlockSpec((tokens, total), lambda j: (0, 0))
    part = pl.BlockSpec((halves, kinds, total, lanes), lambda j: (0, 0, 0, j))
    flops = 9 * 2 * tokens * total * halves * width
    return pl.pallas_call(
        feed_kernel,
        grid=(width // lanes,),
        out_shape=(
            jax.ShapeDtypeStruct(weights.shape, BF),
            jax.ShapeDtypeStruct((tokens, total), BF),
            jax.ShapeDtypeStruct((tokens, total), BF),
        ),
        in_specs=[whole, whole, part],
        out_specs=[part, whole, whole],
        scratch_shapes=[
            pltpu.VMEM((total, tokens), BF),
            pltpu.VMEM((total, tokens), BF),
            pltpu.VMEM((tokens, total), F32),
            pltpu.VMEM((tokens, total), F32),
        ],
        compiler_params=pltpu.CompilerParams(vmem_limit_bytes=48 * 1024 * 1024),
        cost_estimate=pl.CostEstimate(
            flops=flops, bytes_accessed=4 * halves * kinds * total * width, transcendentals=0
        ),
        name="feed_forward",
    )(normed, cotangent, weights)


def shifted(block, axis, distance):
    devices = range(lax.axis_size(axis))
    route = [(i - distance, i) for i in devices if i - distance in devices]
    return lax.ppermute(block, axis, route)


def swapped(block):
    return lax.ppermute(block, "chan", [(0, 1), (1, 0)])


def low(x):
    return lax.reduce_precision(x, 8, 7)


def both_sum(part):
    rounded = low(part)
    return rounded + swapped(rounded.astype(BF)).astype(F32)


def dot(a, b, dims):
    return lax.dot_general(a, b, (dims, ((), ())), preferred_element_type=F32)


def norm_back(values, inverse, gain, back):
    scaled = back * gain
    mean = jnp.mean(scaled * values, axis=-1, keepdims=True)
    return inverse * (scaled - values * (inverse * inverse) * mean)


def adam_update(weight, moment_one, second, gradient, step_rate, weight_decay):
    first_new = beta_one * moment_one + (1.0 - beta_one) * gradient
    second_new = beta_two * second + (1.0 - beta_two) * gradient * gradient
    first_hat = first_new / (1.0 - beta_one**STEP)
    second_hat = second_new / (1.0 - beta_two**STEP)
    weight_new = weight - step_rate * (
        first_hat / (jnp.sqrt(second_hat) + adam_eps) + weight_decay * weight
    )
    return (weight_new, first_new, second_new)


def body(
    tokens,
    cotangent,
    w_in,
    w_in_m,
    w_in_v,
    w_out,
    w_out_m,
    w_out_v,
    w_gu,
    w_gu_m,
    w_gu_v,
    w_down,
    w_down_m,
    w_down_v,
    vectors,
    vectors_m,
    vectors_v,
):
    seq_count = lax.axis_size("seq")
    seq_index = lax.axis_index("seq")
    chan = lax.axis_index("chan")
    half_seq = seq_count // 2
    rows = w_in.shape[0]
    wide = w_in.shape[2]
    n_in = 3 * wide
    n_out = wide
    hid = w_down.shape[1]
    part = hid // 2
    n_vec = hid - n_in - n_out

    theirs = swapped(vectors)
    first = jnp.where(chan == 0, vectors, theirs)
    second = jnp.where(chan == 0, theirs, vectors)
    vec_rows = jnp.concatenate([first, second], axis=1).T
    vec_high = low(vec_rows)
    vec_low = vec_rows - vec_high
    vec_cols = jnp.pad(
        jnp.concatenate([vec_high, vec_low], axis=1).astype(BF), ((0, 0), (0, n_vec - 10))
    )
    mixer_rows = jnp.concatenate(
        [w_in.astype(BF).reshape(rows, n_in), w_out.astype(BF), vec_cols], axis=1
    )
    mixer_rows = jnp.stack([mixer_rows[:, :part], mixer_rows[:, part:]], axis=0)
    low_gu = w_gu.astype(BF)
    low_down = w_down.astype(BF)
    feed_rows = jnp.stack(
        [
            jnp.stack([low_gu[:, 0, at], low_gu[:, 1, at], low_down[:, at]], axis=0)
            for at in (slice(0, part), slice(part, hid))
        ],
        axis=0,
    )
    full_mixer, full_feed = gather(mixer_rows, feed_rows)
    cut = n_in - part
    full_in = jnp.concatenate([full_mixer[0], full_mixer[1, :, :cut]], axis=1)
    full_out = full_mixer[1, :, cut : cut + n_out]
    vec_all = full_mixer[1, :, cut + n_out : cut + n_out + 10].astype(F32)
    vec_all = (vec_all[:, :5] + vec_all[:, 5:]).T
    taps = lax.dynamic_slice_in_dim(vec_all[2:5], chan * wide, wide, 1)
    gain_one, gain_two = vec_all[0], vec_all[1]

    inputs = tokens.astype(F32)
    inverse_one = lax.rsqrt(jnp.mean(inputs * inputs, axis=-1, keepdims=True) + norm_eps)
    normed = (inputs * inverse_one * gain_one).astype(BF)
    mixed = dot(normed, full_in, ((1,), (0,)))
    gate_b = mixed[:, :wide]
    gate_c = mixed[:, wide : 2 * wide]
    values = mixed[:, 2 * wide :]
    gated = (gate_b * values).astype(BF)
    carried = shifted(gated[-2:], "seq", 1)
    carried = jnp.where(seq_index % half_seq == 0, jnp.zeros_like(carried), carried)
    extended = jnp.concatenate([carried, gated], axis=0).astype(F32)
    convolved = taps[0] * extended[:-2] + taps[1] * extended[1:-1] + taps[2] * extended[2:]
    inner = (gate_c * convolved).astype(BF)
    middle = inputs + both_sum(dot(inner, full_out, ((1,), (1,))))
    inverse_two = lax.rsqrt(jnp.mean(middle * middle, axis=-1, keepdims=True) + norm_eps)
    normed_two = (middle * inverse_two * gain_two).astype(BF)

    term_feed, feed_part, back_two_part = feed_forward(normed_two, cotangent, full_feed)
    back_two_theirs = swapped(back_two_part)
    back_normed_two = back_two_part.astype(F32) + back_two_theirs.astype(F32)
    feed_part, _ = lax.optimization_barrier((feed_part, back_two_theirs))
    block_out = middle + (feed_part.astype(F32) + swapped(feed_part).astype(F32))

    back_out = cotangent.astype(F32)
    back_middle = back_out + norm_back(middle, inverse_two, gain_two, back_normed_two)
    gain_two_grad = jnp.sum(back_two_part.astype(F32) * middle * inverse_two, axis=0)
    back_branch = back_middle.astype(BF)
    back_inner = dot(back_branch, full_out, ((1,), (0,)))
    back_gate_c = back_inner * convolved
    back_conv = (back_inner * gate_c).astype(BF)
    ahead = shifted(back_conv[:2], "seq", -1)
    ahead = jnp.where(seq_index % half_seq == half_seq - 1, jnp.zeros_like(ahead), ahead)
    back_extended = jnp.concatenate([back_conv, ahead], axis=0).astype(F32)
    back_gated = (
        taps[0] * back_extended[2:] + taps[1] * back_extended[1:-1] + taps[2] * back_extended[:-2]
    )
    back_conv_wide = back_conv.astype(F32)
    tap_grads = jnp.stack(
        [
            jnp.sum(back_conv_wide * extended[:-2], axis=0),
            jnp.sum(back_conv_wide * extended[1:-1], axis=0),
            jnp.sum(back_conv_wide * extended[2:], axis=0),
        ],
        axis=0,
    )
    back_mixed = jnp.concatenate(
        [
            (back_gated * values).astype(BF),
            back_gate_c.astype(BF),
            (back_gated * gate_b).astype(BF),
        ],
        axis=1,
    )
    back_one_part = low(dot(back_mixed, full_in, ((1,), (1,))))
    back_normed = back_one_part + swapped(back_one_part.astype(BF)).astype(F32)
    input_grad = back_middle + norm_back(inputs, inverse_one, gain_one, back_normed)
    gain_one_grad = jnp.sum(back_one_part * inputs * inverse_one, axis=0)
    term_in = dot(normed, back_mixed, ((0,), (0,))).astype(BF)
    term_out = dot(back_branch, inner, ((0,), (0,))).astype(BF)

    width = inputs.shape[1]
    tap_rows = lax.dynamic_update_slice_in_dim(
        jnp.zeros((3, width), F32), tap_grads, chan * wide, 1
    )
    vec_grad = jnp.concatenate([gain_one_grad[None], gain_two_grad[None], tap_rows], axis=0)
    vec_term = jnp.pad(vec_grad.T.astype(BF), ((0, 0), (0, n_vec - 5)))
    term_mixer = jnp.stack(
        [term_in[:, :part], jnp.concatenate([term_in[:, part:], term_out, vec_term], axis=1)],
        axis=0,
    )
    sum_mixer, sum_feed = scatter(term_mixer, term_feed)
    grad_in = jnp.concatenate([sum_mixer[0], sum_mixer[1, :, :cut]], axis=1).reshape(w_in.shape)
    grad_out = sum_mixer[1, :, cut : cut + n_out]
    both = jnp.concatenate([sum_feed[0], sum_feed[1]], axis=2)
    grad_gu = jnp.stack([both[0], both[1]], axis=1)
    grad_down = both[2]
    sum_vec = sum_mixer[1, :, cut + n_out : cut + n_out + 5].T
    sum_vec = sum_vec + swapped(sum_vec)
    grad_vectors = lax.dynamic_slice_in_dim(sum_vec, chan * (rows // 2), rows // 2, 1)
    in_new = adam_update(w_in, w_in_m, w_in_v, grad_in, rate_matrix, decay_matrix)
    out_new = adam_update(w_out, w_out_m, w_out_v, grad_out, rate_matrix, decay_matrix)
    gu_new = adam_update(w_gu, w_gu_m, w_gu_v, grad_gu, rate_matrix, decay_matrix)
    down_new = adam_update(w_down, w_down_m, w_down_v, grad_down, rate_matrix, decay_matrix)
    vec_new = adam_update(vectors, vectors_m, vectors_v, grad_vectors, rate_vector, 0.0)
    return (block_out, input_grad, *in_new, *out_new, *gu_new, *down_new, *vec_new)


def solution(mesh):
    matrices = [P("seq", None, "chan")] * 3 + [P("seq", "chan")] * 3
    weights = (*matrices, *matrices, *[P(None, ("seq", "chan"))] * 3)
    return jax.shard_map(
        body,
        mesh=mesh,
        in_specs=(P("seq", None), P("seq", None), *weights),
        out_specs=(P("seq", None), P("seq", None), *weights),
        check_vma=False,
    )
```

```python
import jax
import jax.numpy as jnp
from jax import lax
from jax.experimental import pallas as pl
from jax.experimental.pallas import tpu as pltpu
from jax.sharding import PartitionSpec as P

STEP = 10
norm_eps = 1e-05
beta_one = 0.9
beta_two = 0.95
adam_eps = 1e-08
rate_matrix = 0.05
rate_vector = 0.5
decay_matrix = 0.1

MESH = pl.DeviceIdType.MESH
BF = jnp.bfloat16
F32 = jnp.float32

RING = 4


class Place:
    def __init__(self):
        s = lax.axis_index("seq")
        core = s % 2
        z = (s // 2) % RING
        x = (s // (2 * RING)) % RING
        y = s // (2 * RING * RING)
        self.s, self.core, self.y = s, core, y
        self.pa = x + core * (z - x)
        self.pb = z + core * (x - z)
        self.x, self.z = x, z
        step_x, step_z = 2 * RING, 2
        self.step_a = step_x + core * (step_z - step_x)
        self.step_b = step_z + core * (step_x - step_z)
        self.sibling = s + 1 - 2 * core
        self.other_y = s + (1 - 2 * y) * 2 * RING * RING

    def on_a(self, off):
        return self.s + ((self.pa + off) % RING - self.pa) * self.step_a

    def on_b(self, off):
        return self.s + ((self.pb + off) % RING - self.pb) * self.step_b

    def row(self, rr):
        return self.y + rr * (1 - 2 * self.y)

    def spot(self, rr, a, b):
        xi = a + self.core * (b - a)
        zi = b + self.core * (a - b)
        return self.row(rr), xi, zi

    def peers(self):
        near = (self.sibling, self.other_y, self.on_a(1), self.on_a(3), self.on_b(1), self.on_b(3))
        return [{"seq": peer} for peer in near]

    def along(self):
        count = lax.axis_size("seq")
        return {"seq": (self.s + 1) % count}, {"seq": (self.s + count - 1) % count}

    def pair(self):
        return {"chan": 1 - lax.axis_index("chan")}

    def greet(self, more=()):
        barrier = pltpu.get_barrier_semaphore()
        peers = [*self.peers(), *more]
        for peer in peers:
            pl.semaphore_signal(barrier, inc=1, device_id=peer, device_id_type=MESH)
        pl.semaphore_wait(barrier, len(peers))


def remote(src, dst, send_sem, recv_sem, target):
    return pltpu.make_async_remote_copy(
        src_ref=src,
        dst_ref=dst,
        send_sem=send_sem,
        recv_sem=recv_sem,
        device_id=target if isinstance(target, dict) else {"seq": target},
        device_id_type=MESH,
    )


class Gathering:
    def __init__(self, me, shard, out, sems, lead):
        self.me, self.shard, self.out, self.lead = me, shard, out, lead
        self.local_sem, self.first_sem, self.send, self.recv, self.sib_recv = sems
        self.targets = (
            me.sibling, me.other_y, me.on_a(1), me.on_a(3), me.on_b(1), me.on_b(3)
        )

    def block(self, half, *where):
        return self.out.at[(half, *self.lead, *where)]

    def copy(self, kind, rr, a, b):
        yy, xi, zi = self.me.spot(rr, a % RING, b % RING)
        block = self.block(self.me.core, yy, xi, zi)
        at = (yy * RING + xi) * RING + zi
        got = self.sib_recv if kind == SIB else self.recv
        return remote(block, block, self.send.at[kind, at], got.at[at], self.targets[kind])

    def arrived(self, rr, a, b):
        self.copy(AR, rr, a, b).wait_recv()

    def start(self, kinds, rr, a, b):
        for kind in kinds:
            self.copy(kind, rr, a, b).start()

    def own(self):
        me = self.me
        return pltpu.make_async_copy(
            self.shard.at[me.core],
            self.block(me.core, me.y, me.x, me.z, me.core),
            self.local_sem,
        )

    def first(self, half, core):
        me = self.me
        return remote(
            self.shard.at[half],
            self.block(half, me.y, me.x, me.z, core),
            self.first_sem.at[0],
            self.first_sem.at[1],
            me.sibling,
        )

    def begin(self):
        me = self.me
        self.own().start()
        self.first(1 - me.core, me.core).start()

    def enter(self):
        me = self.me
        self.own().wait()
        self.first(me.core, 1 - me.core).wait_recv()
        self.start((YY, AR, AL, BR, BL, SIB), 0, me.pa, me.pb)

    def second_row(self):
        me = self.me
        self.copy(YY, 1, me.pa, me.pb).wait_recv()
        self.start((AR, AL, BR, BL, SIB), 1, me.pa, me.pb)

    def along_b(self):
        pa, pb = self.me.pa, self.me.pb
        for rr in range(2):
            self.arrived(rr, pa, pb + 3)
            self.start((BR, AR, AL, SIB) if rr == 0 else (AR, AL, SIB), rr, pa, pb + 3)
            self.arrived(rr, pa, pb + 1)
            self.start((BL, AR, AL, SIB) if rr == 1 else (AR, AL, SIB), rr, pa, pb + 1)

    def across_b(self):
        pa, pb = self.me.pa, self.me.pb
        for rr in range(2):
            self.arrived(rr, pa, pb + 2)
            self.start((AR, AL, SIB), rr, pa, pb + 2)

    def order(self, j):
        return self.me.pb + (j * 3) % 4 - (j // 2) * ((j * 3) % 4 - (j - 1))

    def along_a(self):
        pa = self.me.pa

        def step(j, carry):
            b = self.order(j)
            self.arrived(0, pa + 3, b)
            self.start((AR, SIB), 0, pa + 3, b)
            self.arrived(0, pa + 1, b)
            self.start((SIB,), 0, pa + 1, b)
            self.arrived(1, pa + 3, b)
            self.start((SIB,), 1, pa + 3, b)
            self.arrived(1, pa + 1, b)
            self.start((AL, SIB), 1, pa + 1, b)
            return carry

        lax.fori_loop(0, RING, step, 0)

    def across_a(self):
        pa = self.me.pa

        def step(j, carry):
            b = self.order(j)
            for rr in range(2):
                self.arrived(rr, pa + 2, b)
                self.start((SIB,), rr, pa + 2, b)
            return carry

        lax.fori_loop(0, RING, step, 0)

    def from_sibling(self):
        me = self.me

        def step(at, carry):
            where = (at // 16, (at // 4) % 4, at % 4)
            for half, wait in ((1 - me.core, "r"), (me.core, "s")):
                block = self.block(half, *where)
                copy = remote(block, block, self.send.at[SIB, at], self.sib_recv.at[at], me.sibling)
                copy.wait_recv() if wait == "r" else copy.wait_send()
            return carry

        lax.fori_loop(0, 2 * RING * RING, step, 0)

    def sent(self):
        me = self.me
        pa, pb = me.pa, me.pb
        self.first(1 - me.core, me.core).wait_send()
        self.copy(YY, 0, pa, pb).wait_send()
        for rr in range(2):
            self.copy(BR, rr, pa, pb).wait_send()
            self.copy(BL, rr, pa, pb).wait_send()
        self.copy(BR, 0, pa, pb + 3).wait_send()
        self.copy(BL, 1, pa, pb + 1).wait_send()

        def step(b, carry):
            for rr in range(2):
                self.copy(AR, rr, pa, b).wait_send()
                self.copy(AL, rr, pa, b).wait_send()
            self.copy(AR, 0, pa + 3, b).wait_send()
            self.copy(AL, 1, pa + 1, b).wait_send()
            return carry

        lax.fori_loop(0, RING, step, 0)


SIB, YY, AR, AL, BR, BL = range(6)
EVERY = (slice(None),)


def gather_sems():
    blocks = 2 * RING * RING
    return [
        pltpu.SemaphoreType.DMA,
        pltpu.SemaphoreType.DMA((2,)),
        pltpu.SemaphoreType.DMA((6, blocks)),
        pltpu.SemaphoreType.DMA((blocks,)),
        pltpu.SemaphoreType.DMA((blocks,)),
    ]


def gather_kernel(wm_ref, wf_ref, m_ref, f_ref, *sems):
    me = Place()
    me.greet()
    mixer = Gathering(me, wm_ref, m_ref, sems[:5], ())
    feed = Gathering(me, wf_ref, f_ref, sems[5:], EVERY)
    mixer.begin()
    feed.begin()
    mixer.enter()
    mixer.second_row()
    feed.enter()
    mixer.along_b()
    feed.second_row()
    mixer.across_b()
    feed.along_b()
    mixer.along_a()
    feed.across_b()
    mixer.across_a()
    feed.along_a()
    feed.across_a()
    for part in (mixer, feed):
        part.from_sibling()
        part.sent()


def gather(mixer_rows, feed_rows):
    halves, rows, width = mixer_rows.shape
    kinds = feed_rows.shape[1]
    whole = (2, RING, RING, 2, rows, width)
    mixer, feed = pl.pallas_call(
        gather_kernel,
        out_shape=(
            jax.ShapeDtypeStruct((halves, *whole), BF),
            jax.ShapeDtypeStruct((halves, kinds, *whole), BF),
        ),
        in_specs=[pl.BlockSpec(memory_space=pl.ANY)] * 2,
        out_specs=[pl.BlockSpec(memory_space=pl.ANY)] * 2,
        scratch_shapes=gather_sems() + gather_sems(),
        compiler_params=pltpu.CompilerParams(collective_id=0, has_side_effects=True),
        name="gather_weights",
    )(mixer_rows, feed_rows)
    total = 4 * RING * RING * rows
    return mixer.reshape(halves, total, width), feed.reshape(halves, kinds, total, width)


class Scattering:
    def __init__(self, me, partial, out, refs, lead, in_place=False):
        self.me, self.partial, self.out, self.lead = me, partial, out, lead
        self.in_place = in_place
        self.head = (me.core, *lead) if in_place else lead
        if in_place:
            refs = (partial, *refs[:5], None, *refs[5:])
        (
            self.mine,
            self.sib,
            self.from_a,
            self.from_b,
            self.from_y,
            self.from_core,
            self.load_sem,
            self.sib_send,
            self.sib_recv,
            self.a_send,
            self.a_recv,
            self.b_send,
            self.b_recv,
            self.last_sem,
        ) = refs

    def at(self, rr, a, b):
        return self.me.spot(rr, a % RING, b % RING)

    def add(self, where, *others):
        index = (*self.head, *where)
        total = self.mine[index].astype(F32)
        for ref, i in others:
            total = total + ref[i].astype(F32)
        self.mine[index] = total.astype(self.mine.dtype)

    def load(self):
        return pltpu.make_async_copy(self.partial.at[self.me.core], self.mine, self.load_sem)

    def to_sibling(self, at):
        me = self.me
        group = at // 8
        a = (me.pb + 2 + group + (group // 2) * (5 - 2 * group)) % RING
        b = (me.pa + 2 + (at // 2) % RING) % RING
        peer_core = 1 - me.core
        where = (me.row(at % 2), a + peer_core * (b - a), b + peer_core * (a - b))
        index = (*self.lead, *where)
        return self.sibling_copy(self.partial.at[(peer_core, *index)], where)

    def sibling_copy(self, src, where):
        i = (where[0] * RING + where[1]) * RING + where[2]
        return remote(
            src,
            self.sib.at[(*self.lead, *where)],
            self.sib_send.at[i],
            self.sib_recv.at[i],
            self.me.sibling,
        )

    def begin(self):
        if not self.in_place:
            self.load().start()

        def step(at, carry):
            self.to_sibling(at).start()
            return carry

        lax.fori_loop(0, 2 * RING * RING, step, 0)

    def with_sibling(self, rr, a, b):
        where = self.at(rr, a, b)
        index = (*self.lead, *where)
        self.sibling_copy(self.sib.at[index], where).wait_recv()
        self.add(where, (self.sib, index))

    def send_a(self, side, slot, rr, a, b):
        return remote(
            self.mine.at[(*self.head, *self.at(rr, a, b))],
            self.from_a.at[side, slot],
            self.a_send.at[side, slot],
            self.a_recv.at[side, slot],
            self.me.on_a(1 if side == 0 else 3),
        )

    def add_a(self, side, slot, rr, a, b):
        self.send_a(side, slot, rr, a, b).wait_recv()
        self.add(self.at(rr, a, b), (self.from_a, (side, slot)))

    def over_b(self, step):
        def body(j, carry):
            step((self.me.pb + 2 + j) % RING)
            return carry

        lax.fori_loop(0, RING, body, 0)

    def opposite(self):
        pa = self.me.pa

        def step(b):
            self.with_sibling(0, pa + 2, b)
            self.send_a(0, b, 0, pa + 2, b).start()
            self.with_sibling(1, pa + 2, b)
            self.send_a(1, b, 1, pa + 2, b).start()

        self.over_b(step)

    def direct(self):
        pa = self.me.pa

        def step(b):
            self.with_sibling(1, pa + 1, b)
            self.send_a(0, 8 + b, 1, pa + 1, b).start()
            self.with_sibling(0, pa + 3, b)
            self.send_a(1, 4 + b, 0, pa + 3, b).start()

        self.over_b(step)

    def onward(self):
        pa = self.me.pa

        def step(b):
            self.with_sibling(0, pa + 1, b)
            self.add_a(0, b, 0, pa + 1, b)
            self.send_a(0, 4 + b, 0, pa + 1, b).start()
            self.with_sibling(1, pa + 3, b)
            self.add_a(1, b, 1, pa + 3, b)
            self.send_a(1, 8 + b, 1, pa + 3, b).start()

        self.over_b(step)

    def kept(self):
        pa = self.me.pa

        def step(b):
            self.with_sibling(0, pa, b)
            self.with_sibling(1, pa, b)

        self.over_b(step)

    def finish_a(self, rr, b):
        slot = 4 + 4 * rr + b % RING
        pa = self.me.pa
        self.send_a(0, slot, rr, pa, b).wait_recv()
        self.send_a(1, slot, rr, pa, b).wait_recv()
        self.add(self.at(rr, pa, b), (self.from_a, (0, slot)), (self.from_a, (1, slot)))

    def send_b(self, side, slot, rr, b):
        return remote(
            self.mine.at[(*self.head, *self.at(rr, self.me.pa, b))],
            self.from_b.at[side, slot],
            self.b_send.at[side, slot],
            self.b_recv.at[side, slot],
            self.me.on_b(1 if side == 0 else 3),
        )

    def add_b(self, side, slot, rr, b):
        self.send_b(side, slot, rr, b).wait_recv()
        self.add(self.at(rr, self.me.pa, b), (self.from_b, (side, slot)))

    def ring_b(self):
        pb = self.me.pb
        self.finish_a(0, pb + 2)
        self.send_b(0, 0, 0, pb + 2).start()
        self.finish_a(1, pb + 2)
        self.send_b(1, 0, 1, pb + 2).start()
        self.finish_a(1, pb + 1)
        self.send_b(0, 2, 1, pb + 1).start()
        self.finish_a(0, pb + 3)
        self.send_b(1, 1, 0, pb + 3).start()
        self.finish_a(0, pb + 1)
        self.add_b(0, 0, 0, pb + 1)
        self.send_b(0, 1, 0, pb + 1).start()
        self.finish_a(1, pb + 3)
        self.add_b(1, 0, 1, pb + 3)
        self.send_b(1, 2, 1, pb + 3).start()
        self.finish_a(1, pb)
        self.finish_a(0, pb)

    def over(self):
        me = self.me
        return remote(
            self.mine.at[(*self.head, *self.at(1, me.pa, me.pb))],
            self.from_y,
            self.last_sem.at[0],
            self.last_sem.at[1],
            me.other_y,
        )

    def last(self):
        me = self.me
        return remote(
            self.mine.at[(*self.head, *self.at(0, me.pa, me.pb), 1 - me.core)],
            self.from_core,
            self.last_sem.at[2],
            self.last_sem.at[3],
            me.sibling,
        )

    def across_y(self):
        pb = self.me.pb
        self.add_b(0, 2, 1, pb)
        self.add_b(1, 2, 1, pb)
        self.over().start()
        self.add_b(0, 1, 0, pb)
        self.add_b(1, 1, 0, pb)

    def across_cores(self):
        me = self.me
        self.over().wait_recv()
        self.add(self.at(0, me.pa, me.pb), (self.from_y, ...))
        self.last().start()
        self.out[me.core] = self.mine[
            (*self.head, *self.at(0, me.pa, me.pb), me.core)
        ].astype(F32)

    def finish(self):
        self.last().wait_recv()
        self.out[1 - self.me.core] = self.from_core[...].astype(F32)
        self.last().wait_send()
        self.over().wait_send()

        def sent_sibling(at, carry):
            self.to_sibling(at).wait_send()
            return carry

        lax.fori_loop(0, 2 * RING * RING, sent_sibling, 0)

        def sent_a(slot, carry):
            self.send_a(0, slot, 0, 0, 0).wait_send()
            self.send_a(1, slot, 0, 0, 0).wait_send()
            return carry

        lax.fori_loop(0, 3 * RING, sent_a, 0)
        for slot in range(3):
            self.send_b(0, slot, 0, 0).wait_send()
            self.send_b(1, slot, 0, 0).wait_send()


def scatter_scratch(kinds, rows, width, in_place=False):
    blocks = 2 * RING * RING
    dma = pltpu.SemaphoreType.DMA
    mine = [] if in_place else [pltpu.VMEM((*kinds, 2, RING, RING, 2, rows, width), BF)]
    return [
        *mine,
        pltpu.VMEM((*kinds, 2, RING, RING, 2, rows, width), BF),
        pltpu.VMEM((2, 3 * RING, *kinds, 2, rows, width), BF),
        pltpu.VMEM((2, 3, *kinds, 2, rows, width), BF),
        pltpu.VMEM((*kinds, 2, rows, width), BF),
        pltpu.VMEM((*kinds, rows, width), BF),
        *([] if in_place else [dma]),
        dma((blocks,)),
        dma((blocks,)),
        dma((2, 3 * RING)),
        dma((2, 3 * RING)),
        dma((2, 3)),
        dma((2, 3)),
        dma((4,)),
    ]


def rows_of(count, step):
    return [slice(i, i + step) for i in range(0, count, step)]


def mean_square(values):
    return jnp.mean(values * values, axis=-1, keepdims=True)


ROWS = 32
HALO = 16


def backward_kernel(
    pf_ref,
    back_hbm,
    feed_hbm,
    middle_hbm,
    cot_hbm,
    tokens_hbm,
    mixed_hbm,
    gated_hbm,
    weights_hbm,
    vec_hbm,
    om_ref,
    of_ref,
    block_ref,
    grad_ref,
    *refs,
):
    (
        back_own,
        feed_own,
        middle,
        cot,
        tokens,
        mixed,
        gated,
        weights,
        vec,
        back_theirs,
        feed_theirs,
        one_theirs,
        branch,
        turned,
        inner,
        wide_gated,
        wide_conv,
        back_inner,
        back_mixed,
        sums,
        halo_out,
        halo_in,
        pm_ref,
        loads,
        pairs,
        halo_sem,
    ) = refs[:26]
    me = Place()
    pair = me.pair()
    ahead_of, behind = me.along()
    chan = lax.axis_index("chan")
    mixer = Scattering(me, pm_ref, om_ref, refs[26:38], (), in_place=True)
    feed = Scattering(me, pf_ref, of_ref, refs[38:], EVERY)
    one_own, one_sum = cot, block_ref
    count, width = middle.shape
    wide = back_inner.shape[1]
    part = weights.shape[2]

    def load(i):
        src, dst = (
            (back_hbm, back_own),
            (middle_hbm, middle),
            (cot_hbm, cot),
            (vec_hbm, vec),
            (weights_hbm, weights),
            (mixed_hbm, mixed),
            (gated_hbm, gated),
            (tokens_hbm, tokens),
            (feed_hbm, feed_own),
        )[i]
        return pltpu.make_async_copy(src, dst, loads.at[i])

    def exchange(i):
        src, dst = ((back_own, back_theirs), (feed_own, feed_theirs), (one_own, one_theirs))[i]
        return remote(src, dst, pairs.at[0, i], pairs.at[1, i], pair)

    for i in range(9):
        load(i).start()
    me.greet((pair, ahead_of, behind))
    load(0).wait()
    exchange(0).start()
    feed.begin()
    for i in range(1, 9):
        load(i).wait()
    feed.load().wait()
    feed.opposite()

    gain_one = vec[0:1, :]
    gain_two = vec[1:2, :]
    taps = [vec[2 + i : 3 + i, :wide] for i in range(3)]
    sums[...] = jnp.zeros_like(sums)
    wide_gated[...] = gated[...].astype(F32)

    def convolved(at):
        total = taps[0] * wide_gated[at.start + HALO - 2 : at.stop + HALO - 2, :]
        total = total + taps[1] * wide_gated[at.start + HALO - 1 : at.stop + HALO - 1, :]
        return total + taps[2] * wide_gated[at.start + HALO : at.stop + HALO, :]

    for at in rows_of(count, ROWS):
        inner[at, :] = (mixed[at, wide : 2 * wide] * convolved(at)).astype(BF)
    feed.direct()
    feed.onward()

    exchange(0).wait_recv()
    exchange(1).start()

    def norm_step(i, carry):
        at = pl.ds(pl.multiple_of(i * ROWS, ROWS), ROWS)
        mid = middle[at, :]
        inverse = lax.rsqrt(mean_square(mid) + norm_eps)
        own = back_own[at, :].astype(F32)
        back = own + back_theirs[at, :].astype(F32)
        total = cot[at, :].astype(F32) + norm_back(mid, inverse, gain_two, back)
        grad_ref[at, :] = total
        branch[at, :] = total.astype(BF)
        sums[1:2, :] += jnp.sum(own * mid * inverse, axis=0, keepdims=True)
        return carry

    lax.fori_loop(0, count // ROWS, norm_step, 0)
    cut = 3 * wide - part
    w_out = weights[1, :, cut : cut + wide]
    back_inner[...] = dot(branch[...], w_out, ((1,), (0,)))
    for at in rows_of(count, ROWS):
        wide_conv[at, :] = (back_inner[at, :] * mixed[at, wide : 2 * wide]).astype(BF).astype(F32)
    halo_out[...] = wide_conv[0:HALO, :].astype(BF)
    halo = remote(halo_out, halo_in, halo_sem.at[0], halo_sem.at[1], behind)
    halo.start()
    turned[...] = branch[...].T
    term_out = dot(turned[...], inner[...], ((1,), (0,))).astype(BF)
    shape = pm_ref.shape[1:-1]
    pm_ref[1, :, :, :, :, :, cut : cut + wide] = term_out.reshape(*shape, wide)
    for at in rows_of(count, ROWS):
        values = tokens[at, :].astype(F32)
        inverse = lax.rsqrt(mean_square(values) + norm_eps)
        branch[at, :] = (values * inverse * gain_one).astype(BF)
    turned[...] = branch[...].T
    feed.kept()
    halo.wait_recv()
    last = me.s % (lax.axis_size("seq") // 2) == lax.axis_size("seq") // 2 - 1
    wide_conv[count : count + HALO, :] = jnp.where(last, 0.0, halo_in[...].astype(F32))
    tap_at = pl.ds(pl.multiple_of(chan * wide, wide), wide)
    for at in rows_of(count, ROWS):
        back_gated = (
            taps[0] * wide_conv[at.start + 2 : at.stop + 2, :]
            + taps[1] * wide_conv[at.start + 1 : at.stop + 1, :]
            + taps[2] * wide_conv[at, :]
        )
        back_mixed[at, :wide] = (back_gated * mixed[at, 2 * wide :]).astype(BF)
        back_mixed[at, wide : 2 * wide] = (back_inner[at, :] * convolved(at)).astype(BF)
        back_mixed[at, 2 * wide :] = (back_gated * mixed[at, :wide]).astype(BF)
        for i in range(3):
            shift = HALO - 2 + i
            term = wide_conv[at, :] * wide_gated[at.start + shift : at.stop + shift, :]
            sums[2 + i : 3 + i, tap_at] += jnp.sum(term, axis=0, keepdims=True)

    def in_tile(j):
        lanes = part // 3
        at = pl.ds(pl.multiple_of((j % 3) * lanes, 128), lanes)
        return j // 3, at, pl.ds(pl.multiple_of(j * lanes, 128), lanes)

    one_sum[...] = jnp.zeros_like(one_sum)

    def back_step(j, carry):
        half, at, lanes = in_tile(j)
        one_sum[...] += dot(back_mixed[:, lanes], weights[half, :, at], ((1,), (1,)))
        return carry

    lax.fori_loop(0, 4, back_step, 0)

    def gain_step(i, carry):
        at = pl.ds(pl.multiple_of(i * ROWS, ROWS), ROWS)
        values = tokens[at, :].astype(F32)
        inverse = lax.rsqrt(mean_square(values) + norm_eps)
        own = one_sum[at, :]
        one_own[at, :] = own.astype(BF)
        sums[0:1, :] += jnp.sum(own * values * inverse, axis=0, keepdims=True)
        return carry

    lax.fori_loop(0, count // ROWS, gain_step, 0)
    exchange(2).start()

    def term_step(j, carry):
        half, at, lanes = in_tile(j)
        term = dot(turned[...], back_mixed[:, lanes], ((1,), (0,))).astype(BF)
        pm_ref[half, :, :, :, :, :, at] = term.reshape(*shape, part // 3)
        return carry

    lax.fori_loop(0, 4, term_step, 0)
    vec_term = sums[...].T.astype(BF)
    lanes = vec_term.shape[1]
    pm_ref[1, :, :, :, :, :, cut + wide : cut + wide + lanes] = vec_term.reshape(*shape, lanes)
    pm_ref[1, :, :, :, :, :, cut + wide + lanes :] = jnp.zeros(
        (*shape, part - cut - wide - lanes), BF
    )
    mixer.begin()
    feed.ring_b()
    mixer.opposite()
    mixer.direct()
    feed.across_y()
    mixer.onward()
    mixer.kept()
    feed.across_cores()
    exchange(1).wait_recv()

    def out_step(i, carry):
        at = pl.ds(pl.multiple_of(i * ROWS, ROWS), ROWS)
        total = feed_own[at, :].astype(F32) + feed_theirs[at, :].astype(F32)
        block_ref[at, :] = middle[at, :] + total
        return carry

    lax.fori_loop(0, count // ROWS, out_step, 0)
    mixer.ring_b()
    mixer.across_y()
    mixer.across_cores()
    exchange(2).wait_recv()

    def grad_step(i, carry):
        at = pl.ds(pl.multiple_of(i * ROWS, ROWS), ROWS)
        values = tokens[at, :].astype(F32)
        inverse = lax.rsqrt(mean_square(values) + norm_eps)
        back = one_own[at, :].astype(F32) + one_theirs[at, :].astype(F32)
        grad_ref[at, :] += norm_back(values, inverse, gain_one, back)
        return carry

    lax.fori_loop(0, count // ROWS, grad_step, 0)
    feed.finish()
    mixer.finish()
    halo.wait_send()
    for i in range(3):
        exchange(i).wait_send()


def backward(term_feed, back_two, feed_part, middle, cotangent, tokens, mixed, gated, weights, vec):
    halves, kinds, total, width = term_feed.shape
    rows = total // (4 * RING * RING)
    whole = (2, RING, RING, 2, rows, width)
    count, features = middle.shape
    wide = gated.shape[1]
    dma = pltpu.SemaphoreType.DMA

    def like(x):
        return pltpu.VMEM(x.shape, x.dtype)

    low_act = pltpu.VMEM((count, features), BF)
    return pl.pallas_call(
        backward_kernel,
        out_shape=(
            jax.ShapeDtypeStruct((halves, rows, width), F32),
            jax.ShapeDtypeStruct((halves, kinds, rows, width), F32),
            jax.ShapeDtypeStruct((count, features), F32),
            jax.ShapeDtypeStruct((count, features), F32),
        ),
        in_specs=[pl.BlockSpec(memory_space=pl.ANY)] * 10,
        out_specs=[pl.BlockSpec(memory_space=pltpu.VMEM)] * 4,
        scratch_shapes=[
            *[like(x) for x in (back_two, feed_part, middle, cotangent, tokens, mixed, gated)],
            like(weights),
            like(vec),
            low_act,
            low_act,
            low_act,
            low_act,
            pltpu.VMEM((features, count), BF),
            pltpu.VMEM((count, wide), BF),
            pltpu.VMEM((count + HALO, wide), F32),
            pltpu.VMEM((count + HALO, wide), F32),
            pltpu.VMEM((count, wide), F32),
            pltpu.VMEM((count, 3 * wide), BF),
            pltpu.VMEM((128, features), F32),
            pltpu.VMEM((HALO, wide), BF),
            pltpu.VMEM((HALO, wide), BF),
            pltpu.VMEM((halves, *whole), BF),
            dma((9,)),
            dma((2, 3)),
            dma((2,)),
            *scatter_scratch((), rows, width, in_place=True),
            *scatter_scratch((kinds,), rows, width),
        ],
        compiler_params=pltpu.CompilerParams(
            collective_id=1, has_side_effects=True, vmem_limit_bytes=60 * 1024 * 1024
        ),
        name="backward_and_scatter",
    )(
        term_feed.reshape(halves, kinds, *whole),
        back_two,
        feed_part,
        middle,
        cotangent,
        tokens,
        mixed,
        gated,
        weights,
        vec,
    )


def feed_kernel(n_ref, c_ref, w_ref, t_ref, out_ref, back_ref, n_turned, c_turned, out_sum, back_sum):
    step = pl.program_id(0)

    @pl.when(step == 0)
    def _():
        n_turned[...] = n_ref[...].T
        c_turned[...] = c_ref[...].T
        out_sum[...] = jnp.zeros_like(out_sum)
        back_sum[...] = jnp.zeros_like(back_sum)

    def weight(kind):
        return jnp.concatenate([w_ref[0, kind], w_ref[1, kind]], axis=1)

    def keep(kind, term):
        term = term.astype(BF)
        lanes = term.shape[1] // 2
        t_ref[0, kind] = term[:, :lanes]
        t_ref[1, kind] = term[:, lanes:]

    w_gate, w_up, w_down = weight(0), weight(1), weight(2)
    normed = n_ref[...]
    back_out = c_ref[...]
    gate = dot(normed, w_gate, ((1,), (0,)))
    up = dot(normed, w_up, ((1,), (0,)))
    back_hidden = dot(back_out, w_down, ((1,), (0,)))
    sig = jax.nn.sigmoid(gate)
    act = gate * sig
    hidden = (act * up).astype(BF)
    back_gate = (back_hidden * up * sig * (1.0 + gate * (1.0 - sig))).astype(BF)
    back_up = (back_hidden * act).astype(BF)
    out_sum[...] += dot(hidden, w_down, ((1,), (1,)))
    back_sum[...] += dot(back_gate, w_gate, ((1,), (1,))) + dot(back_up, w_up, ((1,), (1,)))
    keep(0, dot(n_turned[...], back_gate, ((1,), (0,))))
    keep(1, dot(n_turned[...], back_up, ((1,), (0,))))
    keep(2, dot(c_turned[...], hidden, ((1,), (0,))))

    @pl.when(step == pl.num_programs(0) - 1)
    def _():
        out_ref[...] = out_sum[...].astype(BF)
        back_ref[...] = back_sum[...].astype(BF)


def feed_forward(normed, cotangent, weights):
    halves, kinds, total, width = weights.shape
    tokens = normed.shape[0]
    lanes = 128
    whole = pl.BlockSpec((tokens, total), lambda j: (0, 0))
    part = pl.BlockSpec((halves, kinds, total, lanes), lambda j: (0, 0, 0, j))
    flops = 9 * 2 * tokens * total * halves * width
    return pl.pallas_call(
        feed_kernel,
        grid=(width // lanes,),
        out_shape=(
            jax.ShapeDtypeStruct(weights.shape, BF),
            jax.ShapeDtypeStruct((tokens, total), BF),
            jax.ShapeDtypeStruct((tokens, total), BF),
        ),
        in_specs=[whole, whole, part],
        out_specs=[part, whole, whole],
        scratch_shapes=[
            pltpu.VMEM((total, tokens), BF),
            pltpu.VMEM((total, tokens), BF),
            pltpu.VMEM((tokens, total), F32),
            pltpu.VMEM((tokens, total), F32),
        ],
        compiler_params=pltpu.CompilerParams(vmem_limit_bytes=48 * 1024 * 1024),
        cost_estimate=pl.CostEstimate(
            flops=flops, bytes_accessed=4 * halves * kinds * total * width, transcendentals=0
        ),
        name="feed_forward",
    )(normed, cotangent, weights)


def shifted(block, axis, distance):
    devices = range(lax.axis_size(axis))
    route = [(i - distance, i) for i in devices if i - distance in devices]
    return lax.ppermute(block, axis, route)


def swapped(block):
    return lax.ppermute(block, "chan", [(0, 1), (1, 0)])


def low(x):
    return lax.reduce_precision(x, 8, 7)


def both_sum(part):
    rounded = low(part)
    return rounded + swapped(rounded.astype(BF)).astype(F32)


def dot(a, b, dims):
    return lax.dot_general(a, b, (dims, ((), ())), preferred_element_type=F32)


def norm_back(values, inverse, gain, back):
    scaled = back * gain
    mean = jnp.mean(scaled * values, axis=-1, keepdims=True)
    return inverse * (scaled - values * (inverse * inverse) * mean)


def adam_update(weight, moment_one, second, gradient, step_rate, weight_decay):
    first_new = beta_one * moment_one + (1.0 - beta_one) * gradient
    second_new = beta_two * second + (1.0 - beta_two) * gradient * gradient
    first_hat = first_new / (1.0 - beta_one**STEP)
    second_hat = second_new / (1.0 - beta_two**STEP)
    weight_new = weight - step_rate * (
        first_hat / (jnp.sqrt(second_hat) + adam_eps) + weight_decay * weight
    )
    return (weight_new, first_new, second_new)


def body(
    tokens,
    cotangent,
    w_in,
    w_in_m,
    w_in_v,
    w_out,
    w_out_m,
    w_out_v,
    w_gu,
    w_gu_m,
    w_gu_v,
    w_down,
    w_down_m,
    w_down_v,
    vectors,
    vectors_m,
    vectors_v,
):
    seq_count = lax.axis_size("seq")
    seq_index = lax.axis_index("seq")
    chan = lax.axis_index("chan")
    half_seq = seq_count // 2
    rows = w_in.shape[0]
    wide = w_in.shape[2]
    n_in = 3 * wide
    n_out = wide
    hid = w_down.shape[1]
    part = hid // 2
    n_vec = hid - n_in - n_out

    theirs = swapped(vectors)
    first = jnp.where(chan == 0, vectors, theirs)
    second = jnp.where(chan == 0, theirs, vectors)
    vec_rows = jnp.concatenate([first, second], axis=1).T
    vec_high = low(vec_rows)
    vec_low = vec_rows - vec_high
    vec_cols = jnp.pad(
        jnp.concatenate([vec_high, vec_low], axis=1).astype(BF), ((0, 0), (0, n_vec - 10))
    )
    mixer_rows = jnp.concatenate(
        [w_in.astype(BF).reshape(rows, n_in), w_out.astype(BF), vec_cols], axis=1
    )
    mixer_rows = jnp.stack([mixer_rows[:, :part], mixer_rows[:, part:]], axis=0)
    low_gu = w_gu.astype(BF)
    low_down = w_down.astype(BF)
    feed_rows = jnp.stack(
        [
            jnp.stack([low_gu[:, 0, at], low_gu[:, 1, at], low_down[:, at]], axis=0)
            for at in (slice(0, part), slice(part, hid))
        ],
        axis=0,
    )
    full_mixer, full_feed = gather(mixer_rows, feed_rows)
    cut = n_in - part
    full_in = jnp.concatenate([full_mixer[0], full_mixer[1, :, :cut]], axis=1)
    full_out = full_mixer[1, :, cut : cut + n_out]
    vec_all = full_mixer[1, :, cut + n_out : cut + n_out + 10].astype(F32)
    vec_all = (vec_all[:, :5] + vec_all[:, 5:]).T
    taps = lax.dynamic_slice_in_dim(vec_all[2:5], chan * wide, wide, 1)
    gain_one, gain_two = vec_all[0], vec_all[1]

    inputs = tokens.astype(F32)
    inverse_one = lax.rsqrt(jnp.mean(inputs * inputs, axis=-1, keepdims=True) + norm_eps)
    normed = (inputs * inverse_one * gain_one).astype(BF)
    mixed = dot(normed, full_in, ((1,), (0,)))
    gate_b = mixed[:, :wide]
    gate_c = mixed[:, wide : 2 * wide]
    values = mixed[:, 2 * wide :]
    gated = (gate_b * values).astype(BF)
    carried = shifted(gated[-HALO:], "seq", 1)
    carried = jnp.where(seq_index % half_seq == 0, jnp.zeros_like(carried), carried)
    gated = jnp.concatenate([carried, gated], axis=0)
    extended = gated[HALO - 2 :].astype(F32)
    convolved = taps[0] * extended[:-2] + taps[1] * extended[1:-1] + taps[2] * extended[2:]
    inner = (gate_c * convolved).astype(BF)
    middle = inputs + both_sum(dot(inner, full_out, ((1,), (1,))))
    inverse_two = lax.rsqrt(jnp.mean(middle * middle, axis=-1, keepdims=True) + norm_eps)
    normed_two = (middle * inverse_two * gain_two).astype(BF)

    term_feed, feed_part, back_two_part = feed_forward(normed_two, cotangent, full_feed)
    width = inputs.shape[1]
    vec = jnp.concatenate(
        [vec_all[:2], jnp.pad(taps, ((0, 0), (0, width - wide))), jnp.zeros((3, width), F32)], axis=0
    )
    sum_mixer, sum_feed, block_out, input_grad = backward(
        term_feed, back_two_part, feed_part, middle, cotangent, tokens, mixed, gated, full_mixer, vec
    )
    grad_in = jnp.concatenate([sum_mixer[0], sum_mixer[1, :, :cut]], axis=1).reshape(w_in.shape)
    grad_out = sum_mixer[1, :, cut : cut + n_out]
    both = jnp.concatenate([sum_feed[0], sum_feed[1]], axis=2)
    grad_gu = jnp.stack([both[0], both[1]], axis=1)
    grad_down = both[2]
    sum_vec = sum_mixer[1, :, cut + n_out : cut + n_out + 5].T
    sum_vec = sum_vec + swapped(sum_vec)
    grad_vectors = lax.dynamic_slice_in_dim(sum_vec, chan * (rows // 2), rows // 2, 1)
    in_new = adam_update(w_in, w_in_m, w_in_v, grad_in, rate_matrix, decay_matrix)
    out_new = adam_update(w_out, w_out_m, w_out_v, grad_out, rate_matrix, decay_matrix)
    gu_new = adam_update(w_gu, w_gu_m, w_gu_v, grad_gu, rate_matrix, decay_matrix)
    down_new = adam_update(w_down, w_down_m, w_down_v, grad_down, rate_matrix, decay_matrix)
    vec_new = adam_update(vectors, vectors_m, vectors_v, grad_vectors, rate_vector, 0.0)
    return (block_out, input_grad, *in_new, *out_new, *gu_new, *down_new, *vec_new)


def solution(mesh):
    matrices = [P("seq", None, "chan")] * 3 + [P("seq", "chan")] * 3
    weights = (*matrices, *matrices, *[P(None, ("seq", "chan"))] * 3)
    return jax.shard_map(
        body,
        mesh=mesh,
        in_specs=(P("seq", None), P("seq", None), *weights),
        out_specs=(P("seq", None), P("seq", None), *weights),
        check_vma=False,
    )
```

```python
import jax
import jax.numpy as jnp
from jax import lax
from jax.experimental import pallas as pl
from jax.experimental.pallas import tpu as pltpu
from jax.sharding import PartitionSpec as P

STEP = 10
norm_eps = 1e-05
beta_one = 0.9
beta_two = 0.95
adam_eps = 1e-08
rate_matrix = 0.05
rate_vector = 0.5
decay_matrix = 0.1

MESH = pl.DeviceIdType.MESH
BF = jnp.bfloat16
F32 = jnp.float32

RING = 4


class Place:
    def __init__(self):
        s = lax.axis_index("seq")
        core = s % 2
        z = (s // 2) % RING
        x = (s // (2 * RING)) % RING
        y = s // (2 * RING * RING)
        self.s, self.core, self.y = s, core, y
        self.pa = x + core * (z - x)
        self.pb = z + core * (x - z)
        self.x, self.z = x, z
        step_x, step_z = 2 * RING, 2
        self.step_a = step_x + core * (step_z - step_x)
        self.step_b = step_z + core * (step_x - step_z)
        self.sibling = s + 1 - 2 * core
        self.other_y = s + (1 - 2 * y) * 2 * RING * RING

    def on_a(self, off):
        return self.s + ((self.pa + off) % RING - self.pa) * self.step_a

    def on_b(self, off):
        return self.s + ((self.pb + off) % RING - self.pb) * self.step_b

    def row(self, rr):
        return self.y + rr * (1 - 2 * self.y)

    def spot(self, rr, a, b):
        xi = a + self.core * (b - a)
        zi = b + self.core * (a - b)
        return self.row(rr), xi, zi

    def peers(self):
        near = (self.sibling, self.other_y, self.on_a(1), self.on_a(3), self.on_b(1), self.on_b(3))
        return [{"seq": peer} for peer in near]

    def along(self):
        count = lax.axis_size("seq")
        return {"seq": (self.s + 1) % count}, {"seq": (self.s + count - 1) % count}

    def pair(self):
        return {"chan": 1 - lax.axis_index("chan")}

    def greet(self, more=()):
        barrier = pltpu.get_barrier_semaphore()
        peers = [*self.peers(), *more]
        for peer in peers:
            pl.semaphore_signal(barrier, inc=1, device_id=peer, device_id_type=MESH)
        pl.semaphore_wait(barrier, len(peers))


def remote(src, dst, send_sem, recv_sem, target):
    return pltpu.make_async_remote_copy(
        src_ref=src,
        dst_ref=dst,
        send_sem=send_sem,
        recv_sem=recv_sem,
        device_id=target if isinstance(target, dict) else {"seq": target},
        device_id_type=MESH,
    )


class Gathering:
    def __init__(self, me, shard, out, sems, lead):
        self.me, self.shard, self.out, self.lead = me, shard, out, lead
        self.local_sem, self.first_sem, self.send, self.recv, self.sib_recv = sems
        self.targets = (
            me.sibling, me.other_y, me.on_a(1), me.on_a(3), me.on_b(1), me.on_b(3)
        )

    def block(self, half, *where):
        return self.out.at[(half, *self.lead, *where)]

    def copy(self, kind, rr, a, b):
        yy, xi, zi = self.me.spot(rr, a % RING, b % RING)
        block = self.block(self.me.core, yy, xi, zi)
        at = (yy * RING + xi) * RING + zi
        got = self.sib_recv if kind == SIB else self.recv
        return remote(block, block, self.send.at[kind, at], got.at[at], self.targets[kind])

    def arrived(self, rr, a, b):
        self.copy(AR, rr, a, b).wait_recv()

    def start(self, kinds, rr, a, b):
        for kind in kinds:
            self.copy(kind, rr, a, b).start()

    def own(self):
        me = self.me
        return pltpu.make_async_copy(
            self.shard.at[me.core],
            self.block(me.core, me.y, me.x, me.z, me.core),
            self.local_sem,
        )

    def first(self, half, core):
        me = self.me
        return remote(
            self.shard.at[half],
            self.block(half, me.y, me.x, me.z, core),
            self.first_sem.at[0],
            self.first_sem.at[1],
            me.sibling,
        )

    def begin(self):
        me = self.me
        self.own().start()
        self.first(1 - me.core, me.core).start()

    def enter(self):
        me = self.me
        self.own().wait()
        self.first(me.core, 1 - me.core).wait_recv()
        self.start((YY, AR, AL, BR, BL, SIB), 0, me.pa, me.pb)

    def second_row(self):
        me = self.me
        self.copy(YY, 1, me.pa, me.pb).wait_recv()
        self.start((AR, AL, BR, BL, SIB), 1, me.pa, me.pb)

    def along_b(self):
        pa, pb = self.me.pa, self.me.pb
        for rr in range(2):
            self.arrived(rr, pa, pb + 3)
            self.start((BR, AR, AL, SIB) if rr == 0 else (AR, AL, SIB), rr, pa, pb + 3)
            self.arrived(rr, pa, pb + 1)
            self.start((BL, AR, AL, SIB) if rr == 1 else (AR, AL, SIB), rr, pa, pb + 1)

    def across_b(self):
        pa, pb = self.me.pa, self.me.pb
        for rr in range(2):
            self.arrived(rr, pa, pb + 2)
            self.start((AR, AL, SIB), rr, pa, pb + 2)

    def order(self, j):
        return self.me.pb + (j * 3) % 4 - (j // 2) * ((j * 3) % 4 - (j - 1))

    def along_a(self):
        pa = self.me.pa

        def step(j, carry):
            b = self.order(j)
            self.arrived(0, pa + 3, b)
            self.start((AR, SIB), 0, pa + 3, b)
            self.arrived(0, pa + 1, b)
            self.start((SIB,), 0, pa + 1, b)
            self.arrived(1, pa + 3, b)
            self.start((SIB,), 1, pa + 3, b)
            self.arrived(1, pa + 1, b)
            self.start((AL, SIB), 1, pa + 1, b)
            return carry

        lax.fori_loop(0, RING, step, 0)

    def across_a(self):
        pa = self.me.pa

        def step(j, carry):
            b = self.order(j)
            for rr in range(2):
                self.arrived(rr, pa + 2, b)
                self.start((SIB,), rr, pa + 2, b)
            return carry

        lax.fori_loop(0, RING, step, 0)

    def from_sibling(self):
        me = self.me

        def step(at, carry):
            where = (at // 16, (at // 4) % 4, at % 4)
            for half, wait in ((1 - me.core, "r"), (me.core, "s")):
                block = self.block(half, *where)
                copy = remote(block, block, self.send.at[SIB, at], self.sib_recv.at[at], me.sibling)
                copy.wait_recv() if wait == "r" else copy.wait_send()
            return carry

        lax.fori_loop(0, 2 * RING * RING, step, 0)

    def sent(self):
        me = self.me
        pa, pb = me.pa, me.pb
        self.first(1 - me.core, me.core).wait_send()
        self.copy(YY, 0, pa, pb).wait_send()
        for rr in range(2):
            self.copy(BR, rr, pa, pb).wait_send()
            self.copy(BL, rr, pa, pb).wait_send()
        self.copy(BR, 0, pa, pb + 3).wait_send()
        self.copy(BL, 1, pa, pb + 1).wait_send()

        def step(b, carry):
            for rr in range(2):
                self.copy(AR, rr, pa, b).wait_send()
                self.copy(AL, rr, pa, b).wait_send()
            self.copy(AR, 0, pa + 3, b).wait_send()
            self.copy(AL, 1, pa + 1, b).wait_send()
            return carry

        lax.fori_loop(0, RING, step, 0)


SIB, YY, AR, AL, BR, BL = range(6)
EVERY = (slice(None),)


def gather_sems():
    blocks = 2 * RING * RING
    return [
        pltpu.SemaphoreType.DMA,
        pltpu.SemaphoreType.DMA((2,)),
        pltpu.SemaphoreType.DMA((6, blocks)),
        pltpu.SemaphoreType.DMA((blocks,)),
        pltpu.SemaphoreType.DMA((blocks,)),
    ]


def rows_of(count, step):
    return [slice(i, i + step) for i in range(0, count, step)]


def mean_square(values):
    return jnp.mean(values * values, axis=-1, keepdims=True)


def in_tile(j, part):
    lanes = part // 3
    at = pl.ds(pl.multiple_of((j % 3) * lanes, 128), lanes)
    return j // 3, at, pl.ds(pl.multiple_of(j * lanes, 128), lanes)


def row_loop(count, step):
    def body(i, carry):
        step(pl.ds(pl.multiple_of(i * ROWS, ROWS), ROWS))
        return carry

    lax.fori_loop(0, count // ROWS, body, 0)


ROWS = 32
HALO = 16
LANES = 128


def forward_kernel(
    tokens_hbm,
    in_ref,
    out_ref,
    gu_ref,
    down_ref,
    vec_rows,
    m_ref,
    f_ref,
    middle,
    normed_two,
    mixed,
    gated,
    vec,
    *refs,
):
    (
        tokens,
        mixer_rows,
        feed_rows,
        vec_theirs,
        normed,
        wide_gated,
        inner,
        part_own,
        part_theirs,
        halo_in,
        load_sem,
        pairs,
        halo_sem,
    ) = refs[:13]
    me = Place()
    pair = me.pair()
    ahead_of, behind = me.along()
    mixer = Gathering(me, mixer_rows, m_ref, refs[13:18], ())
    feed = Gathering(me, feed_rows, f_ref, refs[18:], EVERY)
    count, width = middle.shape
    wide = inner.shape[1]
    part = mixer_rows.shape[2]
    cut = 3 * wide - part
    load = pltpu.make_async_copy(tokens_hbm, tokens, load_sem)
    load.start()
    swap_vec = remote(vec_rows, vec_theirs, pairs.at[0, 0], pairs.at[1, 0], pair)
    swap_part = remote(part_own, part_theirs, pairs.at[0, 1], pairs.at[1, 1], pair)
    me.greet((pair, ahead_of, behind))
    swap_vec.start()
    for kind in range(2):
        feed_rows[0, kind] = gu_ref[:, kind, :part].astype(BF)
        feed_rows[1, kind] = gu_ref[:, kind, part:].astype(BF)
    feed_rows[0, 2] = down_ref[:, :part].astype(BF)
    feed_rows[1, 2] = down_ref[:, part:].astype(BF)
    mixer_rows[0, :, :wide] = in_ref[:, 0, :].astype(BF)
    mixer_rows[0, :, wide : 2 * wide] = in_ref[:, 1, :].astype(BF)
    mixer_rows[0, :, 2 * wide :] = in_ref[:, 2, : part - 2 * wide].astype(BF)
    mixer_rows[1, :, :cut] = in_ref[:, 2, part - 2 * wide :].astype(BF)
    mixer_rows[1, :, cut : cut + wide] = out_ref[...].astype(BF)
    swap_vec.wait_recv()
    both = vec_rows[...] + vec_theirs[...]
    high = both.astype(BF)
    mixer_rows[1, :, cut + wide : cut + wide + LANES] = high
    mixer_rows[1, :, cut + wide + LANES :] = (both - high.astype(F32)).astype(BF)
    mixer.begin()
    feed.begin()
    mixer.enter()
    mixer.second_row()
    feed.enter()
    mixer.along_b()
    feed.second_row()
    mixer.across_b()
    feed.along_b()
    mixer.along_a()
    feed.across_b()
    mixer.across_a()
    mixer.from_sibling()
    load.wait()

    def columns(at, lanes):
        return m_ref[1, :, :, :, :, :, at : at + lanes].reshape(width, lanes)

    vec_columns = columns(cut + wide, LANES).astype(F32)
    vec_columns = vec_columns + columns(cut + wide + LANES, LANES).astype(F32)
    vec[...] = vec_columns.T[:8, :]
    gain_one = vec[0:1, :]
    gain_two = vec[1:2, :]
    chan = lax.axis_index("chan")
    tap_at = pl.ds(pl.multiple_of(chan * wide, LANES), wide)
    taps = [vec[2 + i : 3 + i, tap_at] for i in range(3)]

    def norm_step(at):
        values = tokens[at, :].astype(F32)
        normed[at, :] = (values * lax.rsqrt(mean_square(values) + norm_eps) * gain_one).astype(BF)

    row_loop(count, norm_step)

    def mixed_step(j, carry):
        half, at, lanes = in_tile(j, part)
        block = m_ref[half, :, :, :, :, :, at].reshape(width, part // 3)
        mixed[:, lanes] = dot(normed[...], block, ((1,), (0,)))
        return carry

    lax.fori_loop(0, 4, mixed_step, 0)
    for at in rows_of(count, ROWS):
        rows = slice(at.start + HALO, at.stop + HALO)
        product = (mixed[at, :wide] * mixed[at, 2 * wide :]).astype(BF)
        gated[rows, :] = product
        wide_gated[rows, :] = product.astype(F32)
    halo = remote(
        gated.at[pl.ds(count, HALO)], halo_in, halo_sem.at[0], halo_sem.at[1], ahead_of
    )
    halo.start()
    halo.wait_recv()
    starts = me.s % (lax.axis_size("seq") // 2) == 0
    carried = jnp.where(starts, 0.0, halo_in[...].astype(F32))
    gated[:HALO, :] = carried.astype(BF)
    wide_gated[:HALO, :] = carried
    for at in rows_of(count, ROWS):
        convolved = taps[0] * wide_gated[at.start + HALO - 2 : at.stop + HALO - 2, :]
        convolved = convolved + taps[1] * wide_gated[at.start + HALO - 1 : at.stop + HALO - 1, :]
        convolved = convolved + taps[2] * wide_gated[at.start + HALO : at.stop + HALO, :]
        inner[at, :] = (mixed[at, wide : 2 * wide] * convolved).astype(BF)
    for rr in range(2):
        at = slice(rr * (count // 2), (rr + 1) * (count // 2))
        part_own[at, :] = dot(inner[at, :], columns(cut, wide), ((1,), (1,))).astype(BF)
    swap_part.start()
    feed.along_a()
    feed.across_a()
    swap_part.wait_recv()

    def middle_step(at):
        total = part_own[at, :].astype(F32) + part_theirs[at, :].astype(F32)
        total = tokens[at, :].astype(F32) + total
        middle[at, :] = total
        inverse = lax.rsqrt(mean_square(total) + norm_eps)
        normed_two[at, :] = (total * inverse * gain_two).astype(BF)

    row_loop(count, middle_step)
    feed.from_sibling()
    mixer.sent()
    feed.sent()
    swap_vec.wait_send()
    swap_part.wait_send()
    halo.wait_send()


def forward(tokens, w_in, w_out, w_gu, w_down, vec_rows):
    count, width = tokens.shape
    rows, _, wide = w_in.shape
    part = w_down.shape[1] // 2
    whole = (2, RING, RING, 2, rows, part)
    vmem = pl.BlockSpec(memory_space=pltpu.VMEM)
    hbm = pl.BlockSpec(memory_space=pl.ANY)
    dma = pltpu.SemaphoreType.DMA
    mixer, feed, *rest = pl.pallas_call(
        forward_kernel,
        out_shape=(
            jax.ShapeDtypeStruct((2, *whole), BF),
            jax.ShapeDtypeStruct((2, 3, *whole), BF),
            jax.ShapeDtypeStruct((count, width), F32),
            jax.ShapeDtypeStruct((count, width), BF),
            jax.ShapeDtypeStruct((count, 3 * wide), F32),
            jax.ShapeDtypeStruct((count + HALO, wide), BF),
            jax.ShapeDtypeStruct((8, width), F32),
        ),
        in_specs=[hbm] + [vmem] * 5,
        out_specs=[vmem, hbm] + [vmem] * 5,
        scratch_shapes=[
            pltpu.VMEM((count, width), BF),
            pltpu.VMEM((2, rows, part), BF),
            pltpu.VMEM((2, 3, rows, part), BF),
            pltpu.VMEM(vec_rows.shape, F32),
            pltpu.VMEM((count, width), BF),
            pltpu.VMEM((count + HALO, wide), F32),
            pltpu.VMEM((count, wide), BF),
            pltpu.VMEM((count, width), BF),
            pltpu.VMEM((count, width), BF),
            pltpu.VMEM((HALO, wide), BF),
            dma,
            dma((2, 2)),
            dma((2,)),
            *gather_sems(),
            *gather_sems(),
        ],
        compiler_params=pltpu.CompilerParams(
            collective_id=0, has_side_effects=True, vmem_limit_bytes=48 * 1024 * 1024
        ),
        name="gather_and_forward",
    )(tokens, w_in, w_out, w_gu, w_down, vec_rows)
    total = 4 * RING * RING * rows
    return (mixer.reshape(2, total, part), feed.reshape(2, 3, total, part), *rest)


class Scattering:
    def __init__(self, me, partial, out, refs, lead, in_place=False):
        self.me, self.partial, self.out, self.lead = me, partial, out, lead
        self.in_place = in_place
        self.head = (me.core, *lead) if in_place else lead
        if in_place:
            refs = (partial, *refs[:5], None, *refs[5:])
        (
            self.mine,
            self.sib,
            self.from_a,
            self.from_b,
            self.from_y,
            self.from_core,
            self.load_sem,
            self.sib_send,
            self.sib_recv,
            self.a_send,
            self.a_recv,
            self.b_send,
            self.b_recv,
            self.last_sem,
        ) = refs

    def at(self, rr, a, b):
        return self.me.spot(rr, a % RING, b % RING)

    def add(self, where, *others):
        index = (*self.head, *where)
        total = self.mine[index].astype(F32)
        for ref, i in others:
            total = total + ref[i].astype(F32)
        self.mine[index] = total.astype(self.mine.dtype)

    def load(self):
        return pltpu.make_async_copy(self.partial.at[self.me.core], self.mine, self.load_sem)

    def to_sibling(self, at):
        me = self.me
        group = at // 8
        a = (me.pb + 2 + group + (group // 2) * (5 - 2 * group)) % RING
        b = (me.pa + 2 + (at // 2) % RING) % RING
        peer_core = 1 - me.core
        where = (me.row(at % 2), a + peer_core * (b - a), b + peer_core * (a - b))
        index = (*self.lead, *where)
        return self.sibling_copy(self.partial.at[(peer_core, *index)], where)

    def sibling_copy(self, src, where):
        i = (where[0] * RING + where[1]) * RING + where[2]
        return remote(
            src,
            self.sib.at[(*self.lead, *where)],
            self.sib_send.at[i],
            self.sib_recv.at[i],
            self.me.sibling,
        )

    def begin(self):
        if not self.in_place:
            self.load().start()

        def step(at, carry):
            self.to_sibling(at).start()
            return carry

        lax.fori_loop(0, 2 * RING * RING, step, 0)

    def with_sibling(self, rr, a, b):
        where = self.at(rr, a, b)
        index = (*self.lead, *where)
        self.sibling_copy(self.sib.at[index], where).wait_recv()
        self.add(where, (self.sib, index))

    def send_a(self, side, slot, rr, a, b):
        return remote(
            self.mine.at[(*self.head, *self.at(rr, a, b))],
            self.from_a.at[side, slot],
            self.a_send.at[side, slot],
            self.a_recv.at[side, slot],
            self.me.on_a(1 if side == 0 else 3),
        )

    def add_a(self, side, slot, rr, a, b):
        self.send_a(side, slot, rr, a, b).wait_recv()
        self.add(self.at(rr, a, b), (self.from_a, (side, slot)))

    def over_b(self, step):
        def body(j, carry):
            step((self.me.pb + 2 + j) % RING)
            return carry

        lax.fori_loop(0, RING, body, 0)

    def opposite(self):
        pa = self.me.pa

        def step(b):
            self.with_sibling(0, pa + 2, b)
            self.send_a(0, b, 0, pa + 2, b).start()
            self.with_sibling(1, pa + 2, b)
            self.send_a(1, b, 1, pa + 2, b).start()

        self.over_b(step)

    def direct(self):
        pa = self.me.pa

        def step(b):
            self.with_sibling(1, pa + 1, b)
            self.send_a(0, 8 + b, 1, pa + 1, b).start()
            self.with_sibling(0, pa + 3, b)
            self.send_a(1, 4 + b, 0, pa + 3, b).start()

        self.over_b(step)

    def onward(self):
        pa = self.me.pa

        def step(b):
            self.with_sibling(0, pa + 1, b)
            self.add_a(0, b, 0, pa + 1, b)
            self.send_a(0, 4 + b, 0, pa + 1, b).start()
            self.with_sibling(1, pa + 3, b)
            self.add_a(1, b, 1, pa + 3, b)
            self.send_a(1, 8 + b, 1, pa + 3, b).start()

        self.over_b(step)

    def kept(self):
        pa = self.me.pa

        def step(b):
            self.with_sibling(0, pa, b)
            self.with_sibling(1, pa, b)

        self.over_b(step)

    def finish_a(self, rr, b):
        slot = 4 + 4 * rr + b % RING
        pa = self.me.pa
        self.send_a(0, slot, rr, pa, b).wait_recv()
        self.send_a(1, slot, rr, pa, b).wait_recv()
        self.add(self.at(rr, pa, b), (self.from_a, (0, slot)), (self.from_a, (1, slot)))

    def send_b(self, side, slot, rr, b):
        return remote(
            self.mine.at[(*self.head, *self.at(rr, self.me.pa, b))],
            self.from_b.at[side, slot],
            self.b_send.at[side, slot],
            self.b_recv.at[side, slot],
            self.me.on_b(1 if side == 0 else 3),
        )

    def add_b(self, side, slot, rr, b):
        self.send_b(side, slot, rr, b).wait_recv()
        self.add(self.at(rr, self.me.pa, b), (self.from_b, (side, slot)))

    def ring_b(self):
        pb = self.me.pb
        self.finish_a(0, pb + 2)
        self.send_b(0, 0, 0, pb + 2).start()
        self.finish_a(1, pb + 2)
        self.send_b(1, 0, 1, pb + 2).start()
        self.finish_a(1, pb + 1)
        self.send_b(0, 2, 1, pb + 1).start()
        self.finish_a(0, pb + 3)
        self.send_b(1, 1, 0, pb + 3).start()
        self.finish_a(0, pb + 1)
        self.add_b(0, 0, 0, pb + 1)
        self.send_b(0, 1, 0, pb + 1).start()
        self.finish_a(1, pb + 3)
        self.add_b(1, 0, 1, pb + 3)
        self.send_b(1, 2, 1, pb + 3).start()
        self.finish_a(1, pb)
        self.finish_a(0, pb)

    def over(self):
        me = self.me
        return remote(
            self.mine.at[(*self.head, *self.at(1, me.pa, me.pb))],
            self.from_y,
            self.last_sem.at[0],
            self.last_sem.at[1],
            me.other_y,
        )

    def last(self):
        me = self.me
        return remote(
            self.mine.at[(*self.head, *self.at(0, me.pa, me.pb), 1 - me.core)],
            self.from_core,
            self.last_sem.at[2],
            self.last_sem.at[3],
            me.sibling,
        )

    def across_y(self):
        pb = self.me.pb
        self.add_b(0, 2, 1, pb)
        self.add_b(1, 2, 1, pb)
        self.over().start()
        self.add_b(0, 1, 0, pb)
        self.add_b(1, 1, 0, pb)

    def across_cores(self):
        me = self.me
        self.over().wait_recv()
        self.add(self.at(0, me.pa, me.pb), (self.from_y, ...))
        self.last().start()
        self.out[me.core] = self.mine[
            (*self.head, *self.at(0, me.pa, me.pb), me.core)
        ].astype(F32)

    def finish(self):
        self.last().wait_recv()
        self.out[1 - self.me.core] = self.from_core[...].astype(F32)
        self.last().wait_send()
        self.over().wait_send()

        def sent_sibling(at, carry):
            self.to_sibling(at).wait_send()
            return carry

        lax.fori_loop(0, 2 * RING * RING, sent_sibling, 0)

        def sent_a(slot, carry):
            self.send_a(0, slot, 0, 0, 0).wait_send()
            self.send_a(1, slot, 0, 0, 0).wait_send()
            return carry

        lax.fori_loop(0, 3 * RING, sent_a, 0)
        for slot in range(3):
            self.send_b(0, slot, 0, 0).wait_send()
            self.send_b(1, slot, 0, 0).wait_send()


def scatter_scratch(kinds, rows, width, in_place=False):
    blocks = 2 * RING * RING
    dma = pltpu.SemaphoreType.DMA
    mine = [] if in_place else [pltpu.VMEM((*kinds, 2, RING, RING, 2, rows, width), BF)]
    return [
        *mine,
        pltpu.VMEM((*kinds, 2, RING, RING, 2, rows, width), BF),
        pltpu.VMEM((2, 3 * RING, *kinds, 2, rows, width), BF),
        pltpu.VMEM((2, 3, *kinds, 2, rows, width), BF),
        pltpu.VMEM((*kinds, 2, rows, width), BF),
        pltpu.VMEM((*kinds, rows, width), BF),
        *([] if in_place else [dma]),
        dma((blocks,)),
        dma((blocks,)),
        dma((2, 3 * RING)),
        dma((2, 3 * RING)),
        dma((2, 3)),
        dma((2, 3)),
        dma((4,)),
    ]


def backward_kernel(
    pf_ref,
    back_hbm,
    feed_hbm,
    middle_hbm,
    cot_hbm,
    tokens_hbm,
    mixed_hbm,
    gated_hbm,
    weights_hbm,
    vec_hbm,
    om_ref,
    of_ref,
    block_ref,
    grad_ref,
    *refs,
):
    (
        back_own,
        feed_own,
        middle,
        cot,
        tokens,
        mixed,
        gated,
        weights,
        vec,
        back_theirs,
        feed_theirs,
        one_theirs,
        branch,
        turned,
        inner,
        wide_gated,
        wide_conv,
        back_inner,
        back_mixed,
        sums,
        halo_out,
        halo_in,
        pm_ref,
        loads,
        pairs,
        halo_sem,
        vec_own,
        vec_theirs,
        vec_sem,
    ) = refs[:29]
    me = Place()
    pair = me.pair()
    ahead_of, behind = me.along()
    chan = lax.axis_index("chan")
    mixer = Scattering(me, pm_ref, om_ref, refs[29:41], (), in_place=True)
    feed = Scattering(me, pf_ref, of_ref, refs[41:], EVERY)
    one_own, one_sum = cot, block_ref
    count, width = middle.shape
    wide = back_inner.shape[1]
    part = weights.shape[2]

    def load(i):
        src, dst = (
            (back_hbm, back_own),
            (middle_hbm, middle),
            (cot_hbm, cot),
            (vec_hbm, vec),
            (weights_hbm, weights),
            (mixed_hbm, mixed),
            (gated_hbm, gated),
            (tokens_hbm, tokens),
            (feed_hbm, feed_own),
        )[i]
        return pltpu.make_async_copy(src, dst, loads.at[i])

    def exchange(i):
        src, dst = ((back_own, back_theirs), (feed_own, feed_theirs), (one_own, one_theirs))[i]
        return remote(src, dst, pairs.at[0, i], pairs.at[1, i], pair)

    for i in range(9):
        load(i).start()
    me.greet((pair, ahead_of, behind))
    load(0).wait()
    exchange(0).start()
    feed.begin()
    for i in range(1, 9):
        load(i).wait()
    feed.load().wait()
    feed.opposite()

    gain_one = vec[0:1, :]
    gain_two = vec[1:2, :]
    tap_at = pl.ds(pl.multiple_of(chan * wide, LANES), wide)
    taps = [vec[2 + i : 3 + i, tap_at] for i in range(3)]
    sums[...] = jnp.zeros_like(sums)
    wide_gated[...] = gated[...].astype(F32)

    def convolved(at):
        total = taps[0] * wide_gated[at.start + HALO - 2 : at.stop + HALO - 2, :]
        total = total + taps[1] * wide_gated[at.start + HALO - 1 : at.stop + HALO - 1, :]
        return total + taps[2] * wide_gated[at.start + HALO : at.stop + HALO, :]

    for at in rows_of(count, ROWS):
        inner[at, :] = (mixed[at, wide : 2 * wide] * convolved(at)).astype(BF)
    feed.direct()
    feed.onward()

    exchange(0).wait_recv()
    exchange(1).start()

    def norm_step(i, carry):
        at = pl.ds(pl.multiple_of(i * ROWS, ROWS), ROWS)
        mid = middle[at, :]
        inverse = lax.rsqrt(mean_square(mid) + norm_eps)
        own = back_own[at, :].astype(F32)
        back = own + back_theirs[at, :].astype(F32)
        total = cot[at, :].astype(F32) + norm_back(mid, inverse, gain_two, back)
        grad_ref[at, :] = total
        branch[at, :] = total.astype(BF)
        sums[1:2, :] += jnp.sum(own * mid * inverse, axis=0, keepdims=True)
        return carry

    lax.fori_loop(0, count // ROWS, norm_step, 0)
    cut = 3 * wide - part
    w_out = weights[1, :, cut : cut + wide]
    back_inner[...] = dot(branch[...], w_out, ((1,), (0,)))
    for at in rows_of(count, ROWS):
        wide_conv[at, :] = (back_inner[at, :] * mixed[at, wide : 2 * wide]).astype(BF).astype(F32)
    halo_out[...] = wide_conv[0:HALO, :].astype(BF)
    halo = remote(halo_out, halo_in, halo_sem.at[0], halo_sem.at[1], behind)
    halo.start()
    turned[...] = branch[...].T
    term_out = dot(turned[...], inner[...], ((1,), (0,))).astype(BF)
    shape = pm_ref.shape[1:-1]
    pm_ref[1, :, :, :, :, :, cut : cut + wide] = term_out.reshape(*shape, wide)
    for at in rows_of(count, ROWS):
        values = tokens[at, :].astype(F32)
        inverse = lax.rsqrt(mean_square(values) + norm_eps)
        branch[at, :] = (values * inverse * gain_one).astype(BF)
    turned[...] = branch[...].T
    feed.kept()
    halo.wait_recv()
    last = me.s % (lax.axis_size("seq") // 2) == lax.axis_size("seq") // 2 - 1
    wide_conv[count : count + HALO, :] = jnp.where(last, 0.0, halo_in[...].astype(F32))
    for at in rows_of(count, ROWS):
        back_gated = (
            taps[0] * wide_conv[at.start + 2 : at.stop + 2, :]
            + taps[1] * wide_conv[at.start + 1 : at.stop + 1, :]
            + taps[2] * wide_conv[at, :]
        )
        back_mixed[at, :wide] = (back_gated * mixed[at, 2 * wide :]).astype(BF)
        back_mixed[at, wide : 2 * wide] = (back_inner[at, :] * convolved(at)).astype(BF)
        back_mixed[at, 2 * wide :] = (back_gated * mixed[at, :wide]).astype(BF)
        for i in range(3):
            shift = HALO - 2 + i
            term = wide_conv[at, :] * wide_gated[at.start + shift : at.stop + shift, :]
            sums[2 + i : 3 + i, tap_at] += jnp.sum(term, axis=0, keepdims=True)

    one_sum[...] = jnp.zeros_like(one_sum)

    def back_step(j, carry):
        half, at, lanes = in_tile(j, part)
        one_sum[...] += dot(back_mixed[:, lanes], weights[half, :, at], ((1,), (1,)))
        return carry

    lax.fori_loop(0, 4, back_step, 0)

    def gain_step(i, carry):
        at = pl.ds(pl.multiple_of(i * ROWS, ROWS), ROWS)
        values = tokens[at, :].astype(F32)
        inverse = lax.rsqrt(mean_square(values) + norm_eps)
        own = one_sum[at, :]
        one_own[at, :] = own.astype(BF)
        sums[0:1, :] += jnp.sum(own * values * inverse, axis=0, keepdims=True)
        return carry

    lax.fori_loop(0, count // ROWS, gain_step, 0)
    exchange(2).start()

    def term_step(j, carry):
        half, at, lanes = in_tile(j, part)
        term = dot(turned[...], back_mixed[:, lanes], ((1,), (0,))).astype(BF)
        pm_ref[half, :, :, :, :, :, at] = term.reshape(*shape, part // 3)
        return carry

    lax.fori_loop(0, 4, term_step, 0)
    vec_term = sums[...].T.astype(BF)
    lanes = vec_term.shape[1]
    pm_ref[1, :, :, :, :, :, cut + wide : cut + wide + lanes] = vec_term.reshape(*shape, lanes)
    pm_ref[1, :, :, :, :, :, cut + wide + lanes :] = jnp.zeros(
        (*shape, part - cut - wide - lanes), BF
    )
    mixer.begin()
    feed.ring_b()
    mixer.opposite()
    mixer.direct()
    feed.across_y()
    mixer.onward()
    mixer.kept()
    feed.across_cores()
    exchange(1).wait_recv()

    def out_step(i, carry):
        at = pl.ds(pl.multiple_of(i * ROWS, ROWS), ROWS)
        total = feed_own[at, :].astype(F32) + feed_theirs[at, :].astype(F32)
        block_ref[at, :] = middle[at, :] + total
        return carry

    lax.fori_loop(0, count // ROWS, out_step, 0)
    mixer.ring_b()
    mixer.across_y()
    mixer.across_cores()
    exchange(2).wait_recv()

    def grad_step(i, carry):
        at = pl.ds(pl.multiple_of(i * ROWS, ROWS), ROWS)
        values = tokens[at, :].astype(F32)
        inverse = lax.rsqrt(mean_square(values) + norm_eps)
        back = one_own[at, :].astype(F32) + one_theirs[at, :].astype(F32)
        grad_ref[at, :] += norm_back(values, inverse, gain_one, back)
        return carry

    lax.fori_loop(0, count // ROWS, grad_step, 0)
    mixer.finish()
    vec_own[...] = om_ref[1, :, cut + wide : cut + wide + LANES]
    swap_vec = remote(vec_own, vec_theirs, vec_sem.at[0], vec_sem.at[1], pair)
    swap_vec.start()
    feed.finish()
    swap_vec.wait()
    om_ref[1, :, cut + wide : cut + wide + LANES] = vec_own[...] + vec_theirs[...]
    halo.wait_send()
    for i in range(3):
        exchange(i).wait_send()


def backward(term_feed, back_two, feed_part, middle, cotangent, tokens, mixed, gated, weights, vec):
    halves, kinds, total, width = term_feed.shape
    rows = total // (4 * RING * RING)
    whole = (2, RING, RING, 2, rows, width)
    count, features = middle.shape
    wide = gated.shape[1]
    dma = pltpu.SemaphoreType.DMA

    def like(x):
        return pltpu.VMEM(x.shape, x.dtype)

    low_act = pltpu.VMEM((count, features), BF)
    return pl.pallas_call(
        backward_kernel,
        out_shape=(
            jax.ShapeDtypeStruct((halves, rows, width), F32),
            jax.ShapeDtypeStruct((halves, kinds, rows, width), F32),
            jax.ShapeDtypeStruct((count, features), F32),
            jax.ShapeDtypeStruct((count, features), F32),
        ),
        in_specs=[pl.BlockSpec(memory_space=pl.ANY)] * 10,
        out_specs=[pl.BlockSpec(memory_space=pltpu.VMEM)] * 4,
        scratch_shapes=[
            *[like(x) for x in (back_two, feed_part, middle, cotangent, tokens, mixed, gated)],
            like(weights),
            like(vec),
            low_act,
            low_act,
            low_act,
            low_act,
            pltpu.VMEM((features, count), BF),
            pltpu.VMEM((count, wide), BF),
            pltpu.VMEM((count + HALO, wide), F32),
            pltpu.VMEM((count + HALO, wide), F32),
            pltpu.VMEM((count, wide), F32),
            pltpu.VMEM((count, 3 * wide), BF),
            pltpu.VMEM((128, features), F32),
            pltpu.VMEM((HALO, wide), BF),
            pltpu.VMEM((HALO, wide), BF),
            pltpu.VMEM((halves, *whole), BF),
            dma((9,)),
            dma((2, 3)),
            dma((2,)),
            pltpu.VMEM((rows, LANES), F32),
            pltpu.VMEM((rows, LANES), F32),
            dma((2,)),
            *scatter_scratch((), rows, width, in_place=True),
            *scatter_scratch((kinds,), rows, width),
        ],
        compiler_params=pltpu.CompilerParams(
            collective_id=1, has_side_effects=True, vmem_limit_bytes=60 * 1024 * 1024
        ),
        name="backward_and_scatter",
    )(
        term_feed.reshape(halves, kinds, *whole),
        back_two,
        feed_part,
        middle,
        cotangent,
        tokens,
        mixed,
        gated,
        weights,
        vec,
    )


def feed_kernel(n_ref, c_ref, w_ref, t_ref, out_ref, back_ref, n_turned, c_turned, out_sum, back_sum):
    step = pl.program_id(0)

    @pl.when(step == 0)
    def _():
        n_turned[...] = n_ref[...].T
        c_turned[...] = c_ref[...].T
        out_sum[...] = jnp.zeros_like(out_sum)
        back_sum[...] = jnp.zeros_like(back_sum)

    def weight(kind):
        return jnp.concatenate([w_ref[0, kind], w_ref[1, kind]], axis=1)

    def keep(kind, term):
        term = term.astype(BF)
        lanes = term.shape[1] // 2
        t_ref[0, kind] = term[:, :lanes]
        t_ref[1, kind] = term[:, lanes:]

    w_gate, w_up, w_down = weight(0), weight(1), weight(2)
    normed = n_ref[...]
    back_out = c_ref[...]
    gate = dot(normed, w_gate, ((1,), (0,)))
    up = dot(normed, w_up, ((1,), (0,)))
    back_hidden = dot(back_out, w_down, ((1,), (0,)))
    sig = jax.nn.sigmoid(gate)
    act = gate * sig
    hidden = (act * up).astype(BF)
    back_gate = (back_hidden * up * sig * (1.0 + gate * (1.0 - sig))).astype(BF)
    back_up = (back_hidden * act).astype(BF)
    out_sum[...] += dot(hidden, w_down, ((1,), (1,)))
    back_sum[...] += dot(back_gate, w_gate, ((1,), (1,))) + dot(back_up, w_up, ((1,), (1,)))
    keep(0, dot(n_turned[...], back_gate, ((1,), (0,))))
    keep(1, dot(n_turned[...], back_up, ((1,), (0,))))
    keep(2, dot(c_turned[...], hidden, ((1,), (0,))))

    @pl.when(step == pl.num_programs(0) - 1)
    def _():
        out_ref[...] = out_sum[...].astype(BF)
        back_ref[...] = back_sum[...].astype(BF)


def feed_forward(normed, cotangent, weights):
    halves, kinds, total, width = weights.shape
    tokens = normed.shape[0]
    lanes = 128
    whole = pl.BlockSpec((tokens, total), lambda j: (0, 0))
    part = pl.BlockSpec((halves, kinds, total, lanes), lambda j: (0, 0, 0, j))
    flops = 9 * 2 * tokens * total * halves * width
    return pl.pallas_call(
        feed_kernel,
        grid=(width // lanes,),
        out_shape=(
            jax.ShapeDtypeStruct(weights.shape, BF),
            jax.ShapeDtypeStruct((tokens, total), BF),
            jax.ShapeDtypeStruct((tokens, total), BF),
        ),
        in_specs=[whole, whole, part],
        out_specs=[part, whole, whole],
        scratch_shapes=[
            pltpu.VMEM((total, tokens), BF),
            pltpu.VMEM((total, tokens), BF),
            pltpu.VMEM((tokens, total), F32),
            pltpu.VMEM((tokens, total), F32),
        ],
        compiler_params=pltpu.CompilerParams(vmem_limit_bytes=48 * 1024 * 1024),
        cost_estimate=pl.CostEstimate(
            flops=flops, bytes_accessed=4 * halves * kinds * total * width, transcendentals=0
        ),
        name="feed_forward",
    )(normed, cotangent, weights)


def dot(a, b, dims):
    return lax.dot_general(a, b, (dims, ((), ())), preferred_element_type=F32)


def norm_back(values, inverse, gain, back):
    scaled = back * gain
    mean = jnp.mean(scaled * values, axis=-1, keepdims=True)
    return inverse * (scaled - values * (inverse * inverse) * mean)


def adam_update(weight, moment_one, second, gradient, step_rate, weight_decay):
    first_new = beta_one * moment_one + (1.0 - beta_one) * gradient
    second_new = beta_two * second + (1.0 - beta_two) * gradient * gradient
    first_hat = first_new / (1.0 - beta_one**STEP)
    second_hat = second_new / (1.0 - beta_two**STEP)
    weight_new = weight - step_rate * (
        first_hat / (jnp.sqrt(second_hat) + adam_eps) + weight_decay * weight
    )
    return (weight_new, first_new, second_new)


def adam_kernel(om_ref, of_ref, *refs):
    chan = lax.axis_index("chan")
    w_in, w_out, w_gu, w_down, vectors = [refs[3 * i : 3 * i + 3] for i in range(5)]
    in_new, out_new, gu_new, down_new, vec_new = [refs[15 + 3 * i : 18 + 3 * i] for i in range(5)]
    part = om_ref.shape[2]
    wide = w_out[0].shape[1]
    cut = 3 * wide - part

    def update(arrays, results, index, gradient, rate=rate_matrix, decay=decay_matrix):
        new = adam_update(*[a[index] for a in arrays], gradient, rate, decay)
        for ref, value in zip(results, new):
            ref[index] = value

    def both(at):
        return slice(None), at

    for c in range(2):
        at = slice(c * wide, (c + 1) * wide)
        update(w_in, in_new, (slice(None), c), om_ref[0, :, at])
    left = part - 2 * wide
    update(w_in, in_new, (slice(None), 2, slice(0, left)), om_ref[0, :, 2 * wide :])
    update(w_in, in_new, (slice(None), 2, slice(left, wide)), om_ref[1, :, :cut])
    update(w_out, out_new, both(slice(None)), om_ref[1, :, cut : cut + wide])
    for half in range(2):
        at = slice(half * part, (half + 1) * part)
        for kind in range(2):
            update(w_gu, gu_new, (slice(None), kind, at), of_ref[half, kind])
        update(w_down, down_new, both(at), of_ref[half, 2])
    rows = om_ref.shape[1]
    block = om_ref[1, :, cut + wide : cut + wide + LANES]
    turned = jnp.concatenate([block, jnp.zeros((LANES - rows, LANES), F32)], axis=0).T
    own = jnp.where(chan == 0, turned[:5, : rows // 2], turned[:5, rows // 2 : rows])
    update(vectors, vec_new, both(slice(None)), own, rate_vector, 0.0)


def adam(sum_mixer, sum_feed, arrays):
    def whole(x):
        return pl.BlockSpec(x.shape, lambda i, n=x.ndim: (0,) * n)

    ins = (sum_mixer, sum_feed, *arrays)
    return pl.pallas_call(
        adam_kernel,
        grid=(1,),
        out_shape=[jax.ShapeDtypeStruct(x.shape, x.dtype) for x in arrays],
        in_specs=[whole(x) for x in ins],
        out_specs=[whole(x) for x in arrays],
        compiler_params=pltpu.CompilerParams(vmem_limit_bytes=48 * 1024 * 1024),
        name="adam",
    )(*ins)


def body(
    tokens,
    cotangent,
    w_in,
    w_in_m,
    w_in_v,
    w_out,
    w_out_m,
    w_out_v,
    w_gu,
    w_gu_m,
    w_gu_v,
    w_down,
    w_down_m,
    w_down_v,
    vectors,
    vectors_m,
    vectors_v,
):
    chan = lax.axis_index("chan")
    turned = vectors.T
    none = jnp.zeros_like(turned)
    vec_rows = jnp.where(
        chan == 0,
        jnp.concatenate([turned, none], axis=0),
        jnp.concatenate([none, turned], axis=0),
    )
    vec_rows = jnp.pad(vec_rows, ((0, 0), (0, LANES - vec_rows.shape[1])))
    full_mixer, full_feed, middle, normed_two, mixed, gated, vec = forward(
        tokens, w_in, w_out, w_gu, w_down, vec_rows
    )
    term_feed, feed_part, back_two_part = feed_forward(normed_two, cotangent, full_feed)
    sum_mixer, sum_feed, block_out, input_grad = backward(
        term_feed, back_two_part, feed_part, middle, cotangent, tokens, mixed, gated, full_mixer, vec
    )
    state = (
        *(w_in, w_in_m, w_in_v),
        *(w_out, w_out_m, w_out_v),
        *(w_gu, w_gu_m, w_gu_v),
        *(w_down, w_down_m, w_down_v),
        *(vectors, vectors_m, vectors_v),
    )
    return (block_out, input_grad, *adam(sum_mixer, sum_feed, state))


def solution(mesh):
    matrices = [P("seq", None, "chan")] * 3 + [P("seq", "chan")] * 3
    weights = (*matrices, *matrices, *[P(None, ("seq", "chan"))] * 3)
    return jax.shard_map(
        body,
        mesh=mesh,
        in_specs=(P("seq", None), P("seq", None), *weights),
        out_specs=(P("seq", None), P("seq", None), *weights),
        check_vma=False,
    )
```

```python
import jax
import jax.numpy as jnp
from jax import lax
from jax.experimental import pallas as pl
from jax.experimental.pallas import tpu as pltpu
from jax.sharding import PartitionSpec as P

STEP = 10
norm_eps = 1e-05
beta_one = 0.9
beta_two = 0.95
adam_eps = 1e-08
rate_matrix = 0.05
rate_vector = 0.5
decay_matrix = 0.1

MESH = pl.DeviceIdType.MESH
BF = jnp.bfloat16
F32 = jnp.float32

RING = 4
PLANE = ((1, 0), (0, 3), (0, 1), (1, 3), (1, 1), (0, 2), (1, 2))


class Place:
    def __init__(self):
        s = lax.axis_index("seq")
        core = s % 2
        z = (s // 2) % RING
        x = (s // (2 * RING)) % RING
        y = s // (2 * RING * RING)
        self.s, self.core, self.y = s, core, y
        self.pa = x + core * (z - x)
        self.pb = z + core * (x - z)
        self.x, self.z = x, z
        step_x, step_z = 2 * RING, 2
        self.step_a = step_x + core * (step_z - step_x)
        self.step_b = step_z + core * (step_x - step_z)
        self.sibling = s + 1 - 2 * core
        self.other_y = s + (1 - 2 * y) * 2 * RING * RING

    def on_a(self, off):
        return self.s + ((self.pa + off) % RING - self.pa) * self.step_a

    def on_b(self, off):
        return self.s + ((self.pb + off) % RING - self.pb) * self.step_b

    def on_plane(self, rr, off):
        return self.on_b(off) + rr * (1 - 2 * self.y) * 2 * RING * RING

    def row(self, rr):
        return self.y + rr * (1 - 2 * self.y)

    def spot(self, rr, a, b):
        xi = a + self.core * (b - a)
        zi = b + self.core * (a - b)
        return self.row(rr), xi, zi

    def peers(self):
        near = (self.sibling, self.other_y, self.on_a(1), self.on_a(3), self.on_b(1), self.on_b(3))
        far = [self.on_plane(rr, off) for rr, off in PLANE if (rr, off) not in ((1, 0), (0, 3), (0, 1))]
        return [{"seq": peer} for peer in (*near, *far)]

    def along(self):
        count = lax.axis_size("seq")
        return {"seq": (self.s + 1) % count}, {"seq": (self.s + count - 1) % count}

    def pair(self):
        return {"chan": 1 - lax.axis_index("chan")}

    def greet(self, more=()):
        barrier = pltpu.get_barrier_semaphore()
        peers = [*self.peers(), *more]
        for peer in peers:
            pl.semaphore_signal(barrier, inc=1, device_id=peer, device_id_type=MESH)
        pl.semaphore_wait(barrier, len(peers))


def remote(src, dst, send_sem, recv_sem, target):
    return pltpu.make_async_remote_copy(
        src_ref=src,
        dst_ref=dst,
        send_sem=send_sem,
        recv_sem=recv_sem,
        device_id=target if isinstance(target, dict) else {"seq": target},
        device_id_type=MESH,
    )


class Gathering:
    def __init__(self, me, shard, out, sems, lead):
        self.me, self.shard, self.out, self.lead = me, shard, out, lead
        self.local_sem, self.first_sem, self.send, self.recv, self.sib_recv = sems
        self.targets = (
            me.sibling, me.other_y, me.on_a(1), me.on_a(3), me.on_b(1), me.on_b(3)
        )

    def block(self, half, *where):
        return self.out.at[(half, *self.lead, *where)]

    def copy(self, kind, rr, a, b):
        yy, xi, zi = self.me.spot(rr, a % RING, b % RING)
        block = self.block(self.me.core, yy, xi, zi)
        at = (yy * RING + xi) * RING + zi
        got = self.sib_recv if kind == SIB else self.recv
        return remote(block, block, self.send.at[kind, at], got.at[at], self.targets[kind])

    def arrived(self, rr, a, b):
        self.copy(AR, rr, a, b).wait_recv()

    def start(self, kinds, rr, a, b):
        for kind in kinds:
            self.copy(kind, rr, a, b).start()

    def own(self):
        me = self.me
        return pltpu.make_async_copy(
            self.shard.at[me.core],
            self.block(me.core, me.y, me.x, me.z, me.core),
            self.local_sem,
        )

    def first(self, half, core):
        me = self.me
        return remote(
            self.shard.at[half],
            self.block(half, me.y, me.x, me.z, core),
            self.first_sem.at[0],
            self.first_sem.at[1],
            me.sibling,
        )

    def begin(self):
        me = self.me
        self.own().start()
        self.first(1 - me.core, me.core).start()

    def enter(self):
        me = self.me
        self.own().wait()
        self.first(me.core, 1 - me.core).wait_recv()
        self.start((YY, AR, AL, BR, BL, SIB), 0, me.pa, me.pb)

    def plane_copy(self, rr, off):
        me = self.me
        block = self.block(me.core, me.y, me.x, me.z)
        at = (me.y * RING + me.x) * RING + me.z
        send = self.send.at[YY, rr * RING + off]
        return remote(block, block, send, self.recv.at[at], me.on_plane(rr, off))

    def enter_plane(self):
        me = self.me
        self.own().wait()
        self.first(me.core, 1 - me.core).wait_recv()
        for rr, off in PLANE:
            self.plane_copy(rr, off).start()
        self.start((AR, AL, SIB), 0, me.pa, me.pb)

    def along_plane(self):
        me = self.me
        for rr, off in PLANE:
            self.arrived(rr, me.pa, me.pb + off)
            self.start((AR, AL, SIB), rr, me.pa, me.pb + off)

    def second_row(self):
        me = self.me
        self.copy(YY, 1, me.pa, me.pb).wait_recv()
        self.start((AR, AL, BR, BL, SIB), 1, me.pa, me.pb)

    def along_b(self):
        pa, pb = self.me.pa, self.me.pb
        for rr in range(2):
            self.arrived(rr, pa, pb + 3)
            self.start((BR, AR, AL, SIB) if rr == 0 else (AR, AL, SIB), rr, pa, pb + 3)
            self.arrived(rr, pa, pb + 1)
            self.start((BL, AR, AL, SIB) if rr == 1 else (AR, AL, SIB), rr, pa, pb + 1)

    def across_b(self):
        pa, pb = self.me.pa, self.me.pb
        for rr in range(2):
            self.arrived(rr, pa, pb + 2)
            self.start((AR, AL, SIB), rr, pa, pb + 2)

    def order(self, j):
        return self.me.pb + (j * 3) % 4 - (j // 2) * ((j * 3) % 4 - (j - 1))

    def along_a(self):
        pa = self.me.pa

        def step(j, carry):
            b = self.order(j)
            self.arrived(0, pa + 3, b)
            self.start((AR, SIB), 0, pa + 3, b)
            self.arrived(0, pa + 1, b)
            self.start((SIB,), 0, pa + 1, b)
            self.arrived(1, pa + 3, b)
            self.start((SIB,), 1, pa + 3, b)
            self.arrived(1, pa + 1, b)
            self.start((AL, SIB), 1, pa + 1, b)
            return carry

        lax.fori_loop(0, RING, step, 0)

    def across_a(self):
        pa = self.me.pa

        def step(j, carry):
            b = self.order(j)
            for rr in range(2):
                self.arrived(rr, pa + 2, b)
                self.start((SIB,), rr, pa + 2, b)
            return carry

        lax.fori_loop(0, RING, step, 0)

    def from_sibling(self):
        me = self.me

        def step(at, carry):
            where = (at // 16, (at // 4) % 4, at % 4)
            for half, wait in ((1 - me.core, "r"), (me.core, "s")):
                block = self.block(half, *where)
                copy = remote(block, block, self.send.at[SIB, at], self.sib_recv.at[at], me.sibling)
                copy.wait_recv() if wait == "r" else copy.wait_send()
            return carry

        lax.fori_loop(0, 2 * RING * RING, step, 0)

    def sent(self, plane=False):
        me = self.me
        pa, pb = me.pa, me.pb
        self.first(1 - me.core, me.core).wait_send()
        if plane:
            for rr, off in PLANE:
                self.plane_copy(rr, off).wait_send()
        else:
            self.copy(YY, 0, pa, pb).wait_send()
            for rr in range(2):
                self.copy(BR, rr, pa, pb).wait_send()
                self.copy(BL, rr, pa, pb).wait_send()
            self.copy(BR, 0, pa, pb + 3).wait_send()
            self.copy(BL, 1, pa, pb + 1).wait_send()

        def step(b, carry):
            for rr in range(2):
                self.copy(AR, rr, pa, b).wait_send()
                self.copy(AL, rr, pa, b).wait_send()
            self.copy(AR, 0, pa + 3, b).wait_send()
            self.copy(AL, 1, pa + 1, b).wait_send()
            return carry

        lax.fori_loop(0, RING, step, 0)


SIB, YY, AR, AL, BR, BL = range(6)
EVERY = (slice(None),)


def gather_sems():
    blocks = 2 * RING * RING
    return [
        pltpu.SemaphoreType.DMA,
        pltpu.SemaphoreType.DMA((2,)),
        pltpu.SemaphoreType.DMA((6, blocks)),
        pltpu.SemaphoreType.DMA((blocks,)),
        pltpu.SemaphoreType.DMA((blocks,)),
    ]


def rows_of(stop, step, start=0):
    return [slice(i, i + step) for i in range(start, stop, step)]


def mean_square(values):
    return jnp.mean(values * values, axis=-1, keepdims=True)


def in_tile(j, part):
    lanes = part // 3
    at = pl.ds(pl.multiple_of((j % 3) * lanes, 128), lanes)
    return j // 3, at, pl.ds(pl.multiple_of(j * lanes, 128), lanes)


def row_loop(count, step, start=0, rows=32):
    def body(i, carry):
        step(pl.ds(pl.multiple_of(start + i * rows, HALO), rows))
        return carry

    lax.fori_loop(0, count // rows, body, 0)


ROWS = 32
HALO = 16
LANES = 128


def forward_kernel(
    tokens_hbm,
    in_ref,
    out_ref,
    gu_ref,
    down_ref,
    vec_ref,
    m_hbm,
    f_ref,
    middle,
    normed_two,
    mixed_hbm,
    gated_hbm,
    vec,
    *refs,
):
    (
        m_ref,
        mixed,
        gated,
        vec_square,
        vec_rows,
        out_sems,
        tokens,
        mixer_rows,
        feed_rows,
        vec_theirs,
        normed,
        wide_gated,
        inner,
        part_own,
        part_theirs,
        halo_in,
        load_sem,
        pairs,
        halo_sem,
    ) = refs[:19]
    me = Place()
    pair = me.pair()
    ahead_of, behind = me.along()
    mixer = Gathering(me, mixer_rows, m_ref, refs[19:24], ())
    feed = Gathering(me, feed_rows, f_ref, refs[24:], EVERY)
    count, width = middle.shape
    wide = inner.shape[1]
    part = mixer_rows.shape[2]
    cut = 3 * wide - part
    load = pltpu.make_async_copy(tokens_hbm, tokens, load_sem)
    load.start()
    chan = lax.axis_index("chan")
    vec_square[...] = jnp.zeros_like(vec_square)
    vec_square[: vec_ref.shape[0], : vec_ref.shape[1]] = vec_ref[...]
    turned = vec_square[...].T
    own_rows = vec_ref.shape[1]
    vec_rows[...] = jnp.zeros_like(vec_rows)
    vec_rows[pl.ds(pl.multiple_of(chan * own_rows, own_rows), own_rows), :] = turned[:own_rows, :]

    def keep(i):
        src, dst = ((m_ref, m_hbm), (mixed, mixed_hbm), (gated, gated_hbm))[i]
        return pltpu.make_async_copy(src, dst, out_sems.at[i])

    swap_vec = remote(vec_rows, vec_theirs, pairs.at[0, 0], pairs.at[1, 0], pair)

    def swap_part(lo):
        at = pl.ds(lo, count // 2)
        i = 1 if lo else 2
        src, dst = part_own.at[at], part_theirs.at[at]
        return remote(src, dst, pairs.at[0, i], pairs.at[1, i], pair)

    me.greet((pair, ahead_of, behind))
    swap_vec.start()
    for kind in range(2):
        feed_rows[0, kind] = gu_ref[:, kind, :part].astype(BF)
        feed_rows[1, kind] = gu_ref[:, kind, part:].astype(BF)
    feed_rows[0, 2] = down_ref[:, :part].astype(BF)
    feed_rows[1, 2] = down_ref[:, part:].astype(BF)
    mixer_rows[0, :, :wide] = in_ref[0].astype(BF)
    mixer_rows[0, :, wide : 2 * wide] = in_ref[1].astype(BF)
    mixer_rows[0, :, 2 * wide :] = in_ref[2, :, : part - 2 * wide].astype(BF)
    mixer_rows[1, :, :cut] = in_ref[2, :, part - 2 * wide :].astype(BF)
    mixer_rows[1, :, cut : cut + wide] = out_ref[...].astype(BF)
    feed.begin()
    swap_vec.wait_recv()
    both = vec_rows[...] + vec_theirs[...]
    high = both.astype(BF)
    mixer_rows[1, :, cut + wide : cut + wide + LANES] = high
    mixer_rows[1, :, cut + wide + LANES :] = (both - high.astype(F32)).astype(BF)
    mixer.begin()
    feed.enter()
    mixer.enter_plane()
    feed.second_row()
    mixer.along_plane()
    feed.along_b()
    mixer.along_a()
    feed.across_b()
    mixer.across_a()
    mixer.from_sibling()
    keep(0).start()
    load.wait()

    def columns(at, lanes):
        return m_ref[1, :, :, :, :, :, at : at + lanes].reshape(width, lanes)

    vec_columns = columns(cut + wide, LANES).astype(F32)
    vec_columns = vec_columns + columns(cut + wide + LANES, LANES).astype(F32)
    vec[...] = vec_columns.T[:8, :]
    gain_one = vec[0:1, :]
    gain_two = vec[1:2, :]
    tap_at = pl.ds(pl.multiple_of(chan * wide, LANES), wide)
    taps = [vec[2 + i : 3 + i, tap_at] for i in range(3)]

    def norm_step(at):
        values = tokens[at, :].astype(F32)
        normed[at, :] = (values * lax.rsqrt(mean_square(values) + norm_eps) * gain_one).astype(BF)

    row_loop(count, norm_step)

    half = count // 2
    edge = half - HALO

    def gated_rows(lo, hi):
        def mixed_step(j, carry):
            which, at, lanes = in_tile(j, part)
            block = m_ref[which, :, :, :, :, :, at].reshape(width, part // 3)
            mixed[lo:hi, lanes] = dot(normed[lo:hi, :], block, ((1,), (0,)))
            return carry

        lax.fori_loop(0, 4, mixed_step, 0)
        for at in rows_of(hi, HALO, lo):
            rows = slice(at.start + HALO, at.stop + HALO)
            product = (mixed[at, :wide] * mixed[at, 2 * wide :]).astype(BF)
            gated[rows, :] = product
            wide_gated[rows, :] = product.astype(F32)

    def branch_rows(lo, hi):
        for at in rows_of(hi, ROWS, lo):
            convolved = taps[0] * wide_gated[at.start + HALO - 2 : at.stop + HALO - 2, :]
            convolved = convolved + taps[1] * wide_gated[at.start + HALO - 1 : at.stop + HALO - 1, :]
            convolved = convolved + taps[2] * wide_gated[at.start + HALO : at.stop + HALO, :]
            inner[at, :] = (mixed[at, wide : 2 * wide] * convolved).astype(BF)
        part_own[lo:hi, :] = dot(inner[lo:hi, :], columns(cut, wide), ((1,), (1,))).astype(BF)

    gated_rows(edge, count)
    halo = remote(
        gated.at[pl.ds(count, HALO)], halo_in, halo_sem.at[0], halo_sem.at[1], ahead_of
    )
    halo.start()
    branch_rows(half, count)
    swap_part(half).start()
    gated_rows(0, edge)
    keep(1).start()
    halo.wait_recv()
    starts = me.s % (lax.axis_size("seq") // 2) == 0
    carried = jnp.where(starts, 0.0, halo_in[...].astype(F32))
    gated[:HALO, :] = carried.astype(BF)
    keep(2).start()
    wide_gated[:HALO, :] = carried
    branch_rows(0, half)
    swap_part(0).start()
    feed.along_a()
    feed.across_a()

    def middle_step(at):
        total = part_own[at, :].astype(F32) + part_theirs[at, :].astype(F32)
        total = tokens[at, :].astype(F32) + total
        middle[at, :] = total
        inverse = lax.rsqrt(mean_square(total) + norm_eps)
        normed_two[at, :] = (total * inverse * gain_two).astype(BF)

    swap_part(half).wait_recv()
    row_loop(half, middle_step, half)
    swap_part(0).wait_recv()
    row_loop(half, middle_step)
    feed.from_sibling()
    mixer.sent(plane=True)
    feed.sent()
    swap_vec.wait_send()
    swap_part(half).wait_send()
    swap_part(0).wait_send()
    halo.wait_send()
    for i in range(3):
        keep(i).wait()


def forward(tokens, w_in, w_out, w_gu, w_down, vectors):
    count, width = tokens.shape
    _, rows, wide = w_in.shape
    part = w_down.shape[1] // 2
    whole = (2, RING, RING, 2, rows, part)
    vmem = pl.BlockSpec(memory_space=pltpu.VMEM)
    hbm = pl.BlockSpec(memory_space=pl.ANY)
    dma = pltpu.SemaphoreType.DMA
    mixer, feed, *rest = pl.pallas_call(
        forward_kernel,
        out_shape=(
            jax.ShapeDtypeStruct((2, *whole), BF),
            jax.ShapeDtypeStruct((2, 3, *whole), BF),
            jax.ShapeDtypeStruct((count, width), F32),
            jax.ShapeDtypeStruct((count, width), BF),
            jax.ShapeDtypeStruct((count, 3 * wide), F32),
            jax.ShapeDtypeStruct((count + HALO, wide), BF),
            jax.ShapeDtypeStruct((8, width), F32),
        ),
        in_specs=[hbm] + [vmem] * 5,
        out_specs=[hbm, hbm, vmem, vmem, hbm, hbm, vmem],
        scratch_shapes=[
            pltpu.VMEM((2, *whole), BF),
            pltpu.VMEM((count, 3 * wide), F32),
            pltpu.VMEM((count + HALO, wide), BF),
            pltpu.VMEM((LANES, LANES), F32),
            pltpu.VMEM((rows, LANES), F32),
            dma((3,)),
            pltpu.VMEM((count, width), BF),
            pltpu.VMEM((2, rows, part), BF),
            pltpu.VMEM((2, 3, rows, part), BF),
            pltpu.VMEM((rows, LANES), F32),
            pltpu.VMEM((count, width), BF),
            pltpu.VMEM((count + HALO, wide), F32),
            pltpu.VMEM((count, wide), BF),
            pltpu.VMEM((count, width), BF),
            pltpu.VMEM((count, width), BF),
            pltpu.VMEM((HALO, wide), BF),
            dma,
            dma((2, 3)),
            dma((2,)),
            *gather_sems(),
            *gather_sems(),
        ],
        compiler_params=pltpu.CompilerParams(
            collective_id=0, has_side_effects=True, vmem_limit_bytes=60 * 1024 * 1024
        ),
        name="gather_and_forward",
    )(tokens, w_in, w_out, w_gu, w_down, vectors)
    total = 4 * RING * RING * rows
    return (mixer.reshape(2, total, part), feed.reshape(2, 3, total, part), *rest)


class Scattering:
    def __init__(self, me, partial, out, refs, lead, in_place=False):
        self.me, self.partial, self.out, self.lead = me, partial, out, lead
        self.in_place = in_place
        self.head = (me.core, *lead) if in_place else lead
        if in_place:
            refs = (partial, *refs[:5], None, *refs[5:])
        (
            self.mine,
            self.sib,
            self.from_a,
            self.from_b,
            self.from_y,
            self.from_core,
            self.load_sem,
            self.sib_send,
            self.sib_recv,
            self.a_send,
            self.a_recv,
            self.b_send,
            self.b_recv,
            self.last_sem,
        ) = refs

    def at(self, rr, a, b):
        return self.me.spot(rr, a % RING, b % RING)

    def add(self, where, *others):
        index = (*self.head, *where)
        if len(others) == 1:
            self.mine[index] = self.mine[index] + others[0][0][others[0][1]]
            return
        total = self.mine[index].astype(F32)
        for ref, i in others:
            total = total + ref[i].astype(F32)
        self.mine[index] = total.astype(self.mine.dtype)

    def load(self):
        return pltpu.make_async_copy(self.partial.at[self.me.core], self.mine, self.load_sem)

    def to_sibling(self, at):
        me = self.me
        group = at // 8
        a = (me.pb + 2 + group + (group // 2) * (5 - 2 * group)) % RING
        b = (me.pa + 2 + (at // 2) % RING) % RING
        peer_core = 1 - me.core
        where = (me.row(at % 2), a + peer_core * (b - a), b + peer_core * (a - b))
        index = (*self.lead, *where)
        return self.sibling_copy(self.partial.at[(peer_core, *index)], where)

    def sibling_copy(self, src, where):
        i = (where[0] * RING + where[1]) * RING + where[2]
        return remote(
            src,
            self.sib.at[(*self.lead, *where)],
            self.sib_send.at[i],
            self.sib_recv.at[i],
            self.me.sibling,
        )

    def begin(self):
        if not self.in_place:
            self.load().start()

        def step(at, carry):
            self.to_sibling(at).start()
            return carry

        lax.fori_loop(0, 2 * RING * RING, step, 0)

    def with_sibling(self, rr, a, b):
        where = self.at(rr, a, b)
        index = (*self.lead, *where)
        self.sibling_copy(self.sib.at[index], where).wait_recv()
        self.add(where, (self.sib, index))

    def send_a(self, side, slot, rr, a, b):
        return remote(
            self.mine.at[(*self.head, *self.at(rr, a, b))],
            self.from_a.at[side, slot],
            self.a_send.at[side, slot],
            self.a_recv.at[side, slot],
            self.me.on_a(1 if side == 0 else 3),
        )

    def add_a(self, side, slot, rr, a, b):
        self.send_a(side, slot, rr, a, b).wait_recv()
        self.add(self.at(rr, a, b), (self.from_a, (side, slot)))

    def over_b(self, step):
        def body(j, carry):
            step((self.me.pb + 2 + j) % RING)
            return carry

        lax.fori_loop(0, RING, body, 0)

    def opposite(self):
        pa = self.me.pa

        def step(b):
            self.with_sibling(0, pa + 2, b)
            self.send_a(0, b, 0, pa + 2, b).start()
            self.with_sibling(1, pa + 2, b)
            self.send_a(1, b, 1, pa + 2, b).start()

        self.over_b(step)

    def direct(self):
        pa = self.me.pa

        def step(b):
            self.with_sibling(1, pa + 1, b)
            self.send_a(0, 8 + b, 1, pa + 1, b).start()
            self.with_sibling(0, pa + 3, b)
            self.send_a(1, 4 + b, 0, pa + 3, b).start()

        self.over_b(step)

    def onward(self):
        pa = self.me.pa

        def step(b):
            self.with_sibling(0, pa + 1, b)
            self.add_a(0, b, 0, pa + 1, b)
            self.send_a(0, 4 + b, 0, pa + 1, b).start()
            self.with_sibling(1, pa + 3, b)
            self.add_a(1, b, 1, pa + 3, b)
            self.send_a(1, 8 + b, 1, pa + 3, b).start()

        self.over_b(step)

    def kept(self):
        pa = self.me.pa

        def step(b):
            self.with_sibling(0, pa, b)
            self.with_sibling(1, pa, b)

        self.over_b(step)

    def finish_a(self, rr, b):
        slot = 4 + 4 * rr + b % RING
        pa = self.me.pa
        self.send_a(0, slot, rr, pa, b).wait_recv()
        self.send_a(1, slot, rr, pa, b).wait_recv()
        self.add(self.at(rr, pa, b), (self.from_a, (0, slot)), (self.from_a, (1, slot)))

    def send_b(self, side, slot, rr, b):
        return remote(
            self.mine.at[(*self.head, *self.at(rr, self.me.pa, b))],
            self.from_b.at[side, slot],
            self.b_send.at[side, slot],
            self.b_recv.at[side, slot],
            self.me.on_b(1 if side == 0 else 3),
        )

    def add_b(self, side, slot, rr, b):
        self.send_b(side, slot, rr, b).wait_recv()
        self.add(self.at(rr, self.me.pa, b), (self.from_b, (side, slot)))

    def begin_b(self):
        pb = self.me.pb
        self.finish_a(0, pb + 2)
        self.send_b(0, 0, 0, pb + 2).start()
        self.finish_a(1, pb + 2)
        self.send_b(1, 0, 1, pb + 2).start()
        self.finish_a(1, pb + 1)
        self.send_b(0, 2, 1, pb + 1).start()
        self.finish_a(0, pb + 3)
        self.send_b(1, 1, 0, pb + 3).start()
        self.finish_a(0, pb + 1)
        self.finish_a(1, pb + 3)
        self.finish_a(1, pb)
        self.finish_a(0, pb)

    def onward_b(self):
        pb = self.me.pb
        self.add_b(0, 0, 0, pb + 1)
        self.send_b(0, 1, 0, pb + 1).start()
        self.add_b(1, 0, 1, pb + 3)
        self.send_b(1, 2, 1, pb + 3).start()

    def plane_copy(self, rr, off):
        me = self.me
        slot = rr * RING + (RING - off) % RING
        return remote(
            self.mine.at[(*self.head, *self.at(rr, me.pa, me.pb + off))],
            self.from_b.at[slot],
            self.b_send.at[rr * RING + off],
            self.b_recv.at[slot],
            me.on_plane(rr, off),
        )

    def begin_plane(self):
        for rr, off in PLANE[::-1]:
            self.finish_a(rr, self.me.pb + off)
            self.plane_copy(rr, off).start()
        self.finish_a(0, self.me.pb)

    def end_plane(self):
        me = self.me
        for rr, off in PLANE:
            self.plane_copy(rr, off).wait_recv()
        slots = [(self.from_b, (rr * RING + off,)) for rr, off in PLANE]
        self.add(self.at(0, me.pa, me.pb), *slots)
        self.hand_over()

    def hand_over(self):
        me = self.me
        self.last().start()
        self.out[me.core] = self.mine[
            (*self.head, *self.at(0, me.pa, me.pb), me.core)
        ].astype(F32)

    def over(self):
        me = self.me
        return remote(
            self.mine.at[(*self.head, *self.at(1, me.pa, me.pb))],
            self.from_y,
            self.last_sem.at[0],
            self.last_sem.at[1],
            me.other_y,
        )

    def last(self):
        me = self.me
        return remote(
            self.mine.at[(*self.head, *self.at(0, me.pa, me.pb), 1 - me.core)],
            self.from_core,
            self.last_sem.at[2],
            self.last_sem.at[3],
            me.sibling,
        )

    def across_y(self):
        pb = self.me.pb
        self.add_b(0, 2, 1, pb)
        self.add_b(1, 2, 1, pb)
        self.over().start()
        self.add_b(0, 1, 0, pb)
        self.add_b(1, 1, 0, pb)

    def across_cores(self):
        me = self.me
        self.over().wait_recv()
        self.add(self.at(0, me.pa, me.pb), (self.from_y, ...))
        self.hand_over()

    def finish(self, plane=False):
        self.last().wait_recv()
        self.out[1 - self.me.core] = self.from_core[...].astype(F32)
        self.last().wait_send()

        def sent_sibling(at, carry):
            self.to_sibling(at).wait_send()
            return carry

        lax.fori_loop(0, 2 * RING * RING, sent_sibling, 0)

        def sent_a(slot, carry):
            self.send_a(0, slot, 0, 0, 0).wait_send()
            self.send_a(1, slot, 0, 0, 0).wait_send()
            return carry

        lax.fori_loop(0, 3 * RING, sent_a, 0)
        if plane:
            for rr, off in PLANE:
                self.plane_copy(rr, off).wait_send()
            return
        self.over().wait_send()
        for slot in range(3):
            self.send_b(0, slot, 0, 0).wait_send()
            self.send_b(1, slot, 0, 0).wait_send()


def scatter_scratch(kinds, rows, width, in_place=False, plane=False):
    blocks = 2 * RING * RING
    dma = pltpu.SemaphoreType.DMA
    slots = (2 * RING,) if plane else (2, 3)
    mine = [] if in_place else [pltpu.VMEM((*kinds, 2, RING, RING, 2, rows, width), BF)]
    return [
        *mine,
        pltpu.VMEM((*kinds, 2, RING, RING, 2, rows, width), BF),
        pltpu.VMEM((2, 3 * RING, *kinds, 2, rows, width), BF),
        pltpu.VMEM((*slots, *kinds, 2, rows, width), BF),
        pltpu.VMEM((*kinds, 2, rows, width), BF),
        pltpu.VMEM((*kinds, rows, width), BF),
        *([] if in_place else [dma]),
        dma((blocks,)),
        dma((blocks,)),
        dma((2, 3 * RING)),
        dma((2, 3 * RING)),
        dma(slots),
        dma(slots),
        dma((4,)),
    ]


def backward_kernel(
    pf_ref,
    back_hbm,
    feed_hbm,
    middle_hbm,
    cot_hbm,
    tokens_hbm,
    mixed_hbm,
    gated_hbm,
    weights_hbm,
    vec_hbm,
    om_ref,
    of_ref,
    block_ref,
    grad_ref,
    *refs,
):
    (
        back_own,
        feed_own,
        middle,
        cot,
        tokens,
        mixed,
        gated,
        weights,
        vec,
        back_theirs,
        feed_theirs,
        one_theirs,
        branch,
        turned,
        inner,
        wide_gated,
        wide_conv,
        back_inner,
        back_mixed,
        sums,
        halo_out,
        halo_in,
        pm_ref,
        loads,
        pairs,
        halo_sem,
        vec_own,
        vec_theirs,
        vec_sem,
    ) = refs[:29]
    me = Place()
    pair = me.pair()
    ahead_of, behind = me.along()
    chan = lax.axis_index("chan")
    mixer = Scattering(me, pm_ref, om_ref, refs[29:41], (), in_place=True)
    feed = Scattering(me, pf_ref, of_ref, refs[41:], EVERY)
    one_own, one_sum = cot, block_ref
    count, width = middle.shape
    wide = back_inner.shape[1]
    part = weights.shape[2]
    half = count // 2
    edge = half - HALO

    def load(i):
        src, dst = (
            (back_hbm, back_own),
            (middle_hbm, middle),
            (cot_hbm, cot),
            (vec_hbm, vec),
            (weights_hbm, weights),
            (mixed_hbm, mixed),
            (gated_hbm, gated),
            (tokens_hbm, tokens),
            (feed_hbm, feed_own),
        )[i]
        return pltpu.make_async_copy(src, dst, loads.at[i])

    def exchange(i):
        src, dst, lo, hi = (
            (back_own, back_theirs, 0, half),
            (back_own, back_theirs, half, count),
            (one_own, one_theirs, 0, edge),
            (one_own, one_theirs, edge, count),
            (feed_own, feed_theirs, 0, count),
        )[i]
        at = pl.ds(lo, hi - lo)
        return remote(src.at[at], dst.at[at], pairs.at[0, i], pairs.at[1, i], pair)

    for i in range(9):
        load(i).start()
    me.greet((pair, ahead_of, behind))
    load(0).wait()
    exchange(0).start()
    exchange(1).start()
    feed.begin()
    for i in range(1, 9):
        load(i).wait()
    feed.load().wait()
    feed.opposite()

    gain_one = vec[0:1, :]
    gain_two = vec[1:2, :]
    tap_at = pl.ds(pl.multiple_of(chan * wide, LANES), wide)
    taps = [vec[2 + i : 3 + i, tap_at] for i in range(3)]
    sums[...] = jnp.zeros_like(sums)
    wide_gated[...] = gated[...].astype(F32)

    def convolved(at):
        total = taps[0] * wide_gated[at.start + HALO - 2 : at.stop + HALO - 2, :]
        total = total + taps[1] * wide_gated[at.start + HALO - 1 : at.stop + HALO - 1, :]
        return total + taps[2] * wide_gated[at.start + HALO : at.stop + HALO, :]

    for at in rows_of(count, ROWS):
        inner[at, :] = (mixed[at, wide : 2 * wide] * convolved(at)).astype(BF)
    feed.direct()

    def turn_step(at):
        values = tokens[at, :].astype(F32)
        inverse = lax.rsqrt(mean_square(values) + norm_eps)
        branch[at, :] = (values * inverse * gain_one).astype(BF)

    row_loop(count, turn_step)
    turned[...] = branch[...].T
    def norm_step(at):
        mid = middle[at, :]
        inverse = lax.rsqrt(mean_square(mid) + norm_eps)
        own = back_own[at, :].astype(F32)
        back = own + back_theirs[at, :].astype(F32)
        total = cot[at, :].astype(F32) + norm_back(mid, inverse, gain_two, back)
        grad_ref[at, :] = total
        branch[at, :] = total.astype(BF)
        sums[1:2, :] += jnp.sum(own * mid * inverse, axis=0, keepdims=True)

    cut = 3 * wide - part

    def inner_rows(lo, hi):
        row_loop(hi - lo, norm_step, lo)
        w_out = weights[1, :, cut : cut + wide]
        back_inner[lo:hi, :] = dot(branch[lo:hi, :], w_out, ((1,), (0,)))
        for at in rows_of(hi, ROWS, lo):
            product = back_inner[at, :] * mixed[at, wide : 2 * wide]
            wide_conv[at, :] = product.astype(BF).astype(F32)

    def gain_step(at):
        values = tokens[at, :].astype(F32)
        inverse = lax.rsqrt(mean_square(values) + norm_eps)
        own = one_sum[at, :]
        one_own[at, :] = own.astype(BF)
        sums[0:1, :] += jnp.sum(own * values * inverse, axis=0, keepdims=True)

    def mixed_rows(lo, hi):
        for at in rows_of(hi, HALO, lo):
            back_gated = (
                taps[0] * wide_conv[at.start + 2 : at.stop + 2, :]
                + taps[1] * wide_conv[at.start + 1 : at.stop + 1, :]
                + taps[2] * wide_conv[at, :]
            )
            back_mixed[at, :wide] = (back_gated * mixed[at, 2 * wide :]).astype(BF)
            back_mixed[at, wide : 2 * wide] = (back_inner[at, :] * convolved(at)).astype(BF)
            back_mixed[at, 2 * wide :] = (back_gated * mixed[at, :wide]).astype(BF)
            for i in range(3):
                shift = HALO - 2 + i
                term = wide_conv[at, :] * wide_gated[at.start + shift : at.stop + shift, :]
                sums[2 + i : 3 + i, tap_at] += jnp.sum(term, axis=0, keepdims=True)
        one_sum[lo:hi, :] = jnp.zeros((hi - lo, width), F32)

        def back_step(j, carry):
            which, at, lanes = in_tile(j, part)
            one_sum[lo:hi, :] += dot(back_mixed[lo:hi, lanes], weights[which, :, at], ((1,), (1,)))
            return carry

        lax.fori_loop(0, 4, back_step, 0)
        row_loop(hi - lo, gain_step, lo, HALO)

    exchange(0).wait_recv()
    inner_rows(0, half)
    halo_out[...] = wide_conv[0:HALO, :].astype(BF)
    halo = remote(halo_out, halo_in, halo_sem.at[0], halo_sem.at[1], behind)
    halo.start()
    mixed_rows(0, edge)
    exchange(2).start()
    feed.onward()
    exchange(1).wait_recv()
    inner_rows(half, count)
    halo.wait_recv()
    last = me.s % (lax.axis_size("seq") // 2) == lax.axis_size("seq") // 2 - 1
    wide_conv[count : count + HALO, :] = jnp.where(last, 0.0, halo_in[...].astype(F32))
    mixed_rows(edge, count)
    vec_own[...] = sums[: vec_own.shape[0], :]
    swap_vec = remote(vec_own, vec_theirs, vec_sem.at[0], vec_sem.at[1], pair)
    swap_vec.start()
    exchange(3).start()
    exchange(4).start()
    term_out = dot(branch[...], inner[...], ((0,), (0,))).astype(BF)
    shape = pm_ref.shape[1:-1]
    pm_ref[1, :, :, :, :, :, cut : cut + wide] = term_out.reshape(*shape, wide)

    def term_step(j, carry):
        which, at, lanes = in_tile(j, part)
        term = dot(turned[...], back_mixed[:, lanes], ((1,), (0,))).astype(BF)
        pm_ref[which, :, :, :, :, :, at] = term.reshape(*shape, part // 3)
        return carry

    lax.fori_loop(0, 4, term_step, 0)
    swap_vec.wait()
    sums[: vec_own.shape[0], :] = vec_own[...] + vec_theirs[...]
    vec_term = sums[...].T.astype(BF)
    lanes = vec_term.shape[1]
    pm_ref[1, :, :, :, :, :, cut + wide : cut + wide + lanes] = vec_term.reshape(*shape, lanes)
    pm_ref[1, :, :, :, :, :, cut + wide + lanes :] = jnp.zeros(
        (*shape, part - cut - wide - lanes), BF
    )
    def out_step(at):
        total = feed_own[at, :].astype(F32) + feed_theirs[at, :].astype(F32)
        block_ref[at, :] = middle[at, :] + total

    def grad_step(at):
        values = tokens[at, :].astype(F32)
        inverse = lax.rsqrt(mean_square(values) + norm_eps)
        back = one_own[at, :].astype(F32) + one_theirs[at, :].astype(F32)
        grad_ref[at, :] += norm_back(values, inverse, gain_one, back)

    mixer.begin()
    feed.kept()
    feed.begin_b()
    mixer.opposite()
    mixer.direct()
    feed.onward_b()
    mixer.onward()
    mixer.kept()
    feed.across_y()
    mixer.begin_plane()
    feed.across_cores()
    exchange(2).wait_recv()
    exchange(3).wait_recv()
    row_loop(count, grad_step)
    mixer.end_plane()
    mixer.finish(plane=True)
    feed.finish()
    exchange(4).wait_recv()
    row_loop(count, out_step)
    halo.wait_send()
    for i in range(5):
        exchange(i).wait_send()


def backward(term_feed, back_two, feed_part, middle, cotangent, tokens, mixed, gated, weights, vec):
    halves, kinds, total, width = term_feed.shape
    rows = total // (4 * RING * RING)
    whole = (2, RING, RING, 2, rows, width)
    count, features = middle.shape
    wide = gated.shape[1]
    dma = pltpu.SemaphoreType.DMA

    def like(x):
        return pltpu.VMEM(x.shape, x.dtype)

    low_act = pltpu.VMEM((count, features), BF)
    return pl.pallas_call(
        backward_kernel,
        out_shape=(
            jax.ShapeDtypeStruct((halves, rows, width), F32),
            jax.ShapeDtypeStruct((halves, kinds, rows, width), F32),
            jax.ShapeDtypeStruct((count, features), F32),
            jax.ShapeDtypeStruct((count, features), F32),
        ),
        in_specs=[pl.BlockSpec(memory_space=pl.ANY)] * 10,
        out_specs=[pl.BlockSpec(memory_space=pltpu.VMEM)] * 4,
        scratch_shapes=[
            *[like(x) for x in (back_two, feed_part, middle, cotangent, tokens, mixed, gated)],
            like(weights),
            like(vec),
            low_act,
            low_act,
            low_act,
            low_act,
            pltpu.VMEM((features, count), BF),
            pltpu.VMEM((count, wide), BF),
            pltpu.VMEM((count + HALO, wide), F32),
            pltpu.VMEM((count + HALO, wide), F32),
            pltpu.VMEM((count, wide), F32),
            pltpu.VMEM((count, 3 * wide), BF),
            pltpu.VMEM((128, features), F32),
            pltpu.VMEM((HALO, wide), BF),
            pltpu.VMEM((HALO, wide), BF),
            pltpu.VMEM((halves, *whole), BF),
            dma((9,)),
            dma((2, 5)),
            dma((2,)),
            like(vec),
            like(vec),
            dma((2,)),
            *scatter_scratch((), rows, width, in_place=True, plane=True),
            *scatter_scratch((kinds,), rows, width),
        ],
        compiler_params=pltpu.CompilerParams(
            collective_id=1, has_side_effects=True, vmem_limit_bytes=60 * 1024 * 1024
        ),
        name="backward_and_scatter",
    )(
        term_feed.reshape(halves, kinds, *whole),
        back_two,
        feed_part,
        middle,
        cotangent,
        tokens,
        mixed,
        gated,
        weights,
        vec,
    )


def feed_kernel(n_ref, c_ref, w_ref, t_ref, out_ref, back_ref, n_turned, c_turned, out_sum, back_sum):
    step = pl.program_id(0)

    @pl.when(step == 0)
    def _():
        n_turned[...] = n_ref[...].T
        c_turned[...] = c_ref[...].T
        out_sum[...] = jnp.zeros_like(out_sum)
        back_sum[...] = jnp.zeros_like(back_sum)

    def weight(kind):
        return jnp.concatenate([w_ref[0, kind], w_ref[1, kind]], axis=1)

    def keep(kind, term):
        term = term.astype(BF)
        lanes = term.shape[1] // 2
        t_ref[0, kind] = term[:, :lanes]
        t_ref[1, kind] = term[:, lanes:]

    w_gate, w_up, w_down = weight(0), weight(1), weight(2)
    normed = n_ref[...]
    back_out = c_ref[...]
    gate = dot(normed, w_gate, ((1,), (0,)))
    up = dot(normed, w_up, ((1,), (0,)))
    back_hidden = dot(back_out, w_down, ((1,), (0,)))
    sig = jax.nn.sigmoid(gate)
    act = gate * sig
    hidden = (act * up).astype(BF)
    back_gate = (back_hidden * up * sig * (1.0 + gate * (1.0 - sig))).astype(BF)
    back_up = (back_hidden * act).astype(BF)
    out_sum[...] += dot(hidden, w_down, ((1,), (1,)))
    back_sum[...] += dot(back_gate, w_gate, ((1,), (1,))) + dot(back_up, w_up, ((1,), (1,)))
    keep(0, dot(n_turned[...], back_gate, ((1,), (0,))))
    keep(1, dot(n_turned[...], back_up, ((1,), (0,))))
    keep(2, dot(c_turned[...], hidden, ((1,), (0,))))

    @pl.when(step == pl.num_programs(0) - 1)
    def _():
        out_ref[...] = out_sum[...].astype(BF)
        back_ref[...] = back_sum[...].astype(BF)


def feed_forward(normed, cotangent, weights):
    halves, kinds, total, width = weights.shape
    tokens = normed.shape[0]
    lanes = 128
    whole = pl.BlockSpec((tokens, total), lambda j: (0, 0))
    part = pl.BlockSpec((halves, kinds, total, lanes), lambda j: (0, 0, 0, j))
    flops = 9 * 2 * tokens * total * halves * width
    return pl.pallas_call(
        feed_kernel,
        grid=(width // lanes,),
        out_shape=(
            jax.ShapeDtypeStruct(weights.shape, BF),
            jax.ShapeDtypeStruct((tokens, total), BF),
            jax.ShapeDtypeStruct((tokens, total), BF),
        ),
        in_specs=[whole, whole, part],
        out_specs=[part, whole, whole],
        scratch_shapes=[
            pltpu.VMEM((total, tokens), BF),
            pltpu.VMEM((total, tokens), BF),
            pltpu.VMEM((tokens, total), F32),
            pltpu.VMEM((tokens, total), F32),
        ],
        compiler_params=pltpu.CompilerParams(vmem_limit_bytes=60 * 1024 * 1024),
        cost_estimate=pl.CostEstimate(
            flops=flops, bytes_accessed=4 * halves * kinds * total * width, transcendentals=0
        ),
        name="feed_forward",
    )(normed, cotangent, weights)


def dot(a, b, dims):
    return lax.dot_general(a, b, (dims, ((), ())), preferred_element_type=F32)


def norm_back(values, inverse, gain, back):
    scaled = back * gain
    mean = jnp.mean(scaled * values, axis=-1, keepdims=True)
    return inverse * (scaled - values * (inverse * inverse) * mean)


def adam_update(weight, moment_one, second, gradient, step_rate, weight_decay):
    first_new = beta_one * moment_one + (1.0 - beta_one) * gradient
    second_new = beta_two * second + (1.0 - beta_two) * gradient * gradient
    first_hat = first_new / (1.0 - beta_one**STEP)
    second_hat = second_new / (1.0 - beta_two**STEP)
    weight_new = weight - step_rate * (
        first_hat / (jnp.sqrt(second_hat) + adam_eps) + weight_decay * weight
    )
    return (weight_new, first_new, second_new)


def adam_kernel(om_ref, of_ref, block_ref, grad_ref, *refs):
    chan = lax.axis_index("chan")
    w_in, w_out, w_gu, w_down, vectors = [refs[3 * i : 3 * i + 3] for i in range(5)]
    in_new, out_new, gu_new, down_new, vec_new = [refs[15 + 3 * i : 18 + 3 * i] for i in range(5)]
    count = block_ref.shape[0] // 4
    moves = []
    for k, (src, dst) in enumerate(((block_ref, refs[30]), (grad_ref, refs[31]))):
        held = refs[32].at[k]
        for i in range(4):
            at = pl.ds(i * count, count)
            into = pltpu.make_async_copy(src.at[at], held.at[at], refs[33].at[0, k, i])
            out = pltpu.make_async_copy(held.at[at], dst.at[at], refs[33].at[1, k, i])
            into.start()
            moves.append((into, out))
    part = om_ref.shape[2]
    wide = w_out[0].shape[1]
    cut = 3 * wide - part

    def update(arrays, results, index, gradient, rate=rate_matrix, decay=decay_matrix):
        new = adam_update(*[a[index] for a in arrays], gradient, rate, decay)
        for ref, value in zip(results, new, strict=True):
            ref[index] = value

    def both(at):
        return slice(None), at

    for c in range(2):
        at = slice(c * wide, (c + 1) * wide)
        update(w_in, in_new, (c,), om_ref[0, :, at])
    left = part - 2 * wide
    update(w_in, in_new, (2, slice(None), slice(0, left)), om_ref[0, :, 2 * wide :])
    update(w_in, in_new, (2, slice(None), slice(left, wide)), om_ref[1, :, :cut])
    update(w_out, out_new, both(slice(None)), om_ref[1, :, cut : cut + wide])
    for half in range(2):
        at = slice(half * part, (half + 1) * part)
        for kind in range(2):
            update(w_gu, gu_new, (slice(None), kind, at), of_ref[half, kind])
        update(w_down, down_new, both(at), of_ref[half, 2])
    rows = om_ref.shape[1]
    block = om_ref[1, :, cut + wide : cut + wide + LANES]
    turned = jnp.concatenate([block, jnp.zeros((LANES - rows, LANES), F32)], axis=0).T
    own = jnp.where(chan == 0, turned[:5, : rows // 2], turned[:5, rows // 2 : rows])
    update(vectors, vec_new, both(slice(None)), own, rate_vector, 0.0)
    for into, out in moves:
        into.wait()
        out.start()
    for _, out in moves:
        out.wait()


def adam(sum_mixer, sum_feed, block_out, input_grad, arrays):
    def whole(x):
        return pl.BlockSpec(x.shape, lambda i, n=x.ndim: (0,) * n)

    moved = (block_out, input_grad)
    hbm = pl.BlockSpec(memory_space=pl.ANY)
    dma = pltpu.SemaphoreType.DMA
    return pl.pallas_call(
        adam_kernel,
        grid=(1,),
        out_shape=[jax.ShapeDtypeStruct(x.shape, x.dtype) for x in (*arrays, *moved)],
        in_specs=[whole(sum_mixer), whole(sum_feed), hbm, hbm, *[whole(x) for x in arrays]],
        out_specs=[*[whole(x) for x in arrays], hbm, hbm],
        scratch_shapes=[pltpu.VMEM((2, *block_out.shape), F32), dma((2, 2, 4))],
        compiler_params=pltpu.CompilerParams(vmem_limit_bytes=60 * 1024 * 1024),
        name="adam",
    )(sum_mixer, sum_feed, *moved, *arrays)


def body(
    tokens,
    cotangent,
    w_in,
    w_in_m,
    w_in_v,
    w_out,
    w_out_m,
    w_out_v,
    w_gu,
    w_gu_m,
    w_gu_v,
    w_down,
    w_down_m,
    w_down_v,
    vectors,
    vectors_m,
    vectors_v,
):
    in_state = [jnp.transpose(a, (1, 0, 2)) for a in (w_in, w_in_m, w_in_v)]
    full_mixer, full_feed, middle, normed_two, mixed, gated, vec = forward(
        tokens, in_state[0], w_out, w_gu, w_down, vectors
    )
    term_feed, feed_part, back_two_part = feed_forward(normed_two, cotangent, full_feed)
    sum_mixer, sum_feed, block_out, input_grad = backward(
        term_feed, back_two_part, feed_part, middle, cotangent, tokens, mixed, gated, full_mixer, vec
    )
    state = (
        *in_state,
        *(w_out, w_out_m, w_out_v),
        *(w_gu, w_gu_m, w_gu_v),
        *(w_down, w_down_m, w_down_v),
        *(vectors, vectors_m, vectors_v),
    )
    *new, block_out, input_grad = adam(sum_mixer, sum_feed, block_out, input_grad, state)
    in_new = [jnp.transpose(a, (1, 0, 2)) for a in new[:3]]
    return (block_out, input_grad, *in_new, *new[3:])


def solution(mesh):
    matrices = [P("seq", None, "chan")] * 3 + [P("seq", "chan")] * 3
    weights = (*matrices, *matrices, *[P(None, ("seq", "chan"))] * 3)
    return jax.shard_map(
        body,
        mesh=mesh,
        in_specs=(P("seq", None), P("seq", None), *weights),
        out_specs=(P("seq", None), P("seq", None), *weights),
        check_vma=False,
    )
```
